32 devices in a mesh: row: 4 (over y, core), col: 8 (over z, x).
Axes of the slice: x: 2, y: 2, z: 4, core: 2. Of those that a mesh axis runs over, the one named last changes fastest.
Arguments:
- tokens: bfloat16 [4096, 768], P(('row', 'col')), may hold values from -6 to 6
- expert_ids: int32 [4096, 2], P(('row', 'col')), may hold values from 0 to 31, all different within a row; in each aligned block of 128 rows (0 to 127, 128 to 255, ...) at most 16 rows name the same one
- keep_mask: int32 [4096, 2], P(('row', 'col')), may hold values 0 or 1
- gate_weights: float32 [4096, 2], P(('row', 'col')), may hold values from 0.2 to 1
- weight_in: bfloat16 [32, 768, 4096], P(('row', 'col')), may hold values from -0.21875 to 0.21875
- weight_out: bfloat16 [32, 4096, 768], P(('row', 'col')), may hold values from -0.09375 to 0.09375
- grad_output: bfloat16 [4096, 768], P(('row', 'col')), may hold values from -6 to 6
Outputs:
- combined: bfloat16 [4096, 768], P(('row', 'col'))
- grad_tokens: bfloat16 [4096, 768], P(('row', 'col'))
- grad_gates: float32 [4096, 2], P(('row', 'col'))
- grad_weight_in: bfloat16 [32, 768, 4096], P(('row', 'col'))
- grad_weight_out: bfloat16 [32, 4096, 768], P(('row', 'col'))
The draws below stay inside these ranges and needn't reach their ends.
Inputs may be any that keep to these rules, and one draw needn't show every extreme that they name: `expert_ids`: the two experts of a token differ. Among the choices of one device's tokens, at most 16 name one expert, and in every draw some expert is named by exactly 16 choices of some device.
All inputs are finite; a program needn't handle non-finite values. Where the reference program divides by a largest or mean magnitude, that divisor is 1e-20 or more. No bound on the sum of `keep_mask` on one device may be relied on, other than what follows from the above.
Results may differ from the reference program's by a relative error of at most 0.0067.
Values may be sent and summed in bfloat16 or wider, within the bound.
No kernel may reach another device: no remote copies, remote signals or barrier semaphores. Data moves between devices by JAX's collectives and lax.ppermute only.
A program may use at most 128 MiB of HBM per device.

```python
import math
import jax
import jax.numpy as jnp
import numpy as np
from jax import lax

D = 768
FF = 4096
TOPK = 2
BLOCK = 128
TOK_DEV = 128
EXPERTS = 32
TOKENS = 4096
CAP = 16
N_ROW = 4
N_COL = 8


def plant(drawn, stream_key, low, largest):
    longest = drawn.shape.index(max(drawn.shape))
    spots = []
    for shift in (0, 1):
        where = [jax.random.randint(jax.random.fold_in(stream_key, axis), (), 0, length) for axis, length in enumerate(drawn.shape)]
        where[longest] = (where[longest] + shift) % drawn.shape[longest]
        spots.append(tuple(where))
    return drawn.at[spots[0]].set(low).at[spots[1]].set(largest)


def block_levels(rng, dims, pieces, smallest, high):
    factor_of, own = 1.0, jax.random.fold_in(rng, 6)
    for position, shards_of in pieces:
        steps = jnp.exp(jax.random.uniform(jax.random.fold_in(own, position), (shards_of,), jnp.float32, smallest / len(pieces), high / len(pieces)))
        factor_of = factor_of * jnp.repeat(steps, dims[position] // shards_of).reshape([-1 if axis == position else 1 for axis in range(len(dims))])
    return factor_of


def routed_block(stream_key, own, number, rows, amount, top, most, skew):
    ranking = jax.random.permutation(stream_key, amount)
    crowded, usual = shares(amount, rows * top, most, skew, True), shares(amount, rows * top, most, skew, False)
    places = jnp.arange(amount)

    def named(lengths, offset_by):
        used = int((lengths > 0).sum())
        fixed = max(1, used // 4)
        passed = fixed + (places - fixed + offset_by * (used - fixed)) % max(1, amount - fixed)
        return jnp.zeros((amount,), jnp.int32).at[ranking[jnp.where(places < fixed, places, passed)]].set(jnp.asarray(lengths, jnp.int32))

    lengths = jnp.where(number % 4 == 0, named(crowded, number // 4), named(usual, number - number // 4 - 1))
    mixed = jax.random.permutation(jax.random.fold_in(own, 3), amount)
    source_of, taker = mixed[0:amount // 2 * 2:2], mixed[1:amount // 2 * 2:2]
    room = jnp.minimum(lengths[source_of] - 1, most - lengths[taker]) // 2
    room = jnp.where((source_of == ranking[0]) | (taker == ranking[0]) | (lengths[taker] == 0), 0, jnp.maximum(room, 0))
    passed = jax.random.randint(jax.random.fold_in(own, 4), (amount // 2,), 0, 1 << 20) % (room + 1)
    lengths = lengths.at[source_of].add(-passed).at[taker].add(passed)
    items = jnp.searchsorted(jnp.cumsum(lengths), jnp.arange(rows * top), side="right").astype(jnp.int32)
    grid = items.reshape(top, rows).T
    grid = grid[jax.random.permutation(jax.random.fold_in(own, 1), rows)]
    offset_by = jax.random.randint(jax.random.fold_in(own, 2), (rows, 1), 0, top)
    return jnp.take_along_axis(grid, (jnp.arange(top)[None, :] + offset_by) % top, axis=1)


def shares(number_of, total, reach, lean, full):
    portions = [(1 << 20) // math.isqrt(rank ** lean) + 1 for rank in range(1, number_of + 1)]
    largest = reach if full else min(reach, max(-(-total // number_of), total * portions[0] // sum(portions)))
    least = 1 if total - largest >= number_of - 1 else 0
    given, surplus = [largest] + [least] * (number_of - 1), total - largest - least * (number_of - 1)
    while surplus > 0:
        free = [i for i in range(1, number_of) if given[i] < largest] or [i for i in range(1, number_of) if given[i] < reach]
        mass, remaining = sum([portions[i] for i in free]), surplus
        for i in free:
            extra = min(reach - given[i], max(1, remaining * portions[i] // mass), surplus)
            given[i] = given[i] + extra
            surplus = surplus - extra
    return np.array(given)


def gaussian(own_key, extent, deviation, limit, pieces=(), kind=jnp.bfloat16):
    drawn = jax.random.normal(own_key, extent, jnp.float32) * deviation
    if len(pieces) > 0:
        drawn = block_levels(own_key, extent, pieces, -0.22, 0.18) * drawn
    return jnp.clip(drawn, min=-limit, max=limit).astype(kind)


def setup_inputs(seed: int = 0) -> dict:
    key_of = jax.random.split(jax.random.key(seed), 8)
    tokens = gaussian(key_of[0], (TOKENS, D), 1.0, 6.0, ((0, 32),))
    expert_ids_keys = jax.random.split(jax.random.fold_in(key_of[1], 1), TOKENS // TOK_DEV)
    expert_ids_turns = jax.random.permutation(jax.random.fold_in(key_of[1], 3), TOKENS // TOK_DEV)
    expert_ids = jax.vmap(lambda own, number: routed_block(jax.random.fold_in(key_of[1], 2), own, number, TOK_DEV, EXPERTS, TOPK, CAP, 2))(expert_ids_keys, expert_ids_turns).reshape((TOKENS, TOPK))
    keep_mask = plant((jax.random.randint(key_of[2], (TOKENS, TOPK), 0, 8) < 7).astype(jnp.int32), jax.random.fold_in(key_of[2], 1), 0, 1)
    gate_weights = jnp.clip(0.2 + 0.8 * jax.random.uniform(key_of[3], (TOKENS, TOPK), jnp.float32) ** block_levels(key_of[3], (TOKENS, TOPK), ((0, 32),), -0.2, 0.2), 0.2, 1.0)
    weight_in = gaussian(key_of[4], (EXPERTS, D, FF), D ** -0.5, 0.21875, ((0, 32),))
    weight_out = gaussian(key_of[5], (EXPERTS, FF, D), FF ** -0.5, 0.09375, ((0, 32),))
    grad_output = gaussian(key_of[6], (TOKENS, D), 1.0, 6.0, ((0, 32),))
    return {"tokens": tokens, "expert_ids": expert_ids, "keep_mask": keep_mask, "gate_weights": gate_weights, "weight_in": weight_in, "weight_out": weight_out, "grad_output": grad_output}


def arrival_slots(expert_rows):
    flattened = expert_rows.reshape(-1)
    count_all = flattened.shape[0]
    matching = flattened[:, None] == flattened[None, :]
    positions = jnp.arange(count_all, dtype=jnp.int32)
    earlier = positions[:, None] > positions[None, :]
    return lax.optimization_barrier(jnp.sum((matching & earlier).astype(jnp.int32), axis=1)).reshape(expert_rows.shape).astype(jnp.int32)

def expert_work(quantized, scales, cotangent, weight_in, weight_out):
    block_count = scales.shape[-1]
    restored = (quantized.astype(jnp.float32).reshape(-1, block_count, BLOCK) * scales.astype(jnp.float32)[:, :, None]).reshape(quantized.shape).astype(jnp.bfloat16)
    preact = jnp.dot(restored, weight_in, preferred_element_type=jnp.float32)
    hidden_full, hidden_vjp = jax.vjp(jax.nn.gelu, preact)
    hidden = hidden_full.astype(jnp.bfloat16)
    outputs = jnp.dot(hidden, weight_out, preferred_element_type=jnp.float32).astype(jnp.bfloat16)
    grad_out_w = jnp.dot(hidden.T, cotangent, preferred_element_type=jnp.float32).astype(jnp.bfloat16)
    grad_hidden = jnp.dot(cotangent, weight_out.T, preferred_element_type=jnp.float32)
    grad_preact = hidden_vjp(grad_hidden)[0].astype(jnp.bfloat16)
    grad_in_w = jnp.dot(restored.T, grad_preact, preferred_element_type=jnp.float32).astype(jnp.bfloat16)
    grad_rows = jnp.dot(grad_preact, weight_in.T, preferred_element_type=jnp.float32).astype(jnp.bfloat16)
    return (outputs, grad_rows, grad_in_w, grad_out_w)

def place_rows(values, slot_rows, slot_total):
    empty = jnp.zeros((slot_total,) + values.shape[1:], values.dtype)
    return empty.at[slot_rows].set(values, mode='drop')

def reference(tokens, expert_ids, keep_mask, gate_weights, weight_in, weight_out, grad_output):
    experts = N_ROW * N_COL
    block_count = D // BLOCK
    per_expert = experts * CAP
    slot_total = experts * per_expert
    slot_ids = lax.map(arrival_slots, expert_ids.reshape(TOKENS // TOK_DEV, TOK_DEV, TOPK)).reshape(TOKENS, TOPK)
    blocks = tokens.astype(jnp.float32).reshape(TOKENS, block_count, BLOCK)
    scales = (lax.optimization_barrier(jnp.max(jnp.abs(blocks), axis=2)) + 1e-06).astype(jnp.bfloat16)
    quantized = (blocks / scales.astype(jnp.float32)[:, :, None]).astype(jnp.bfloat16).reshape(TOKENS, D)
    cotangent = (gate_weights[:, :, None] * grad_output.astype(jnp.float32)[:, None, :]).astype(jnp.bfloat16).reshape(TOKENS * TOPK, D)
    source = jnp.arange(TOKENS, dtype=jnp.int32) // TOK_DEV
    kept = keep_mask > 0
    slot_index = expert_ids * per_expert + source[:, None] * CAP + slot_ids
    slot_rows = jnp.where(kept, slot_index, slot_total).reshape(-1)
    slot_quant = place_rows(jnp.repeat(quantized, TOPK, axis=0), slot_rows, slot_total).reshape(experts, per_expert, D)
    slot_scales = place_rows(jnp.repeat(scales, TOPK, axis=0), slot_rows, slot_total).reshape(experts, per_expert, block_count)
    slot_cot = place_rows(cotangent, slot_rows, slot_total).reshape(experts, per_expert, D)

    def one_expert(operands):
        return expert_work(*operands)
    outputs, grad_rows, grad_in_w, grad_out_w = lax.map(one_expert, (slot_quant, slot_scales, slot_cot, weight_in, weight_out))
    pick_rows = jnp.where(kept, slot_index, 0)
    picked_out = outputs.reshape(slot_total, D)[pick_rows].astype(jnp.float32)
    weight_kept = jnp.where(kept, gate_weights, 0.0)
    combined = lax.optimization_barrier(jnp.sum(weight_kept[:, :, None] * picked_out, axis=1)).astype(jnp.bfloat16)
    grad_gates = jnp.where(kept, lax.optimization_barrier(jnp.sum(grad_output.astype(jnp.float32)[:, None, :] * picked_out, axis=2)), 0.0)
    picked_grad = grad_rows.reshape(slot_total, D)[pick_rows].astype(jnp.float32)
    grad_tokens = lax.optimization_barrier(jnp.sum(jnp.where(kept[:, :, None], picked_grad, 0.0), axis=1)).astype(jnp.bfloat16)
    return (combined, grad_tokens, grad_gates, grad_in_w, grad_out_w)
```

```python
import jax
import jax.numpy as jnp
from jax import lax
from jax.sharding import PartitionSpec as P

BLOCK = 128


def arrival_slots(expert_rows):
    flattened = expert_rows.reshape(-1)
    count_all = flattened.shape[0]
    matching = flattened[:, None] == flattened[None, :]
    positions = jnp.arange(count_all, dtype=jnp.int32)
    earlier = positions[:, None] > positions[None, :]
    return jnp.sum((matching & earlier).astype(jnp.int32), axis=1).reshape(expert_rows.shape)


def expert_work(restored, cotangent, weight_in, weight_out):
    preact = jnp.dot(restored, weight_in, preferred_element_type=jnp.float32)
    hidden_full, hidden_vjp = jax.vjp(jax.nn.gelu, preact)
    hidden = hidden_full.astype(jnp.bfloat16)
    outputs = jnp.dot(hidden, weight_out, preferred_element_type=jnp.float32).astype(jnp.bfloat16)
    grad_out_w = jnp.dot(hidden.T, cotangent, preferred_element_type=jnp.float32).astype(
        jnp.bfloat16
    )
    grad_hidden = jnp.dot(cotangent, weight_out.T, preferred_element_type=jnp.float32)
    grad_preact = hidden_vjp(grad_hidden)[0].astype(jnp.bfloat16)
    grad_in_w = jnp.dot(restored.T, grad_preact, preferred_element_type=jnp.float32).astype(
        jnp.bfloat16
    )
    grad_rows = jnp.dot(grad_preact, weight_in.T, preferred_element_type=jnp.float32).astype(
        jnp.bfloat16
    )
    return (outputs, grad_rows, grad_in_w, grad_out_w)


def place_rows(values, slot_rows, slot_total):
    empty = jnp.zeros((slot_total,) + values.shape[1:], values.dtype)
    return empty.at[slot_rows].set(values, mode="drop")


def body(tokens, expert_ids, keep_mask, gate_weights, weight_in, weight_out, grad_output):
    token_rows, width = tokens.shape
    top_count = expert_ids.shape[1]
    row_count = lax.axis_size("row")
    col_count = lax.axis_size("col")
    experts = row_count * col_count
    capacity = 2 * top_count * token_rows // experts
    slot_total = experts * capacity
    block_count = width // BLOCK
    slot_ids = arrival_slots(expert_ids)
    blocks = tokens.astype(jnp.float32).reshape(token_rows, block_count, BLOCK)
    scales = (jnp.max(jnp.abs(blocks), axis=2) + 1e-06).astype(jnp.bfloat16)
    quantized = (blocks / scales.astype(jnp.float32)[:, :, None]).astype(jnp.bfloat16)
    restored = (
        (quantized.astype(jnp.float32) * scales.astype(jnp.float32)[:, :, None])
        .astype(jnp.bfloat16)
        .reshape(token_rows, width)
    )
    cotangent = (
        (gate_weights[:, :, None] * grad_output.astype(jnp.float32)[:, None, :])
        .astype(jnp.bfloat16)
        .reshape(token_rows * top_count, width)
    )
    kept = keep_mask > 0
    slot_index = expert_ids * capacity + slot_ids
    slot_rows = jnp.where(kept, slot_index, slot_total).reshape(-1)
    send_rows = place_rows(jnp.repeat(restored, top_count, axis=0), slot_rows, slot_total)
    send_cot = place_rows(cotangent, slot_rows, slot_total)
    flat_shape = (experts, capacity)
    got_rows, got_cot = (
        lax.all_to_all(
            send_rows.reshape(flat_shape + (width,)),
            ("row", "col"),
            split_axis=0,
            concat_axis=0,
            tiled=True,
        ),
        lax.all_to_all(
            send_cot.reshape(flat_shape + (width,)),
            ("row", "col"),
            split_axis=0,
            concat_axis=0,
            tiled=True,
        ),
    )
    outputs, grad_rows, grad_in_w, grad_out_w = expert_work(
        got_rows.reshape(slot_total, width),
        got_cot.reshape(slot_total, width),
        weight_in[0],
        weight_out[0],
    )
    flat_shape = (experts, capacity, width)
    back_out, back_grad = (
        lax.all_to_all(
            outputs.reshape(flat_shape), ("row", "col"), split_axis=0, concat_axis=0, tiled=True
        ),
        lax.all_to_all(
            grad_rows.reshape(flat_shape), ("row", "col"), split_axis=0, concat_axis=0, tiled=True
        ),
    )
    pick_rows = jnp.where(kept, slot_index, 0)
    picked_out = back_out.reshape(slot_total, width)[pick_rows].astype(jnp.float32)
    weight_kept = jnp.where(kept, gate_weights, 0.0)
    combined = jnp.sum(weight_kept[:, :, None] * picked_out, axis=1).astype(jnp.bfloat16)
    grad_gates = jnp.where(
        kept, jnp.sum(grad_output.astype(jnp.float32)[:, None, :] * picked_out, axis=2), 0.0
    )
    picked_grad = back_grad.reshape(slot_total, width)[pick_rows].astype(jnp.float32)
    grad_tokens = jnp.sum(jnp.where(kept[:, :, None], picked_grad, 0.0), axis=1).astype(
        jnp.bfloat16
    )
    return (combined, grad_tokens, grad_gates, grad_in_w[None], grad_out_w[None])


def solution(mesh):
    placed = (
        P(("row", "col"), None),
        P(("row", "col"), None),
        P(("row", "col"), None),
        P(("row", "col"), None),
        P(("row", "col"), None, None),
        P(("row", "col"), None, None),
        P(("row", "col"), None),
    )
    return jax.shard_map(
        body,
        mesh=mesh,
        in_specs=placed,
        out_specs=(
            P(("row", "col"), None),
            P(("row", "col"), None),
            P(("row", "col"), None),
            P(("row", "col"), None, None),
            P(("row", "col"), None, None),
        ),
        check_vma=False,
    )
```

```python
import functools

import jax
import jax.numpy as jnp
from jax import lax
from jax.experimental import pallas as pl
from jax.experimental.pallas import tpu as pltpu
from jax.sharding import Mesh
from jax.sharding import PartitionSpec as P

BLOCK = 128
BF16 = jnp.bfloat16
F32 = jnp.float32
GROUP = ("row", "rest")
VMEM_LIMIT = 56 * 1024 * 1024


def dot(a, b, contract_a, contract_b):
    return lax.dot_general(
        a, b, (((contract_a,), (contract_b,)), ((), ())), preferred_element_type=F32
    )


def column(row):
    count = row.shape[1]
    return jnp.transpose(jnp.broadcast_to(row, (count, count)))


def route_kernel(rest_bits, capacity, half_ref, ids_ref, keep_ref, gates_ref, mine_ref, other_ref):
    token_rows = ids_ref.shape[1]
    ids = ids_ref[...].astype(F32)
    earlier = lax.broadcasted_iota(jnp.int32, (token_rows, token_rows), 0) < lax.broadcasted_iota(
        jnp.int32, (token_rows, token_rows), 1
    )
    columns = (column(ids[0:1]), column(ids[1:2]))
    half = half_ref[0]
    for k in range(2):
        count = jnp.zeros((token_rows, token_rows), F32)
        for other_choice in columns:
            count = count + jnp.where(earlier & (other_choice == ids[k : k + 1]), 1.0, 0.0)
        slot = jnp.sum(count, axis=0, keepdims=True).astype(jnp.int32)
        expert = ids_ref[k : k + 1, :]
        kept = keep_ref[k : k + 1, :] > 0
        side = (expert >> rest_bits) & 1
        local = ((expert >> (rest_bits + 1)) << rest_bits) + (expert & ((1 << rest_bits) - 1))
        base = local * (2 * capacity) + slot
        here = kept & (side == half)
        there = kept & (side != half)
        mine_ref[k : k + 1, :] = jnp.where(here, base, -1).astype(F32)
        other_ref[k : k + 1, :] = jnp.where(there, base + capacity, -1).astype(F32)
        mine_ref[k + 2 : k + 3, :] = gates_ref[k : k + 1, :]
        other_ref[k + 2 : k + 3, :] = gates_ref[k : k + 1, :]
    mine_ref[4:8, :] = jnp.zeros((4, token_rows), F32)
    other_ref[4:8, :] = jnp.zeros((4, token_rows), F32)


def hits(slot_total, meta_ref, k):
    rows = meta_ref[k : k + 1, :].astype(jnp.int32)
    index = lax.broadcasted_iota(jnp.int32, (slot_total, rows.shape[1]), 0)
    return index == rows


def one_hot(mask):
    return jnp.where(mask, 1.0, 0.0).astype(BF16)


def restore(tokens_ref):
    pieces = []
    for b in range(tokens_ref.shape[1] // BLOCK):
        x = tokens_ref[:, b * BLOCK : (b + 1) * BLOCK].astype(F32)
        scale = (jnp.max(jnp.abs(x), axis=1, keepdims=True) + 1e-06).astype(BF16).astype(F32)
        quantized = (x / scale).astype(BF16)
        pieces.append((quantized.astype(F32) * scale).astype(BF16))
    return jnp.concatenate(pieces, axis=1)


def place_tokens_kernel(own_ref, partner_ref, own_meta, partner_meta, out_ref):
    slot_total = out_ref.shape[0]
    total = None
    for tokens_ref, meta in ((own_ref, own_meta), (partner_ref, partner_meta)):
        mask = hits(slot_total, meta, 0) | hits(slot_total, meta, 1)
        part = dot(one_hot(mask), restore(tokens_ref), 1, 0)
        total = part if total is None else total + part
    out_ref[...] = total.astype(BF16)


def scaled_rows(gate_row, grad_ref):
    gate = column(gate_row)
    pieces = [
        gate * grad_ref[:, b * BLOCK : (b + 1) * BLOCK].astype(F32)
        for b in range(grad_ref.shape[1] // BLOCK)
    ]
    return jnp.concatenate(pieces, axis=1)


def place_cotangents_kernel(own_ref, partner_ref, own_meta, partner_meta, out_ref):
    slot_total = out_ref.shape[0]
    total = None
    for grad_ref, meta in ((own_ref, own_meta), (partner_ref, partner_meta)):
        for k in range(2):
            rows = scaled_rows(meta[k + 2 : k + 3, :], grad_ref).astype(BF16)
            part = dot(one_hot(hits(slot_total, meta, k)), rows, 1, 0)
            total = part if total is None else total + part
    out_ref[...] = total.astype(BF16)


def forward_kernel(x_ref, w_in_ref, w_out_ref, hidden_ref, slope_ref, out_ref, total):
    step = pl.program_id(0)
    v = dot(x_ref[...], w_in_ref[...], 1, 0)
    c = 0.7978845608028654
    square = v * v
    t = jnp.tanh(v * (c + (c * 0.044715) * square))
    half = 0.5 + 0.5 * t
    hidden = (v * half).astype(BF16)
    slope_ref[...] = half + (0.5 * v) * (1.0 - t * t) * (c + (3 * c * 0.044715) * square)
    hidden_ref[...] = hidden

    @pl.when(step == 0)
    def _():
        total[...] = jnp.zeros_like(total)

    total[...] += dot(hidden, w_out_ref[...], 1, 0)

    @pl.when(step == pl.num_programs(0) - 1)
    def _():
        out_ref[...] = total[...].astype(BF16)


def backward_kernel(cot_ref, w_in_ref, w_out_ref, slope_ref, grad_pre_ref, out_ref, total):
    step = pl.program_id(0)
    grad_hidden = dot(cot_ref[...], w_out_ref[...], 1, 1)
    grad_pre = (grad_hidden * slope_ref[...]).astype(BF16)
    grad_pre_ref[...] = grad_pre

    @pl.when(step == 0)
    def _():
        total[...] = jnp.zeros_like(total)

    total[...] += dot(grad_pre, w_in_ref[...], 1, 1)

    @pl.when(step == pl.num_programs(0) - 1)
    def _():
        out_ref[...] = total[...].astype(BF16)


def weights_kernel(x_ref, cot_ref, hidden_ref, grad_pre_ref, grad_in_ref, grad_out_ref):
    grad_in_ref[...] = dot(x_ref[...], grad_pre_ref[...], 0, 0).astype(BF16)
    grad_out_ref[...] = dot(hidden_ref[...], cot_ref[...], 0, 0).astype(BF16)


def pick_outputs_kernel(
    back_ref, own_grad, partner_grad, own_meta, partner_meta, own_out, partner_out, own_gates, partner_gates
):
    slot_total = back_ref.shape[0]
    for grad_ref, meta, out_ref, gates_ref in (
        (own_grad, own_meta, own_out, own_gates),
        (partner_grad, partner_meta, partner_out, partner_gates),
    ):
        total = None
        for k in range(2):
            picked = dot(one_hot(hits(slot_total, meta, k)), back_ref[...], 0, 0)
            gate = column(meta[k + 2 : k + 3, :])
            pieces = [
                gate * picked[:, b * BLOCK : (b + 1) * BLOCK]
                for b in range(picked.shape[1] // BLOCK)
            ]
            weighted = jnp.concatenate(pieces, axis=1)
            total = weighted if total is None else total + weighted
            sums = jnp.sum(picked * grad_ref[...].astype(F32), axis=1, keepdims=True)
            rows = jnp.transpose(jnp.broadcast_to(sums, (sums.shape[0], sums.shape[0])))
            gates_ref[k : k + 1, :] = rows[0:1, :]
        out_ref[...] = total.astype(out_ref.dtype)


def pick_gradients_kernel(back_ref, own_meta, partner_meta, own_out, partner_out):
    slot_total = back_ref.shape[0]
    for meta, out_ref in ((own_meta, own_out), (partner_meta, partner_out)):
        mask = hits(slot_total, meta, 0) | hits(slot_total, meta, 1)
        out_ref[...] = dot(one_hot(mask), back_ref[...], 0, 0).astype(out_ref.dtype)


def call(kernel, outs, flops=0, traffic=0, **options):
    shapes = [jax.ShapeDtypeStruct(shape, dtype) for shape, dtype in outs]
    return pl.pallas_call(
        kernel,
        out_shape=shapes if len(shapes) > 1 else shapes[0],
        compiler_params=pltpu.CompilerParams(vmem_limit_bytes=VMEM_LIMIT),
        cost_estimate=pl.CostEstimate(flops=flops, bytes_accessed=traffic, transcendentals=0),
        **options,
    )


def body(tokens, expert_ids, keep_mask, gate_weights, weight_in, weight_out, grad_output):
    token_rows, width = tokens.shape
    hidden_width = weight_in.shape[2]
    rest_count = lax.axis_size("rest")
    members = lax.axis_size("row") * rest_count
    experts = 2 * members
    capacity = 2 * expert_ids.shape[1] * token_rows // experts
    slot_total = experts * capacity
    swap = ((0, 1), (1, 0))

    def exchange(values):
        return lax.ppermute(values, "half", swap)

    def shuffle(rows):
        shaped = rows.reshape(members, 2 * capacity, width)
        return lax.all_to_all(shaped, GROUP, split_axis=0, concat_axis=0, tiled=True).reshape(
            slot_total, width
        )

    partner_tokens = exchange(tokens)
    partner_grad = exchange(grad_output)
    half = lax.axis_index("half").astype(jnp.int32).reshape(1)
    meta_shape = ((8, token_rows), F32)
    vmem = pl.BlockSpec(memory_space=pltpu.VMEM)
    own_meta, sent_meta = call(
        functools.partial(route_kernel, rest_count.bit_length() - 1, capacity),
        [meta_shape, meta_shape],
        in_specs=[pl.BlockSpec(memory_space=pltpu.SMEM), vmem, vmem, vmem],
        traffic=8 * token_rows * 8,
    )(half, expert_ids.T, keep_mask.T, gate_weights.T)
    partner_meta = exchange(sent_meta)

    slot_shape = ((slot_total, width), BF16)
    slot_bytes = slot_total * width * 2
    token_bytes = token_rows * width * 2
    place_flops = 2 * slot_total * 2 * token_rows * width
    sent = call(place_tokens_kernel, [slot_shape], place_flops, 2 * token_bytes + slot_bytes)(
        tokens, partner_tokens, own_meta, partner_meta
    )
    x = shuffle(sent)
    sent_cot = call(
        place_cotangents_kernel, [slot_shape], 2 * place_flops, 2 * token_bytes + slot_bytes
    )(grad_output, partner_grad, own_meta, partner_meta)
    cot = shuffle(sent_cot)

    chunk = 512
    steps = hidden_width // chunk
    whole = pl.BlockSpec((slot_total, width), lambda i: (0, 0))
    in_spec = pl.BlockSpec((None, width, chunk), lambda i: (0, 0, i))
    out_spec = pl.BlockSpec((None, chunk, width), lambda i: (0, i, 0))
    mid_spec = pl.BlockSpec((slot_total, chunk), lambda i: (0, i))
    mid = (slot_total, hidden_width)
    product = 2 * slot_total * width * hidden_width
    weight_bytes = 2 * 2 * width * hidden_width
    mid_count = slot_total * hidden_width
    hidden, slope, outputs = call(
        forward_kernel,
        [(mid, BF16), (mid, F32), slot_shape],
        2 * product,
        2 * slot_bytes + weight_bytes + 6 * mid_count,
        grid=(steps,),
        in_specs=[whole, in_spec, out_spec],
        out_specs=[mid_spec, mid_spec, whole],
        scratch_shapes=[pltpu.VMEM((slot_total, width), F32)],
    )(x, weight_in, weight_out)
    back_out = shuffle(outputs)
    grad_pre, grad_rows = call(
        backward_kernel,
        [(mid, BF16), slot_shape],
        2 * product,
        2 * slot_bytes + weight_bytes + 6 * mid_count,
        grid=(steps,),
        in_specs=[whole, in_spec, out_spec, mid_spec],
        out_specs=[mid_spec, whole],
        scratch_shapes=[pltpu.VMEM((slot_total, width), F32)],
    )(cot, weight_in, weight_out, slope)
    back_grad = shuffle(grad_rows)
    own_shape, partner_shape = ((token_rows, width), F32), ((token_rows, width), BF16)
    gates_shape = ((2, token_rows), F32)
    own_out, partner_out, own_gates, partner_gates = call(
        pick_outputs_kernel,
        [own_shape, partner_shape, gates_shape, gates_shape],
        2 * place_flops,
        2 * token_bytes + slot_bytes,
    )(back_out, grad_output, partner_grad, own_meta, partner_meta)
    grad_in_w, grad_out_w = call(
        weights_kernel,
        [(weight_in.shape, BF16), (weight_out.shape, BF16)],
        2 * product,
        2 * slot_bytes + weight_bytes + 4 * mid_count,
        grid=(steps,),
        in_specs=[whole, whole, mid_spec, mid_spec],
        out_specs=[in_spec, out_spec],
    )(x, cot, hidden, grad_pre)
    combined = (own_out + exchange(partner_out).astype(F32)).astype(BF16)
    grad_gates = (own_gates + exchange(partner_gates)).T
    own_back, partner_back = call(
        pick_gradients_kernel, [own_shape, partner_shape], place_flops, slot_bytes + 3 * token_bytes
    )(back_grad, own_meta, partner_meta)
    grad_tokens = (own_back + exchange(partner_back).astype(F32)).astype(BF16)
    return (combined, grad_tokens, grad_gates, grad_in_w, grad_out_w)


def solution(mesh):
    row_count, col_count = mesh.devices.shape
    split = Mesh(
        mesh.devices.reshape(row_count, 2, col_count // 2), ("row", "half", "rest")
    )
    axes = ("row", "half", "rest")
    flat = P(axes, None)
    deep = P(axes, None, None)
    return jax.shard_map(
        body,
        mesh=split,
        in_specs=(flat, flat, flat, flat, deep, deep, flat),
        out_specs=(flat, flat, flat, deep, deep),
        check_vma=False,
    )
```

```python
import functools

import jax
import jax.numpy as jnp
from jax import lax
from jax.experimental import pallas as pl
from jax.experimental.pallas import tpu as pltpu
from jax.sharding import Mesh
from jax.sharding import PartitionSpec as P

BLOCK = 128
BF16 = jnp.bfloat16
F32 = jnp.float32
GROUP = ("row", "rest")
MIB = 1024 * 1024
SUB = 256


def dot(a, b, contract_a, contract_b):
    return lax.dot_general(
        a, b, (((contract_a,), (contract_b,)), ((), ())), preferred_element_type=F32
    )


def column(row):
    count = row.shape[1]
    return jnp.transpose(jnp.broadcast_to(row, (count, count)))


def route_kernel(rest_bits, capacity, half_ref, ids_ref, keep_ref, gates_ref, mine_ref, other_ref):
    token_rows = ids_ref.shape[1]
    ids = ids_ref[...].astype(F32)
    earlier = lax.broadcasted_iota(jnp.int32, (token_rows, token_rows), 0) < lax.broadcasted_iota(
        jnp.int32, (token_rows, token_rows), 1
    )
    columns = (column(ids[0:1]), column(ids[1:2]))
    half = half_ref[0]
    for k in range(2):
        count = jnp.zeros((token_rows, token_rows), F32)
        for other_choice in columns:
            count = count + jnp.where(earlier & (other_choice == ids[k : k + 1]), 1.0, 0.0)
        slot = jnp.sum(count, axis=0, keepdims=True).astype(jnp.int32)
        expert = ids_ref[k : k + 1, :]
        kept = keep_ref[k : k + 1, :] > 0
        side = (expert >> rest_bits) & 1
        local = ((expert >> (rest_bits + 1)) << rest_bits) + (expert & ((1 << rest_bits) - 1))
        base = local * (2 * capacity) + slot
        here = kept & (side == half)
        there = kept & (side != half)
        mine_ref[k : k + 1, :] = jnp.where(here, base, -1).astype(F32)
        other_ref[k : k + 1, :] = jnp.where(there, base + capacity, -1).astype(F32)
        mine_ref[k + 2 : k + 3, :] = gates_ref[k : k + 1, :]
        other_ref[k + 2 : k + 3, :] = gates_ref[k : k + 1, :]
    mine_ref[4:8, :] = jnp.zeros((4, token_rows), F32)
    other_ref[4:8, :] = jnp.zeros((4, token_rows), F32)


def hits(slot_total, meta_ref, k):
    rows = meta_ref[k : k + 1, :].astype(jnp.int32)
    index = lax.broadcasted_iota(jnp.int32, (slot_total, rows.shape[1]), 0)
    return index == rows


def one_hot(mask):
    return jnp.where(mask, 1.0, 0.0).astype(BF16)


def restore(tokens_ref):
    pieces = []
    for b in range(tokens_ref.shape[1] // BLOCK):
        x = tokens_ref[:, b * BLOCK : (b + 1) * BLOCK].astype(F32)
        scale = (jnp.max(jnp.abs(x), axis=1, keepdims=True) + 1e-06).astype(BF16).astype(F32)
        quantized = (x / scale).astype(BF16)
        pieces.append((quantized.astype(F32) * scale).astype(BF16))
    return jnp.concatenate(pieces, axis=1)


def place_tokens_kernel(own_ref, partner_ref, own_meta, partner_meta, out_ref):
    slot_total = out_ref.shape[0]
    total = None
    for tokens_ref, meta in ((own_ref, own_meta), (partner_ref, partner_meta)):
        mask = hits(slot_total, meta, 0) | hits(slot_total, meta, 1)
        part = dot(one_hot(mask), restore(tokens_ref), 1, 0)
        total = part if total is None else total + part
    out_ref[...] = total.astype(BF16)


def scaled_rows(gate_row, grad_ref):
    gate = column(gate_row)
    pieces = [
        gate * grad_ref[:, b * BLOCK : (b + 1) * BLOCK].astype(F32)
        for b in range(grad_ref.shape[1] // BLOCK)
    ]
    return jnp.concatenate(pieces, axis=1)


def place_cotangents_kernel(own_ref, partner_ref, own_meta, partner_meta, out_ref):
    slot_total = out_ref.shape[0]
    total = None
    for grad_ref, meta in ((own_ref, own_meta), (partner_ref, partner_meta)):
        for k in range(2):
            rows = scaled_rows(meta[k + 2 : k + 3, :], grad_ref).astype(BF16)
            part = dot(one_hot(hits(slot_total, meta, k)), rows, 1, 0)
            total = part if total is None else total + part
    out_ref[...] = total.astype(BF16)


def gelu_parts(v):
    c = 0.7978845608028654
    inner = c + (c * 0.044715) * (v * v)
    s = 0.5 + 0.5 * jnp.tanh(v * inner)
    hidden = v * s
    slope = s + (hidden * (1.0 - s)) * (6.0 * inner - 4.0 * c)
    return hidden.astype(BF16), slope.astype(BF16)


def forward_kernel(x_ref, w_in_ref, w_out_ref, hidden_ref, slope_ref, out_ref, total):
    step = pl.program_id(0)

    @pl.when(step == 0)
    def _():
        total[...] = jnp.zeros_like(total)

    parts = hidden_ref.shape[1] // SUB
    v = dot(x_ref[...], w_in_ref[:, :SUB], 1, 0)
    pieces = []
    for j in range(parts):
        if j + 1 < parts:
            after = dot(x_ref[...], w_in_ref[:, (j + 1) * SUB : (j + 2) * SUB], 1, 0)
        hidden, slope = gelu_parts(v)
        hidden_ref[:, j * SUB : (j + 1) * SUB] = hidden
        slope_ref[:, j * SUB : (j + 1) * SUB] = slope
        pieces.append(hidden)
        v = after
    total[...] += dot(jnp.concatenate(pieces, axis=1), w_out_ref[...], 1, 0)

    @pl.when(step == pl.num_programs(0) - 1)
    def _():
        out_ref[...] = total[...].astype(BF16)


def backward_kernel(cot_ref, w_in_ref, w_out_ref, slope_ref, grad_pre_ref, out_ref, total):
    step = pl.program_id(0)

    @pl.when(step == 0)
    def _():
        total[...] = jnp.zeros_like(total)

    parts = grad_pre_ref.shape[1] // SUB
    pieces = []
    for j in range(parts):
        grad_hidden = dot(cot_ref[...], w_out_ref[j * SUB : (j + 1) * SUB, :], 1, 1)
        slope = slope_ref[:, j * SUB : (j + 1) * SUB].astype(F32)
        grad_pre = (grad_hidden * slope).astype(BF16)
        grad_pre_ref[:, j * SUB : (j + 1) * SUB] = grad_pre
        pieces.append(grad_pre)
    total[...] += dot(jnp.concatenate(pieces, axis=1), w_in_ref[...], 1, 1)

    @pl.when(step == pl.num_programs(0) - 1)
    def _():
        out_ref[...] = total[...].astype(BF16)


def weights_kernel(x_ref, cot_ref, hidden_ref, grad_pre_ref, grad_in_ref, grad_out_ref):
    grad_in_ref[...] = dot(x_ref[...], grad_pre_ref[...], 0, 0).astype(BF16)
    grad_out_ref[...] = dot(hidden_ref[...], cot_ref[...], 0, 0).astype(BF16)


def pick_outputs_kernel(
    back_ref, own_grad, partner_grad, own_meta, partner_meta, own_out, partner_out, own_gates, partner_gates
):
    slot_total = back_ref.shape[0]
    for grad_ref, meta, out_ref, gates_ref in (
        (own_grad, own_meta, own_out, own_gates),
        (partner_grad, partner_meta, partner_out, partner_gates),
    ):
        total = None
        for k in range(2):
            picked = dot(one_hot(hits(slot_total, meta, k)), back_ref[...], 0, 0)
            gate = column(meta[k + 2 : k + 3, :])
            pieces = [
                gate * picked[:, b * BLOCK : (b + 1) * BLOCK]
                for b in range(picked.shape[1] // BLOCK)
            ]
            weighted = jnp.concatenate(pieces, axis=1)
            total = weighted if total is None else total + weighted
            sums = jnp.sum(picked * grad_ref[...].astype(F32), axis=1, keepdims=True)
            rows = jnp.transpose(jnp.broadcast_to(sums, (sums.shape[0], sums.shape[0])))
            gates_ref[k : k + 1, :] = rows[0:1, :]
        out_ref[...] = total.astype(out_ref.dtype)


def pick_gradients_kernel(back_ref, own_meta, partner_meta, own_out, partner_out):
    slot_total = back_ref.shape[0]
    for meta, out_ref in ((own_meta, own_out), (partner_meta, partner_out)):
        mask = hits(slot_total, meta, 0) | hits(slot_total, meta, 1)
        out_ref[...] = dot(one_hot(mask), back_ref[...], 0, 0).astype(out_ref.dtype)


def finish_kernel(
    own_out, got_out, own_back, got_back, own_gates, got_gates, combined, grad_tokens, grad_gates
):
    combined[...] = (own_out[...] + got_out[...].astype(F32)).astype(BF16)
    grad_tokens[...] = (own_back[...] + got_back[...].astype(F32)).astype(BF16)
    grad_gates[...] = own_gates[...] + got_gates[...]


def call(kernel, outs, flops=0, traffic=0, limit=12, **options):
    shapes = [jax.ShapeDtypeStruct(shape, dtype) for shape, dtype in outs]
    return pl.pallas_call(
        kernel,
        out_shape=shapes if len(shapes) > 1 else shapes[0],
        compiler_params=pltpu.CompilerParams(vmem_limit_bytes=limit * MIB),
        cost_estimate=pl.CostEstimate(flops=flops, bytes_accessed=traffic, transcendentals=0),
        **options,
    )


def body(tokens, expert_ids, keep_mask, gate_weights, weight_in, weight_out, grad_output):
    token_rows, width = tokens.shape
    hidden_width = weight_in.shape[2]
    rest_count = lax.axis_size("rest")
    members = lax.axis_size("row") * rest_count
    experts = 2 * members
    capacity = 2 * expert_ids.shape[1] * token_rows // experts
    slot_total = experts * capacity
    swap = ((0, 1), (1, 0))

    def exchange(values):
        return lax.ppermute(values, "half", swap)

    def shuffle(rows):
        shaped = rows.reshape(members, 2 * capacity, width)
        return lax.all_to_all(shaped, GROUP, split_axis=0, concat_axis=0, tiled=True).reshape(
            slot_total, width
        )

    partner_tokens = exchange(tokens)
    partner_grad = exchange(grad_output)
    half = lax.axis_index("half").astype(jnp.int32).reshape(1)
    meta_shape = ((8, token_rows), F32)
    vmem = pl.BlockSpec(memory_space=pltpu.VMEM)
    own_meta, sent_meta = call(
        functools.partial(route_kernel, rest_count.bit_length() - 1, capacity),
        [meta_shape, meta_shape],
        in_specs=[pl.BlockSpec(memory_space=pltpu.SMEM), vmem, vmem, vmem],
        traffic=8 * token_rows * 8,
    )(half, expert_ids.T, keep_mask.T, gate_weights.T)
    partner_meta = exchange(sent_meta)

    slot_shape = ((slot_total, width), BF16)
    slot_bytes = slot_total * width * 2
    token_bytes = token_rows * width * 2
    place_flops = 2 * slot_total * 2 * token_rows * width
    sent = call(place_tokens_kernel, [slot_shape], place_flops, 2 * token_bytes + slot_bytes)(
        tokens, partner_tokens, own_meta, partner_meta
    )
    x = shuffle(sent)
    sent_cot = call(
        place_cotangents_kernel, [slot_shape], 40 * place_flops, 2 * token_bytes + slot_bytes
    )(grad_output, partner_grad, own_meta, partner_meta)
    cot = shuffle(sent_cot)

    chunk = 1024
    steps = hidden_width // chunk
    whole = pl.BlockSpec((slot_total, width), lambda i: (0, 0))
    in_spec = pl.BlockSpec((None, width, chunk), lambda i: (0, 0, i))
    out_spec = pl.BlockSpec((None, chunk, width), lambda i: (0, i, 0))
    mid_spec = pl.BlockSpec((slot_total, chunk), lambda i: (0, i))
    mid = (slot_total, hidden_width)
    product = 2 * slot_total * width * hidden_width
    weight_bytes = 2 * 2 * width * hidden_width
    mid_count = slot_total * hidden_width
    hidden, slope, outputs = call(
        forward_kernel,
        [(mid, BF16), (mid, BF16), slot_shape],
        2 * product,
        2 * slot_bytes + weight_bytes + 4 * mid_count,
        32,
        grid=(steps,),
        in_specs=[whole, in_spec, out_spec],
        out_specs=[mid_spec, mid_spec, whole],
        scratch_shapes=[pltpu.VMEM((slot_total, width), F32)],
    )(x, weight_in, weight_out)
    back_out = shuffle(outputs)
    grad_pre, grad_rows = call(
        backward_kernel,
        [(mid, BF16), slot_shape],
        2 * product,
        2 * slot_bytes + weight_bytes + 4 * mid_count,
        32,
        grid=(steps,),
        in_specs=[whole, in_spec, out_spec, mid_spec],
        out_specs=[mid_spec, whole],
        scratch_shapes=[pltpu.VMEM((slot_total, width), F32)],
    )(cot, weight_in, weight_out, slope)
    back_grad = shuffle(grad_rows)
    own_shape, partner_shape = ((token_rows, width), F32), ((token_rows, width), BF16)
    gates_shape = ((2, token_rows), F32)
    own_out, partner_out, own_gates, partner_gates = call(
        pick_outputs_kernel,
        [own_shape, partner_shape, gates_shape, gates_shape],
        2 * place_flops,
        2 * token_bytes + slot_bytes,
    )(back_out, grad_output, partner_grad, own_meta, partner_meta)
    grad_pre, partner_out, partner_gates = lax.optimization_barrier(
        (grad_pre, partner_out, partner_gates)
    )
    grad_in_w, grad_out_w = call(
        weights_kernel,
        [(weight_in.shape, BF16), (weight_out.shape, BF16)],
        2 * product,
        2 * slot_bytes + weight_bytes + 4 * mid_count,
        32,
        grid=(steps,),
        in_specs=[whole, whole, mid_spec, mid_spec],
        out_specs=[in_spec, out_spec],
    )(x, cot, hidden, grad_pre)
    got_out, got_gates = exchange(partner_out), exchange(partner_gates)
    own_back, partner_back = call(
        pick_gradients_kernel, [own_shape, partner_shape], place_flops, slot_bytes + 3 * token_bytes
    )(back_grad, own_meta, partner_meta)
    got_back = exchange(partner_back)
    combined, grad_tokens, grad_gates = call(
        finish_kernel, [partner_shape, partner_shape, gates_shape], 0, 8 * token_bytes
    )(own_out, got_out, own_back, got_back, own_gates, got_gates)
    return (combined, grad_tokens, grad_gates.T, grad_in_w, grad_out_w)


def solution(mesh):
    row_count, col_count = mesh.devices.shape
    split = Mesh(
        mesh.devices.reshape(row_count, 2, col_count // 2), ("row", "half", "rest")
    )
    axes = ("row", "half", "rest")
    flat = P(axes, None)
    deep = P(axes, None, None)
    return jax.shard_map(
        body,
        mesh=split,
        in_specs=(flat, flat, flat, flat, deep, deep, flat),
        out_specs=(flat, flat, flat, deep, deep),
        check_vma=False,
    )
```

```python
import functools

import jax
import jax.numpy as jnp
from jax import lax
from jax.experimental import pallas as pl
from jax.experimental.pallas import tpu as pltpu
from jax.sharding import Mesh
from jax.sharding import PartitionSpec as P

BLOCK = 128
BF16 = jnp.bfloat16
F32 = jnp.float32
GROUP = ("row", "rest")
MIB = 1024 * 1024
SUB = 256


def dot(a, b, contract_a, contract_b):
    return lax.dot_general(
        a, b, (((contract_a,), (contract_b,)), ((), ())), preferred_element_type=F32
    )


def column(row):
    count = row.shape[1]
    return jnp.transpose(jnp.broadcast_to(row, (count, count)))


def route_kernel(rest_bits, capacity, place_ref, ids_ref, keep_ref, gates_ref, mine_ref, other_ref):
    token_rows = ids_ref.shape[1]
    ids = ids_ref[...].astype(F32)
    earlier = lax.broadcasted_iota(jnp.int32, (token_rows, token_rows), 0) < lax.broadcasted_iota(
        jnp.int32, (token_rows, token_rows), 1
    )
    columns = (column(ids[0:1]), column(ids[1:2]))
    half, member = place_ref[0], place_ref[1]
    for k in range(2):
        count = jnp.zeros((token_rows, token_rows), F32)
        for other_choice in columns:
            count = count + jnp.where(earlier & (other_choice == ids[k : k + 1]), 1.0, 0.0)
        slot = jnp.sum(count, axis=0, keepdims=True).astype(jnp.int32)
        expert = ids_ref[k : k + 1, :]
        kept = keep_ref[k : k + 1, :] > 0
        side = (expert >> rest_bits) & 1
        local = ((expert >> (rest_bits + 1)) << rest_bits) + (expert & ((1 << rest_bits) - 1))
        base = (local ^ member) * (2 * capacity) + slot
        here = kept & (side == half)
        there = kept & (side != half)
        mine_ref[k : k + 1, :] = jnp.where(here, base, -1).astype(F32)
        other_ref[k : k + 1, :] = jnp.where(there, base + capacity, -1).astype(F32)
        mine_ref[k + 2 : k + 3, :] = gates_ref[k : k + 1, :]
        other_ref[k + 2 : k + 3, :] = gates_ref[k : k + 1, :]
    mine_ref[4:8, :] = jnp.zeros((4, token_rows), F32)
    other_ref[4:8, :] = jnp.zeros((4, token_rows), F32)


def hits(slot_total, meta_ref, k):
    rows = meta_ref[k : k + 1, :].astype(jnp.int32)
    index = lax.broadcasted_iota(jnp.int32, (slot_total, rows.shape[1]), 0)
    return index == rows


def one_hot(mask):
    return jnp.where(mask, 1.0, 0.0).astype(BF16)


def restore(tokens_ref):
    pieces = []
    for b in range(tokens_ref.shape[1] // BLOCK):
        x = tokens_ref[:, b * BLOCK : (b + 1) * BLOCK].astype(F32)
        scale = (jnp.max(jnp.abs(x), axis=1, keepdims=True) + 1e-06).astype(BF16).astype(F32)
        quantized = (x / scale).astype(BF16)
        pieces.append((quantized.astype(F32) * scale).astype(BF16))
    return jnp.concatenate(pieces, axis=1)


def split(values, out_refs):
    rows = out_refs[0].shape[0]
    for d, out_ref in enumerate(out_refs):
        out_ref[...] = values[d * rows : (d + 1) * rows, :]


def join(refs):
    return jnp.concatenate([ref[...] for ref in refs], axis=0)


def place_tokens_kernel(own_ref, partner_ref, own_meta, partner_meta, *out_refs):
    slot_total = len(out_refs) * out_refs[0].shape[0]
    total = None
    for tokens_ref, meta in ((own_ref, own_meta), (partner_ref, partner_meta)):
        mask = hits(slot_total, meta, 0) | hits(slot_total, meta, 1)
        part = dot(one_hot(mask), restore(tokens_ref), 1, 0)
        total = part if total is None else total + part
    split(total.astype(BF16), out_refs)


def scaled_rows(gate_row, grad_ref):
    gate = column(gate_row)
    pieces = [
        gate * grad_ref[:, b * BLOCK : (b + 1) * BLOCK].astype(F32)
        for b in range(grad_ref.shape[1] // BLOCK)
    ]
    return jnp.concatenate(pieces, axis=1)


def place_cotangents_kernel(own_ref, partner_ref, own_meta, partner_meta, *out_refs):
    slot_total = len(out_refs) * out_refs[0].shape[0]
    total = None
    for grad_ref, meta in ((own_ref, own_meta), (partner_ref, partner_meta)):
        for k in range(2):
            rows = scaled_rows(meta[k + 2 : k + 3, :], grad_ref).astype(BF16)
            part = dot(one_hot(hits(slot_total, meta, k)), rows, 1, 0)
            total = part if total is None else total + part
    split(total.astype(BF16), out_refs)


def gelu_parts(v):
    c = 0.7978845608028654
    inner = c + (c * 0.044715) * (v * v)
    s = 0.5 + 0.5 * jnp.tanh(v * inner)
    hidden = v * s
    slope = s + (hidden * (1.0 - s)) * (6.0 * inner - 4.0 * c)
    return hidden.astype(BF16), slope.astype(BF16)


def stream(step, chunk, width, slots, refs, kinds):
    specs = {
        "wide": pl.BlockSpec((None, width, chunk), lambda i: (0, 0, i)),
        "tall": pl.BlockSpec((None, chunk, width), lambda i: (0, i, 0)),
        "middle": pl.BlockSpec((slots, chunk), lambda i: (0, i)),
    }
    ins, outs = kinds
    steps = refs[0].shape[2] // chunk
    pltpu.emit_pipeline(
        step,
        grid=(steps,),
        in_specs=[specs[kind] for kind in ins],
        out_specs=[specs[kind] for kind in outs],
    )(*refs)


def forward_kernel(pieces, chunk, *refs):
    x_pieces, (w_in, w_out) = refs[:pieces], refs[pieces : pieces + 2]
    out_pieces = refs[pieces + 2 : 2 * pieces + 2]
    x, hidden_all, slope_all, total = refs[2 * pieces + 2 :]
    x[...] = join(x_pieces)
    total[...] = jnp.zeros_like(total)

    def step(w_in_ref, w_out_ref, hidden_ref, slope_ref):
        parts = chunk // SUB
        v = dot(x[...], w_in_ref[:, :SUB], 1, 0)
        done = []
        for j in range(parts):
            if j + 1 < parts:
                after = dot(x[...], w_in_ref[:, (j + 1) * SUB : (j + 2) * SUB], 1, 0)
            hidden, slope = gelu_parts(v)
            hidden_ref[:, j * SUB : (j + 1) * SUB] = hidden
            slope_ref[:, j * SUB : (j + 1) * SUB] = slope
            done.append(hidden)
            v = after
        total[...] += dot(jnp.concatenate(done, axis=1), w_out_ref[...], 1, 0)

    stream(
        step,
        chunk,
        x.shape[1],
        x.shape[0],
        (w_in, w_out, hidden_all, slope_all),
        (("wide", "tall"), ("middle", "middle")),
    )
    split(total[...].astype(BF16), out_pieces)


def backward_kernel(pieces, chunk, *refs):
    cot_pieces, (w_in, w_out, slope_all) = refs[:pieces], refs[pieces : pieces + 3]
    out_pieces = refs[pieces + 3 : 2 * pieces + 3]
    cot, grad_pre_all, total = refs[2 * pieces + 3 :]
    cot[...] = join(cot_pieces)
    total[...] = jnp.zeros_like(total)

    def step(w_in_ref, w_out_ref, slope_ref, grad_pre_ref):
        done = []
        for j in range(chunk // SUB):
            grad_hidden = dot(cot[...], w_out_ref[j * SUB : (j + 1) * SUB, :], 1, 1)
            slope = slope_ref[:, j * SUB : (j + 1) * SUB].astype(F32)
            grad_pre = (grad_hidden * slope).astype(BF16)
            grad_pre_ref[:, j * SUB : (j + 1) * SUB] = grad_pre
            done.append(grad_pre)
        total[...] += dot(jnp.concatenate(done, axis=1), w_in_ref[...], 1, 1)

    stream(
        step,
        chunk,
        cot.shape[1],
        cot.shape[0],
        (w_in, w_out, slope_all, grad_pre_all),
        (("wide", "tall", "middle"), ("middle",)),
    )
    split(total[...].astype(BF16), out_pieces)


def weights_kernel(chunk, x, cot, hidden_all, grad_pre_all, grad_in_all, grad_out_all):
    def step(hidden_ref, grad_pre_ref, grad_in_ref, grad_out_ref):
        grad_in_ref[...] = dot(x[...], grad_pre_ref[...], 0, 0).astype(BF16)
        grad_out_ref[...] = dot(hidden_ref[...], cot[...], 0, 0).astype(BF16)

    slots, width = x.shape
    pltpu.emit_pipeline(
        step,
        grid=(hidden_all.shape[1] // chunk,),
        in_specs=[pl.BlockSpec((slots, chunk), lambda i: (0, i))] * 2,
        out_specs=[
            pl.BlockSpec((None, width, chunk), lambda i: (0, 0, i)),
            pl.BlockSpec((None, chunk, width), lambda i: (0, i, 0)),
        ],
    )(hidden_all, grad_pre_all, grad_in_all, grad_out_all)


def pick_outputs_kernel(pieces, *refs):
    back = join(refs[:pieces])
    own_grad, partner_grad, own_meta, partner_meta = refs[pieces : pieces + 4]
    own_out, partner_out, own_gates, partner_gates = refs[pieces + 4 :]
    slot_total = back.shape[0]
    for grad_ref, meta, out_ref, gates_ref in (
        (own_grad, own_meta, own_out, own_gates),
        (partner_grad, partner_meta, partner_out, partner_gates),
    ):
        total = None
        for k in range(2):
            picked = dot(one_hot(hits(slot_total, meta, k)), back, 0, 0)
            gate = column(meta[k + 2 : k + 3, :])
            weighted = jnp.concatenate(
                [
                    gate * picked[:, b * BLOCK : (b + 1) * BLOCK]
                    for b in range(picked.shape[1] // BLOCK)
                ],
                axis=1,
            )
            total = weighted if total is None else total + weighted
            sums = jnp.sum(picked * grad_ref[...].astype(F32), axis=1, keepdims=True)
            rows = jnp.transpose(jnp.broadcast_to(sums, (sums.shape[0], sums.shape[0])))
            gates_ref[k : k + 1, :] = rows[0:1, :]
        out_ref[...] = total.astype(out_ref.dtype)


def pick_gradients_kernel(pieces, *refs):
    back = join(refs[:pieces])
    own_meta, partner_meta, own_out, partner_out = refs[pieces:]
    for meta, out_ref in ((own_meta, own_out), (partner_meta, partner_out)):
        mask = hits(back.shape[0], meta, 0) | hits(back.shape[0], meta, 1)
        out_ref[...] = dot(one_hot(mask), back, 0, 0).astype(out_ref.dtype)


def finish_kernel(
    own_out, got_out, own_back, got_back, own_gates, got_gates, combined, grad_tokens, grad_gates
):
    combined[...] = (own_out[...] + got_out[...].astype(F32)).astype(BF16)
    grad_tokens[...] = (own_back[...] + got_back[...].astype(F32)).astype(BF16)
    grad_gates[...] = own_gates[...] + got_gates[...]


def call(kernel, outs, flops=0, traffic=0, limit=12, **options):
    shapes = [jax.ShapeDtypeStruct(shape, dtype) for shape, dtype in outs]
    return pl.pallas_call(
        kernel,
        out_shape=shapes,
        compiler_params=pltpu.CompilerParams(vmem_limit_bytes=limit * MIB),
        cost_estimate=pl.CostEstimate(flops=flops, bytes_accessed=traffic, transcendentals=0),
        **options,
    )


def body(tokens, expert_ids, keep_mask, gate_weights, weight_in, weight_out, grad_output):
    token_rows, width = tokens.shape
    hidden_width = weight_in.shape[2]
    rest_count = lax.axis_size("rest")
    members = lax.axis_size("row") * rest_count
    experts = 2 * members
    capacity = 2 * expert_ids.shape[1] * token_rows // experts
    slot_total = experts * capacity
    swap = ((0, 1), (1, 0))

    def exchange(values):
        return lax.ppermute(values, "half", swap)

    member = lax.axis_index("row") * rest_count + lax.axis_index("rest")
    swaps = members if 2 * capacity % 16 == 0 else 1

    def shuffle(pieces):
        if swaps > 1:
            moved = [
                lax.ppermute(piece, GROUP, [(m, m ^ d) for m in range(members)])
                for d, piece in enumerate(pieces)
                if d > 0
            ]
            return [pieces[0]] + moved
        order = jnp.arange(members) ^ member
        shaped = pieces[0].reshape(members, 2 * capacity, width)[order]
        moved = lax.all_to_all(shaped, GROUP, split_axis=0, concat_axis=0, tiled=True)
        return [moved[order].reshape(slot_total, width)]

    partner_tokens = exchange(tokens)
    partner_grad = exchange(grad_output)
    position = jnp.stack([lax.axis_index("half"), member]).astype(jnp.int32)
    meta_shape = ((8, token_rows), F32)
    vmem = pl.BlockSpec(memory_space=pltpu.VMEM)
    hbm = pl.BlockSpec(memory_space=pltpu.HBM)
    own_meta, sent_meta = call(
        functools.partial(route_kernel, rest_count.bit_length() - 1, capacity),
        [meta_shape, meta_shape],
        in_specs=[pl.BlockSpec(memory_space=pltpu.SMEM), vmem, vmem, vmem],
        traffic=8 * token_rows * 8,
    )(position, expert_ids.T, keep_mask.T, gate_weights.T)
    partner_meta = exchange(sent_meta)

    piece_shape = ((slot_total // swaps, width), BF16)
    slot_shape = ((slot_total, width), BF16)
    slot_bytes = slot_total * width * 2
    token_bytes = token_rows * width * 2
    place_flops = 2 * slot_total * 2 * token_rows * width
    sent = call(
        place_tokens_kernel, [piece_shape] * swaps, place_flops, 2 * token_bytes + slot_bytes
    )(tokens, partner_tokens, own_meta, partner_meta)
    x_pieces = shuffle(sent)
    sent_cot = call(
        place_cotangents_kernel,
        [piece_shape] * swaps,
        2 * place_flops,
        2 * token_bytes + slot_bytes,
    )(grad_output, partner_grad, own_meta, partner_meta)
    cot_pieces = shuffle(sent_cot)

    chunk = 512
    mid = (slot_total, hidden_width)
    product = 2 * slot_total * width * hidden_width
    weight_bytes = 2 * 2 * width * hidden_width
    mid_count = slot_total * hidden_width
    *out_pieces, x, hidden, slope = call(
        functools.partial(forward_kernel, swaps, chunk),
        [piece_shape] * swaps + [slot_shape, (mid, BF16), (mid, BF16)],
        2 * product,
        2 * slot_bytes + weight_bytes + 4 * mid_count,
        32,
        in_specs=[vmem] * swaps + [hbm] * 2,
        out_specs=[vmem] * (swaps + 1) + [hbm] * 2,
        scratch_shapes=[pltpu.VMEM((slot_total, width), F32)],
    )(*x_pieces, weight_in, weight_out)
    back_out = shuffle(out_pieces)
    *grad_pieces, cot, grad_pre = call(
        functools.partial(backward_kernel, swaps, chunk),
        [piece_shape] * swaps + [slot_shape, (mid, BF16)],
        2 * product,
        2 * slot_bytes + weight_bytes + 4 * mid_count,
        32,
        in_specs=[vmem] * swaps + [hbm] * 3,
        out_specs=[vmem] * (swaps + 1) + [hbm],
        scratch_shapes=[pltpu.VMEM((slot_total, width), F32)],
    )(*cot_pieces, weight_in, weight_out, slope)
    back_grad = shuffle(grad_pieces)
    own_shape, partner_shape = ((token_rows, width), F32), ((token_rows, width), BF16)
    gates_shape = ((2, token_rows), F32)
    own_out, partner_out, own_gates, partner_gates = call(
        functools.partial(pick_outputs_kernel, swaps),
        [own_shape, partner_shape, gates_shape, gates_shape],
        2 * place_flops,
        2 * token_bytes + slot_bytes,
    )(*back_out, grad_output, partner_grad, own_meta, partner_meta)
    grad_pre, partner_out, partner_gates = lax.optimization_barrier(
        (grad_pre, partner_out, partner_gates)
    )
    grad_in_w, grad_out_w = call(
        functools.partial(weights_kernel, chunk),
        [(weight_in.shape, BF16), (weight_out.shape, BF16)],
        2 * product,
        2 * slot_bytes + weight_bytes + 4 * mid_count,
        32,
        in_specs=[vmem] * 2 + [hbm] * 2,
        out_specs=[hbm] * 2,
    )(x, cot, hidden, grad_pre)
    got_out, got_gates = exchange(partner_out), exchange(partner_gates)
    own_back, partner_back = call(
        functools.partial(pick_gradients_kernel, swaps),
        [own_shape, partner_shape],
        place_flops,
        slot_bytes + 3 * token_bytes,
    )(*back_grad, own_meta, partner_meta)
    got_back = exchange(partner_back)
    combined, grad_tokens, grad_gates = call(
        finish_kernel, [partner_shape, partner_shape, gates_shape], 0, 8 * token_bytes
    )(own_out, got_out, own_back, got_back, own_gates, got_gates)
    return (combined, grad_tokens, grad_gates.T, grad_in_w, grad_out_w)


def solution(mesh):
    row_count, col_count = mesh.devices.shape
    split = Mesh(
        mesh.devices.reshape(row_count, 2, col_count // 2), ("row", "half", "rest")
    )
    axes = ("row", "half", "rest")
    flat = P(axes, None)
    deep = P(axes, None, None)
    return jax.shard_map(
        body,
        mesh=split,
        in_specs=(flat, flat, flat, flat, deep, deep, flat),
        out_specs=(flat, flat, flat, deep, deep),
        check_vma=False,
    )
```

```python
import functools

import jax
import jax.numpy as jnp
from jax import lax
from jax.experimental import pallas as pl
from jax.experimental.pallas import tpu as pltpu
from jax.sharding import PartitionSpec as P

BLOCK = 128
BF16 = jnp.bfloat16
F32 = jnp.float32
MIB = 1024 * 1024
SUB = 256


def dot(a, b, contract_a, contract_b):
    return lax.dot_general(
        a, b, (((contract_a,), (contract_b,)), ((), ())), preferred_element_type=F32
    )


def column(row):
    count = row.shape[1]
    return jnp.transpose(jnp.broadcast_to(row, (count, count)))


def route(ids_ref, keep_ref, gates_ref, meta_ref, capacity):
    token_rows = ids_ref.shape[1]
    ids = ids_ref[...].astype(F32)
    earlier = lax.broadcasted_iota(jnp.int32, (token_rows, token_rows), 0) < lax.broadcasted_iota(
        jnp.int32, (token_rows, token_rows), 1
    )
    columns = (column(ids[0:1]), column(ids[1:2]))
    for k in range(2):
        count = jnp.zeros((token_rows, token_rows), F32)
        for other_choice in columns:
            count = count + jnp.where(earlier & (other_choice == ids[k : k + 1]), 1.0, 0.0)
        slot = jnp.sum(count, axis=0, keepdims=True).astype(jnp.int32)
        row = ids_ref[k : k + 1, :] * capacity + slot
        meta_ref[k : k + 1, :] = jnp.where(keep_ref[k : k + 1, :] > 0, row, -1).astype(F32)
        meta_ref[k + 2 : k + 3, :] = gates_ref[k : k + 1, :]
    meta_ref[4:8, :] = jnp.zeros((4, token_rows), F32)


def hits(slot_total, meta_ref, k):
    rows = meta_ref[k : k + 1, :].astype(jnp.int32)
    index = lax.broadcasted_iota(jnp.int32, (slot_total, rows.shape[1]), 0)
    return index == rows


def one_hot(mask):
    return jnp.where(mask, 1.0, 0.0).astype(BF16)


def restore(tokens_ref):
    pieces = []
    for b in range(tokens_ref.shape[1] // BLOCK):
        x = tokens_ref[:, b * BLOCK : (b + 1) * BLOCK].astype(F32)
        scale = (jnp.max(jnp.abs(x), axis=1, keepdims=True) + 1e-06).astype(BF16).astype(F32)
        quantized = (x / scale).astype(BF16)
        pieces.append((quantized.astype(F32) * scale).astype(BF16))
    return jnp.concatenate(pieces, axis=1)


def place_tokens_kernel(capacity, tokens_ref, ids_ref, keep_ref, gates_ref, meta_ref, out_ref):
    route(ids_ref, keep_ref, gates_ref, meta_ref, capacity)
    slot_total = out_ref.shape[0]
    mask = hits(slot_total, meta_ref, 0) | hits(slot_total, meta_ref, 1)
    out_ref[...] = dot(one_hot(mask), restore(tokens_ref), 1, 0).astype(BF16)


def scaled_rows(gate_row, grad_ref):
    gate = column(gate_row)
    pieces = [
        gate * grad_ref[:, b * BLOCK : (b + 1) * BLOCK].astype(F32)
        for b in range(grad_ref.shape[1] // BLOCK)
    ]
    return jnp.concatenate(pieces, axis=1)


def place_cotangents_kernel(grad_ref, meta_ref, out_ref):
    slot_total = out_ref.shape[0]
    parts = [
        dot(
            one_hot(hits(slot_total, meta_ref, k)),
            scaled_rows(meta_ref[k + 2 : k + 3, :], grad_ref).astype(BF16),
            1,
            0,
        )
        for k in range(2)
    ]
    out_ref[...] = (parts[0] + parts[1]).astype(BF16)


def gelu_parts(v):
    c = 0.7978845608028654
    inner = c + (c * 0.044715) * (v * v)
    s = 0.5 + 0.5 * jnp.tanh(v * inner)
    hidden = v * s
    slope = s + (hidden * (1.0 - s)) * (6.0 * inner - 4.0 * c)
    return hidden.astype(BF16), slope.astype(BF16)


def forward_kernel(x_ref, w_in_ref, w_out_ref, hidden_ref, slope_ref, out_ref, total):
    step = pl.program_id(0)

    @pl.when(step == 0)
    def _():
        total[...] = jnp.zeros_like(total)

    parts = hidden_ref.shape[1] // SUB
    v = dot(x_ref[...], w_in_ref[:, :SUB], 1, 0)
    pieces = []
    for j in range(parts):
        if j + 1 < parts:
            after = dot(x_ref[...], w_in_ref[:, (j + 1) * SUB : (j + 2) * SUB], 1, 0)
        hidden, slope = gelu_parts(v)
        hidden_ref[:, j * SUB : (j + 1) * SUB] = hidden
        slope_ref[:, j * SUB : (j + 1) * SUB] = slope
        pieces.append(hidden)
        v = after
    total[...] += dot(jnp.concatenate(pieces, axis=1), w_out_ref[...], 1, 0)

    @pl.when(step == pl.num_programs(0) - 1)
    def _():
        out_ref[...] = total[...].astype(BF16)


def backward_kernel(cot_ref, w_in_ref, w_out_ref, slope_ref, grad_pre_ref, out_ref, total):
    step = pl.program_id(0)

    @pl.when(step == 0)
    def _():
        total[...] = jnp.zeros_like(total)

    parts = grad_pre_ref.shape[1] // SUB
    pieces = []
    for j in range(parts):
        grad_hidden = dot(cot_ref[...], w_out_ref[j * SUB : (j + 1) * SUB, :], 1, 1)
        slope = slope_ref[:, j * SUB : (j + 1) * SUB].astype(F32)
        grad_pre = (grad_hidden * slope).astype(BF16)
        grad_pre_ref[:, j * SUB : (j + 1) * SUB] = grad_pre
        pieces.append(grad_pre)
    total[...] += dot(jnp.concatenate(pieces, axis=1), w_in_ref[...], 1, 1)

    @pl.when(step == pl.num_programs(0) - 1)
    def _():
        out_ref[...] = total[...].astype(BF16)


def weights_kernel(x_ref, cot_ref, hidden_ref, grad_pre_ref, grad_in_ref, grad_out_ref):
    grad_in_ref[...] = dot(x_ref[...], grad_pre_ref[...], 0, 0).astype(BF16)
    grad_out_ref[...] = dot(hidden_ref[...], cot_ref[...], 0, 0).astype(BF16)


def pick_outputs_kernel(back_ref, grad_ref, meta_ref, out_ref, gates_ref):
    slot_total = back_ref.shape[0]
    total = None
    for k in range(2):
        picked = dot(one_hot(hits(slot_total, meta_ref, k)), back_ref[...], 0, 0)
        gate = column(meta_ref[k + 2 : k + 3, :])
        weighted = jnp.concatenate(
            [
                gate * picked[:, b * BLOCK : (b + 1) * BLOCK]
                for b in range(picked.shape[1] // BLOCK)
            ],
            axis=1,
        )
        total = weighted if total is None else total + weighted
        sums = jnp.sum(picked * grad_ref[...].astype(F32), axis=1, keepdims=True)
        rows = jnp.transpose(jnp.broadcast_to(sums, (sums.shape[0], sums.shape[0])))
        gates_ref[k : k + 1, :] = rows[0:1, :]
    out_ref[...] = total.astype(BF16)


def pick_gradients_kernel(back_ref, meta_ref, out_ref):
    slot_total = back_ref.shape[0]
    mask = hits(slot_total, meta_ref, 0) | hits(slot_total, meta_ref, 1)
    out_ref[...] = dot(one_hot(mask), back_ref[...], 0, 0).astype(BF16)


def call(kernel, outs, flops=0, traffic=0, limit=12, **options):
    return pl.pallas_call(
        kernel,
        out_shape=outs,
        compiler_params=pltpu.CompilerParams(vmem_limit_bytes=limit * MIB),
        cost_estimate=pl.CostEstimate(flops=flops, bytes_accessed=traffic, transcendentals=0),
        **options,
    )


def in_hbm(values):
    return pltpu.with_memory_space_constraint(values, pltpu.HBM)


def body(tokens, expert_ids, keep_mask, gate_weights, weight_in, weight_out, grad_output):
    token_rows, width = tokens.shape
    hidden_width = weight_in.shape[2]
    experts = lax.axis_size("row") * lax.axis_size("col")
    capacity = 2 * expert_ids.shape[1] * token_rows // experts
    slot_total = experts * capacity

    def shuffle(rows):
        shaped = rows.reshape(experts, capacity, width)
        return lax.all_to_all(
            shaped, ("row", "col"), split_axis=0, concat_axis=0, tiled=True
        ).reshape(slot_total, width)

    slots = jax.ShapeDtypeStruct((slot_total, width), BF16)
    slot_bytes = slot_total * width * 2
    token_bytes = token_rows * width * 2
    place_flops = 2 * slot_total * token_rows * width
    meta, sent = call(
        functools.partial(place_tokens_kernel, capacity),
        [jax.ShapeDtypeStruct((8, token_rows), F32), slots],
        place_flops,
        token_bytes + slot_bytes,
    )(in_hbm(tokens), in_hbm(expert_ids.T), in_hbm(keep_mask.T), in_hbm(gate_weights.T))
    x = shuffle(sent)
    sent_cot = call(
        place_cotangents_kernel, slots, 2 * place_flops, token_bytes + slot_bytes
    )(in_hbm(grad_output), meta)
    cot = shuffle(sent_cot)

    chunk = 1024
    whole = pl.BlockSpec((slot_total, width), lambda i: (0, 0))
    in_spec = pl.BlockSpec((None, width, chunk), lambda i: (0, 0, i))
    out_spec = pl.BlockSpec((None, chunk, width), lambda i: (0, i, 0))
    mid_spec = pl.BlockSpec((slot_total, chunk), lambda i: (0, i))
    mid = pltpu.HBM((slot_total, hidden_width), BF16)
    product = 2 * slot_total * width * hidden_width
    traffic = 2 * slot_bytes + 4 * width * hidden_width + 4 * slot_total * hidden_width
    grid = (hidden_width // chunk,)
    total = pltpu.VMEM((slot_total, width), F32)
    weight_in, weight_out = in_hbm(weight_in), in_hbm(weight_out)
    hidden, slope, outputs = call(
        forward_kernel,
        [mid, mid, slots],
        2 * product,
        traffic,
        32,
        grid=grid,
        in_specs=[whole, in_spec, out_spec],
        out_specs=[mid_spec, mid_spec, whole],
        scratch_shapes=[total],
    )(x, weight_in, weight_out)
    back_out = shuffle(outputs)
    grad_pre, grad_rows = call(
        backward_kernel,
        [mid, slots],
        2 * product,
        traffic,
        32,
        grid=grid,
        in_specs=[whole, in_spec, out_spec, mid_spec],
        out_specs=[mid_spec, whole],
        scratch_shapes=[total],
    )(cot, weight_in, weight_out, in_hbm(slope))
    back_grad = shuffle(grad_rows)
    combined, grad_gates = call(
        pick_outputs_kernel,
        [
            jax.ShapeDtypeStruct((token_rows, width), BF16),
            jax.ShapeDtypeStruct((2, token_rows), F32),
        ],
        2 * place_flops,
        2 * token_bytes + slot_bytes,
    )(back_out, in_hbm(grad_output), meta)
    grad_in_w, grad_out_w = call(
        weights_kernel,
        [pltpu.HBM(weight_in.shape, BF16), pltpu.HBM(weight_out.shape, BF16)],
        2 * product,
        traffic,
        32,
        grid=grid,
        in_specs=[whole, whole, mid_spec, mid_spec],
        out_specs=[in_spec, out_spec],
    )(x, cot, in_hbm(hidden), in_hbm(grad_pre))
    grad_tokens = call(
        pick_gradients_kernel,
        jax.ShapeDtypeStruct((token_rows, width), BF16),
        place_flops,
        slot_bytes + token_bytes,
    )(back_grad, meta)
    return (combined, grad_tokens, grad_gates.T, grad_in_w, grad_out_w)


def solution(mesh):
    flat = P(("row", "col"), None)
    deep = P(("row", "col"), None, None)
    return jax.shard_map(
        body,
        mesh=mesh,
        in_specs=(flat, flat, flat, flat, deep, deep, flat),
        out_specs=(flat, flat, flat, deep, deep),
        check_vma=False,
    )
```

```python
import functools

import jax
import jax.numpy as jnp
from jax import lax
from jax.experimental import pallas as pl
from jax.experimental.pallas import tpu as pltpu
from jax.sharding import Mesh
from jax.sharding import PartitionSpec as P

BLOCK = 128
BF16 = jnp.bfloat16
F32 = jnp.float32
MIB = 1024 * 1024
SUB = 256
GROUP = ("row", "rest")


def dot(a, b, contract_a, contract_b):
    return lax.dot_general(
        a, b, (((contract_a,), (contract_b,)), ((), ())), preferred_element_type=F32
    )


def column(row):
    count = row.shape[1]
    return jnp.transpose(jnp.broadcast_to(row, (count, count)))


def route(rest_bits, capacity, half, ids_ref, keep_ref, gates_ref, mine_ref, other_ref):
    token_rows = ids_ref.shape[1]
    ids = ids_ref[...].astype(F32)
    earlier = lax.broadcasted_iota(jnp.int32, (token_rows, token_rows), 0) < lax.broadcasted_iota(
        jnp.int32, (token_rows, token_rows), 1
    )
    columns = (column(ids[0:1]), column(ids[1:2]))
    for k in range(2):
        count = jnp.zeros((token_rows, token_rows), F32)
        for other_choice in columns:
            count = count + jnp.where(earlier & (other_choice == ids[k : k + 1]), 1.0, 0.0)
        slot = jnp.sum(count, axis=0, keepdims=True).astype(jnp.int32)
        expert = ids_ref[k : k + 1, :]
        kept = keep_ref[k : k + 1, :] > 0
        side = (expert >> rest_bits) & 1
        local = ((expert >> (rest_bits + 1)) << rest_bits) + (expert & ((1 << rest_bits) - 1))
        for ref, there, offset in (
            (mine_ref, kept & (side == half), 0),
            (other_ref, kept & (side != half), capacity),
        ):
            ref[k : k + 1, :] = jnp.where(there, local * capacity + slot, -1).astype(F32)
            joint = local * (2 * capacity) + offset + slot
            ref[k + 4 : k + 5, :] = jnp.where(there, joint, -1).astype(F32)
            ref[k + 2 : k + 3, :] = gates_ref[k : k + 1, :]
    for ref in (mine_ref, other_ref):
        ref[6:8, :] = jnp.zeros((2, token_rows), F32)


def hits(slot_total, meta_ref, k):
    rows = meta_ref[k : k + 1, :].astype(jnp.int32)
    index = lax.broadcasted_iota(jnp.int32, (slot_total, rows.shape[1]), 0)
    return index == rows


def one_hot(mask):
    return jnp.where(mask, 1.0, 0.0).astype(BF16)


def restore(tokens_ref):
    pieces = []
    for b in range(tokens_ref.shape[1] // BLOCK):
        x = tokens_ref[:, b * BLOCK : (b + 1) * BLOCK].astype(F32)
        scale = (jnp.max(jnp.abs(x), axis=1, keepdims=True) + 1e-06).astype(BF16).astype(F32)
        quantized = (x / scale).astype(BF16)
        pieces.append((quantized.astype(F32) * scale).astype(BF16))
    return jnp.concatenate(pieces, axis=1)


def place_own_kernel(
    rest_bits, capacity, half_ref, tokens_ref, ids_ref, keep_ref, gates_ref, mine_ref, other_ref, out_ref
):
    route(rest_bits, capacity, half_ref[0], ids_ref, keep_ref, gates_ref, mine_ref, other_ref)
    slot_total = out_ref.shape[0]
    mask = hits(slot_total, mine_ref, 0) | hits(slot_total, mine_ref, 1)
    out_ref[...] = dot(one_hot(mask), restore(tokens_ref), 1, 0).astype(BF16)


def place_partner_kernel(tokens_ref, meta_ref, grad_ref, out_ref, grad_copy_ref):
    slot_total = out_ref.shape[0]
    mask = hits(slot_total, meta_ref, 0) | hits(slot_total, meta_ref, 1)
    out_ref[...] = dot(one_hot(mask), restore(tokens_ref), 1, 0).astype(BF16)
    grad_copy_ref[...] = grad_ref[...]


def scaled_rows(gate_row, grad_ref):
    gate = column(gate_row)
    pieces = [
        gate * grad_ref[:, b * BLOCK : (b + 1) * BLOCK].astype(F32)
        for b in range(grad_ref.shape[1] // BLOCK)
    ]
    return jnp.concatenate(pieces, axis=1)


def place_cotangents_kernel(own_grad, partner_grad, own_meta, partner_meta, out_ref):
    slot_total = out_ref.shape[0]
    total = None
    for grad_ref, meta_ref in ((own_grad, own_meta), (partner_grad, partner_meta)):
        for k in range(2):
            rows = scaled_rows(meta_ref[k + 2 : k + 3, :], grad_ref).astype(BF16)
            part = dot(one_hot(hits(slot_total, meta_ref, k + 4)), rows, 1, 0)
            total = part if total is None else total + part
    out_ref[...] = total.astype(BF16)


def gelu_parts(v):
    c = 0.7978845608028654
    inner = c + (c * 0.044715) * (v * v)
    s = 0.5 + 0.5 * jnp.tanh(v * inner)
    hidden = v * s
    slope = s + (hidden * (1.0 - s)) * (6.0 * inner - 4.0 * c)
    return hidden.astype(BF16), slope.astype(BF16)


def interleave(block, own, partner):
    pieces = []
    for at in range(0, own.shape[0], block):
        pieces += [own[at : at + block, :], partner[at : at + block, :]]
    return jnp.concatenate(pieces, axis=0)


def separate(block, values):
    pieces = [values[at : at + block, :] for at in range(0, values.shape[0], block)]
    return jnp.concatenate(pieces[0::2], axis=0), jnp.concatenate(pieces[1::2], axis=0)


def at_chunk(j, size):
    return pl.ds(pl.multiple_of(j * size, size), size)


def run_chunks(count, fetches, sends, work):
    ahead = min(2, count)
    for j in range(ahead):
        for copy in fetches(j):
            copy.start()

    def each(j, carry):
        @pl.when(j + ahead < count)
        def _():
            for copy in fetches(j + ahead):
                copy.start()

        work(j, [copy.wait for copy in fetches(j)])
        for copy in sends(j):
            copy.start()
        return carry

    lax.fori_loop(0, count, each, 0)

    def drain(j, carry):
        for copy in sends(j):
            copy.wait()
        return carry

    lax.fori_loop(0, count, drain, 0)


def forward_kernel(
    block, own, partner, w_in, w_out, out_ref, x, hidden, slope, w_in_buf, w_out_buf, hidden_buf, slope_buf, total, in_sem, out_sem
):
    count, _, chunk = hidden.shape
    parts = chunk // SUB
    x[...] = interleave(block, own, partner)
    total[...] = jnp.zeros_like(total)

    def fetches(j):
        copies = [
            pltpu.make_async_copy(
                w_in.at[0, :, at_chunk(j * parts + p, SUB)],
                w_in_buf.at[j * parts + p],
                in_sem.at[j, p],
            )
            for p in range(parts)
        ]
        rows = w_out.at[0, at_chunk(j, chunk), :]
        return copies + [pltpu.make_async_copy(rows, w_out_buf.at[j], in_sem.at[j, parts])]

    def sends(j):
        return [
            pltpu.make_async_copy(hidden_buf.at[j], hidden.at[j], out_sem.at[j, 0]),
            pltpu.make_async_copy(slope_buf.at[j], slope.at[j], out_sem.at[j, 1]),
        ]

    def work(j, waits):
        waits[0]()
        v = dot(x[...], w_in_buf[j * parts], 1, 0)
        done = []
        for p in range(parts):
            if p + 1 < parts:
                waits[p + 1]()
                after = dot(x[...], w_in_buf[j * parts + p + 1], 1, 0)
            else:
                waits[parts]()
            hidden_part, slope_part = gelu_parts(v)
            hidden_buf[j, :, p * SUB : (p + 1) * SUB] = hidden_part
            slope_buf[j, :, p * SUB : (p + 1) * SUB] = slope_part
            done.append(hidden_part)
            v = after
        total[...] += dot(jnp.concatenate(done, axis=1), w_out_buf[j], 1, 0)

    run_chunks(count, fetches, sends, work)
    out_ref[...] = total[...].astype(BF16)


def backward_kernel(
    block, cot, w_in, w_out, slope, own_out, partner_out, grad_pre, w_in_buf, w_out_buf, slope_buf, grad_buf, total, in_sem, out_sem
):
    count, _, chunk = grad_pre.shape
    parts = chunk // SUB
    total[...] = jnp.zeros_like(total)

    def fetches(j):
        copies = [
            pltpu.make_async_copy(
                w_out.at[0, at_chunk(j * parts + p, SUB), :],
                w_out_buf.at[j * parts + p],
                in_sem.at[j, p],
            )
            for p in range(parts)
        ]
        return copies + [
            pltpu.make_async_copy(slope.at[j], slope_buf.at[j], in_sem.at[j, parts]),
            pltpu.make_async_copy(
                w_in.at[0, :, at_chunk(j, chunk)], w_in_buf.at[j], in_sem.at[j, parts + 1]
            ),
        ]

    def sends(j):
        return [pltpu.make_async_copy(grad_buf.at[j], grad_pre.at[j], out_sem.at[j, 0])]

    def work(j, waits):
        done = []
        for p in range(parts):
            waits[p]()
            grad_hidden = dot(cot[...], w_out_buf[j * parts + p], 1, 1)
            if p == 0:
                waits[parts]()
            slope_part = slope_buf[j, :, p * SUB : (p + 1) * SUB].astype(F32)
            part = (grad_hidden * slope_part).astype(BF16)
            grad_buf[j, :, p * SUB : (p + 1) * SUB] = part
            done.append(part)
        waits[parts + 1]()
        total[...] += dot(jnp.concatenate(done, axis=1), w_in_buf[j], 1, 1)

    run_chunks(count, fetches, sends, work)
    own_out[...], partner_out[...] = separate(block, total[...].astype(BF16))


def weights_kernel(
    x, cot, hidden, grad_pre, grad_in, grad_out, hidden_buf, grad_buf, in_buf, out_buf, in_sem, out_sem
):
    count, _, chunk = hidden.shape

    def fetches(j):
        return [
            pltpu.make_async_copy(hidden.at[j], hidden_buf.at[j], in_sem.at[j, 0]),
            pltpu.make_async_copy(grad_pre.at[j], grad_buf.at[j], in_sem.at[j, 1]),
        ]

    def sends(j):
        return [
            pltpu.make_async_copy(in_buf.at[j], grad_in.at[0, :, at_chunk(j, chunk)], out_sem.at[j, 0]),
            pltpu.make_async_copy(out_buf.at[j], grad_out.at[0, at_chunk(j, chunk), :], out_sem.at[j, 1]),
        ]

    def work(j, waits):
        waits[0]()
        waits[1]()
        in_buf[j] = dot(x[...], grad_buf[j], 0, 0).astype(BF16)
        out_buf[j] = dot(hidden_buf[j], cot[...], 0, 0).astype(BF16)

    run_chunks(count, fetches, sends, work)


def pick_outputs_kernel(
    back_ref, own_grad, partner_grad, own_meta, partner_meta, own_out, partner_out, own_gates, partner_gates
):
    slot_total = back_ref.shape[0]
    for grad_ref, meta_ref, out_ref, gates_ref in (
        (own_grad, own_meta, own_out, own_gates),
        (partner_grad, partner_meta, partner_out, partner_gates),
    ):
        total = None
        for k in range(2):
            picked = dot(one_hot(hits(slot_total, meta_ref, k + 4)), back_ref[...], 0, 0)
            gate = column(meta_ref[k + 2 : k + 3, :])
            weighted = jnp.concatenate(
                [
                    gate * picked[:, b * BLOCK : (b + 1) * BLOCK]
                    for b in range(picked.shape[1] // BLOCK)
                ],
                axis=1,
            )
            total = weighted if total is None else total + weighted
            sums = jnp.sum(picked * grad_ref[...].astype(F32), axis=1, keepdims=True)
            rows = jnp.transpose(jnp.broadcast_to(sums, (sums.shape[0], sums.shape[0])))
            gates_ref[k : k + 1, :] = rows[0:1, :]
        out_ref[...] = total.astype(out_ref.dtype)


def pick_partner_kernel(back_ref, meta_ref, out_ref):
    slot_total = back_ref.shape[0]
    mask = hits(slot_total, meta_ref, 0) | hits(slot_total, meta_ref, 1)
    out_ref[...] = dot(one_hot(mask), back_ref[...], 0, 0).astype(BF16)


def finish_kernel(
    back_ref, meta_ref, got_back, own_out, got_out, own_gates, got_gates, combined, grad_tokens, grad_gates
):
    slot_total = back_ref.shape[0]
    mask = hits(slot_total, meta_ref, 0) | hits(slot_total, meta_ref, 1)
    own = dot(one_hot(mask), back_ref[...], 0, 0)
    grad_tokens[...] = (own + got_back[...].astype(F32)).astype(BF16)
    combined[...] = (own_out[...] + got_out[...].astype(F32)).astype(BF16)
    grad_gates[...] = own_gates[...] + got_gates[...]


def call(kernel, outs, flops=0, traffic=0, limit=12, **options):
    return pl.pallas_call(
        kernel,
        out_shape=outs,
        compiler_params=pltpu.CompilerParams(vmem_limit_bytes=limit * MIB),
        cost_estimate=pl.CostEstimate(flops=flops, bytes_accessed=traffic, transcendentals=0),
        **options,
    )


def in_hbm(values):
    return pltpu.with_memory_space_constraint(values, pltpu.HBM)


def body(tokens, expert_ids, keep_mask, gate_weights, weight_in, weight_out, grad_output):
    token_rows, width = tokens.shape
    hidden_width = weight_in.shape[2]
    rest_count = lax.axis_size("rest")
    members = lax.axis_size("row") * rest_count
    capacity = expert_ids.shape[1] * token_rows // members
    slot_total = 2 * members * capacity
    set_total = members * capacity
    aligned = capacity % 16 == 0
    block = capacity if aligned else set_total

    def exchange(values):
        return lax.ppermute(values, "half", ((0, 1), (1, 0)))

    def shuffle(rows):
        shaped = rows.reshape(members, rows.shape[0] // members, width)
        return lax.all_to_all(shaped, GROUP, split_axis=0, concat_axis=0, tiled=True).reshape(
            rows.shape
        )

    def shape(*dims, dtype=BF16):
        return jax.ShapeDtypeStruct(dims, dtype)

    vmem = pl.BlockSpec(memory_space=pltpu.VMEM)
    hbm = pl.BlockSpec(memory_space=pl.ANY)
    meta_shape = shape(8, token_rows, dtype=F32)
    set_bytes, token_bytes = set_total * width * 2, token_rows * width * 2
    place_flops = 2 * set_total * token_rows * width
    far = 200 * 10**9

    partner_tokens = exchange(tokens)
    half = lax.axis_index("half").astype(jnp.int32).reshape(1)
    own_meta, sent_meta, sent_own = call(
        functools.partial(place_own_kernel, rest_count.bit_length() - 1, capacity),
        [meta_shape, meta_shape, shape(set_total, width)],
        place_flops,
        token_bytes + set_bytes,
        in_specs=[pl.BlockSpec(memory_space=pltpu.SMEM)] + [vmem] * 4,
    )(
        half,
        in_hbm(tokens),
        in_hbm(expert_ids.T),
        in_hbm(keep_mask.T),
        in_hbm(gate_weights.T),
    )
    x_own = shuffle(sent_own)
    partner_meta = exchange(sent_meta)
    sent_partner, grad_copy = call(
        place_partner_kernel,
        [shape(set_total, width), shape(token_rows, width)],
        place_flops,
        token_bytes + set_bytes,
    )(partner_tokens, partner_meta, in_hbm(grad_output))
    partner_grad = exchange(grad_copy)
    x_partner = shuffle(sent_partner)
    sent_cot = call(
        place_cotangents_kernel, shape(slot_total, width), far, 2 * (token_bytes + set_bytes)
    )(in_hbm(grad_output), partner_grad, own_meta, partner_meta)
    cot = shuffle(sent_cot)

    if not aligned:
        rows = jnp.stack([x_own, x_partner]).reshape(2, members, capacity, width)
        rows = rows.transpose(1, 0, 2, 3).reshape(slot_total, width)
        x_own, x_partner = rows[:set_total], rows[set_total:]
    chunk = 1024
    count, parts = hidden_width // chunk, chunk // SUB
    mid = pltpu.HBM((count, slot_total, chunk), BF16)
    mid_buf = pltpu.VMEM((count, slot_total, chunk), BF16)
    total = pltpu.VMEM((slot_total, width), F32)
    product = 2 * slot_total * width * hidden_width
    traffic = 4 * set_bytes + 4 * width * hidden_width + 4 * slot_total * hidden_width
    weight_in, weight_out = in_hbm(weight_in), in_hbm(weight_out)
    outputs, x, hidden, slope = call(
        functools.partial(forward_kernel, block),
        [shape(slot_total, width), shape(slot_total, width), mid, mid],
        2 * product,
        traffic,
        40,
        in_specs=[vmem, vmem, hbm, hbm],
        out_specs=[vmem, vmem, hbm, hbm],
        scratch_shapes=[
            pltpu.VMEM((count * parts, width, SUB), BF16),
            pltpu.VMEM((count, chunk, width), BF16),
            mid_buf,
            mid_buf,
            total,
            pltpu.SemaphoreType.DMA((count, parts + 1)),
            pltpu.SemaphoreType.DMA((count, 2)),
        ],
    )(x_own, x_partner, weight_in, weight_out)
    back_out = shuffle(outputs)
    rows_own, rows_partner, grad_pre = call(
        functools.partial(backward_kernel, block),
        [shape(set_total, width), shape(set_total, width), mid],
        2 * product,
        traffic,
        40,
        in_specs=[vmem, hbm, hbm, hbm],
        out_specs=[vmem, vmem, hbm],
        scratch_shapes=[
            pltpu.VMEM((count, width, chunk), BF16),
            pltpu.VMEM((count * parts, SUB, width), BF16),
            mid_buf,
            mid_buf,
            total,
            pltpu.SemaphoreType.DMA((count, parts + 2)),
            pltpu.SemaphoreType.DMA((count, 1)),
        ],
    )(cot, weight_in, weight_out, in_hbm(slope))
    if not aligned:
        rows = jnp.concatenate([rows_own, rows_partner]).reshape(members, 2, capacity, width)
        rows_own = rows[:, 0].reshape(set_total, width)
        rows_partner = rows[:, 1].reshape(set_total, width)
    back_partner = shuffle(rows_partner)
    tokens_f32, gates_shape = shape(token_rows, width, dtype=F32), shape(2, token_rows, dtype=F32)
    own_out, partner_out, own_gates, partner_gates = call(
        pick_outputs_kernel,
        [tokens_f32, shape(token_rows, width), gates_shape, gates_shape],
        8 * place_flops,
        2 * (token_bytes + set_bytes),
    )(back_out, in_hbm(grad_output), partner_grad, own_meta, partner_meta)
    got_out, got_gates = exchange(partner_out), exchange(partner_gates)
    partner_back = call(
        pick_partner_kernel, shape(token_rows, width), place_flops, set_bytes + token_bytes
    )(back_partner, partner_meta)
    back_own = shuffle(rows_own)
    grad_pre, partner_back = lax.optimization_barrier((grad_pre, partner_back))
    got_back = exchange(partner_back)
    grad_in_w, grad_out_w = call(
        weights_kernel,
        [pltpu.HBM(weight_in.shape, BF16), pltpu.HBM(weight_out.shape, BF16)],
        2 * product,
        traffic,
        40,
        in_specs=[vmem, vmem, hbm, hbm],
        out_specs=[hbm, hbm],
        scratch_shapes=[
            mid_buf,
            mid_buf,
            pltpu.VMEM((count, width, chunk), BF16),
            pltpu.VMEM((count, chunk, width), BF16),
            pltpu.SemaphoreType.DMA((count, 2)),
            pltpu.SemaphoreType.DMA((count, 2)),
        ],
    )(x, cot, in_hbm(hidden), in_hbm(grad_pre))
    combined, grad_tokens, grad_gates = call(
        finish_kernel,
        [shape(token_rows, width), shape(token_rows, width), gates_shape],
        place_flops,
        set_bytes + 4 * token_bytes,
    )(back_own, own_meta, got_back, own_out, got_out, own_gates, got_gates)
    return (combined, grad_tokens, grad_gates.T, grad_in_w, grad_out_w)


def solution(mesh):
    rows, cols = mesh.devices.shape
    axes = ("row", "half", "rest")
    halves = Mesh(mesh.devices.reshape(rows, 2, cols // 2), axes)
    flat, deep = P(axes, None), P(axes, None, None)
    return jax.shard_map(
        body,
        mesh=halves,
        in_specs=(flat, flat, flat, flat, deep, deep, flat),
        out_specs=(flat, flat, flat, deep, deep),
        check_vma=False,
    )
```

```python
import functools

import jax
import jax.numpy as jnp
from jax import lax
from jax.experimental import pallas as pl
from jax.experimental.pallas import tpu as pltpu
from jax.sharding import Mesh
from jax.sharding import PartitionSpec as P

BLOCK = 128
BF16 = jnp.bfloat16
F32 = jnp.float32
MIB = 1024 * 1024
SUB = 256
AXES = ("row", "outer", "inner")
GROUP = ("row", "inner", "outer")


def dot(a, b, contract_a, contract_b):
    return lax.dot_general(
        a, b, (((contract_a,), (contract_b,)), ((), ())), preferred_element_type=F32
    )


def column(row):
    count = row.shape[1]
    return jnp.transpose(jnp.broadcast_to(row, (count, count)))


def route(ids_ref, keep_ref, gates_ref, meta_ref, capacity, place_of):
    token_rows = ids_ref.shape[1]
    ids = ids_ref[...].astype(F32)
    earlier = lax.broadcasted_iota(jnp.int32, (token_rows, token_rows), 0) < lax.broadcasted_iota(
        jnp.int32, (token_rows, token_rows), 1
    )
    columns = (column(ids[0:1]), column(ids[1:2]))
    for k in range(2):
        count = jnp.zeros((token_rows, token_rows), F32)
        for other_choice in columns:
            count = count + jnp.where(earlier & (other_choice == ids[k : k + 1]), 1.0, 0.0)
        slot = jnp.sum(count, axis=0, keepdims=True).astype(jnp.int32)
        row = place_of(ids_ref[k : k + 1, :]) * capacity + slot
        meta_ref[k : k + 1, :] = jnp.where(keep_ref[k : k + 1, :] > 0, row, -1).astype(F32)
        meta_ref[k + 2 : k + 3, :] = gates_ref[k : k + 1, :]
    meta_ref[4:8, :] = jnp.zeros((4, token_rows), F32)


def hits(slot_total, meta_ref, k):
    rows = meta_ref[k : k + 1, :].astype(jnp.int32)
    index = lax.broadcasted_iota(jnp.int32, (slot_total, rows.shape[1]), 0)
    return index == rows


def one_hot(mask):
    return jnp.where(mask, 1.0, 0.0).astype(BF16)


def restore(tokens_ref):
    pieces = []
    for b in range(tokens_ref.shape[1] // BLOCK):
        x = tokens_ref[:, b * BLOCK : (b + 1) * BLOCK].astype(F32)
        scale = (jnp.max(jnp.abs(x), axis=1, keepdims=True) + 1e-06).astype(BF16).astype(F32)
        quantized = (x / scale).astype(BF16)
        pieces.append((quantized.astype(F32) * scale).astype(BF16))
    return jnp.concatenate(pieces, axis=1)


def place_tokens_kernel(capacity, place_of, tokens_ref, ids_ref, keep_ref, gates_ref, meta_ref, out_ref):
    route(ids_ref, keep_ref, gates_ref, meta_ref, capacity, place_of)
    slot_total = out_ref.shape[0]
    mask = hits(slot_total, meta_ref, 0) | hits(slot_total, meta_ref, 1)
    out_ref[...] = dot(one_hot(mask), restore(tokens_ref), 1, 0).astype(BF16)


def scaled_rows(gate_row, grad_ref):
    gate = column(gate_row)
    pieces = [
        gate * grad_ref[:, b * BLOCK : (b + 1) * BLOCK].astype(F32)
        for b in range(grad_ref.shape[1] // BLOCK)
    ]
    return jnp.concatenate(pieces, axis=1)


def place_cotangents_kernel(grad_ref, meta_ref, out_ref):
    slot_total = out_ref.shape[0]
    parts = [
        dot(
            one_hot(hits(slot_total, meta_ref, k)),
            scaled_rows(meta_ref[k + 2 : k + 3, :], grad_ref).astype(BF16),
            1,
            0,
        )
        for k in range(2)
    ]
    out_ref[...] = (parts[0] + parts[1]).astype(BF16)


def gelu_parts(v):
    c = 0.7978845608028654
    inner = c + (c * 0.044715) * (v * v)
    s = 0.5 + 0.5 * jnp.tanh(v * inner)
    hidden = v * s
    slope = s + (hidden * (1.0 - s)) * (6.0 * inner - 4.0 * c)
    return hidden.astype(BF16), slope.astype(BF16)


def forward_kernel(x_ref, w_in_ref, w_out_ref, hidden_ref, slope_ref, out_ref, total):
    step = pl.program_id(0)

    @pl.when(step == 0)
    def _():
        total[...] = jnp.zeros_like(total)

    parts = hidden_ref.shape[1] // SUB
    v = dot(x_ref[...], w_in_ref[:, :SUB], 1, 0)
    pieces = []
    for j in range(parts):
        if j + 1 < parts:
            after = dot(x_ref[...], w_in_ref[:, (j + 1) * SUB : (j + 2) * SUB], 1, 0)
        hidden, slope = gelu_parts(v)
        hidden_ref[:, j * SUB : (j + 1) * SUB] = hidden
        slope_ref[:, j * SUB : (j + 1) * SUB] = slope
        pieces.append(hidden)
        v = after
    total[...] += dot(jnp.concatenate(pieces, axis=1), w_out_ref[...], 1, 0)

    @pl.when(step == pl.num_programs(0) - 1)
    def _():
        out_ref[...] = total[...].astype(BF16)


def backward_kernel(cot_ref, w_in_ref, w_out_ref, slope_ref, grad_pre_ref, out_ref, total):
    step = pl.program_id(0)

    @pl.when(step == 0)
    def _():
        total[...] = jnp.zeros_like(total)

    parts = grad_pre_ref.shape[1] // SUB
    pieces = []
    for j in range(parts):
        grad_hidden = dot(cot_ref[...], w_out_ref[j * SUB : (j + 1) * SUB, :], 1, 1)
        slope = slope_ref[:, j * SUB : (j + 1) * SUB].astype(F32)
        grad_pre = (grad_hidden * slope).astype(BF16)
        grad_pre_ref[:, j * SUB : (j + 1) * SUB] = grad_pre
        pieces.append(grad_pre)
    total[...] += dot(jnp.concatenate(pieces, axis=1), w_in_ref[...], 1, 1)

    @pl.when(step == pl.num_programs(0) - 1)
    def _():
        out_ref[...] = total[...].astype(BF16)


def weights_kernel(x_ref, cot_ref, hidden_ref, grad_pre_ref, grad_in_ref, grad_out_ref):
    grad_in_ref[...] = dot(x_ref[...], grad_pre_ref[...], 0, 0).astype(BF16)
    grad_out_ref[...] = dot(hidden_ref[...], cot_ref[...], 0, 0).astype(BF16)


def pick_outputs_kernel(back_ref, grad_ref, meta_ref, out_ref, gates_ref):
    slot_total = back_ref.shape[0]
    total = None
    for k in range(2):
        picked = dot(one_hot(hits(slot_total, meta_ref, k)), back_ref[...], 0, 0)
        gate = column(meta_ref[k + 2 : k + 3, :])
        weighted = jnp.concatenate(
            [
                gate * picked[:, b * BLOCK : (b + 1) * BLOCK]
                for b in range(picked.shape[1] // BLOCK)
            ],
            axis=1,
        )
        total = weighted if total is None else total + weighted
        sums = jnp.sum(picked * grad_ref[...].astype(F32), axis=1, keepdims=True)
        rows = jnp.transpose(jnp.broadcast_to(sums, (sums.shape[0], sums.shape[0])))
        gates_ref[k : k + 1, :] = rows[0:1, :]
    out_ref[...] = total.astype(BF16)


def pick_gradients_kernel(back_ref, meta_ref, out_ref):
    slot_total = back_ref.shape[0]
    mask = hits(slot_total, meta_ref, 0) | hits(slot_total, meta_ref, 1)
    out_ref[...] = dot(one_hot(mask), back_ref[...], 0, 0).astype(BF16)


def call(kernel, outs, flops=0, traffic=0, limit=12, **options):
    return pl.pallas_call(
        kernel,
        out_shape=outs,
        compiler_params=pltpu.CompilerParams(vmem_limit_bytes=limit * MIB),
        cost_estimate=pl.CostEstimate(flops=flops, bytes_accessed=traffic, transcendentals=0),
        **options,
    )


def in_hbm(values):
    return pltpu.with_memory_space_constraint(values, pltpu.HBM)


def body(tokens, expert_ids, keep_mask, gate_weights, weight_in, weight_out, grad_output):
    token_rows, width = tokens.shape
    hidden_width = weight_in.shape[2]
    row_count, outer = lax.axis_size("row"), lax.axis_size("outer")
    experts = row_count * outer * lax.axis_size("inner")
    bits = outer.bit_length() - 1

    def place_of(expert):
        inner_at = expert & 1
        outer_at = (expert >> 1) & (outer - 1)
        row_at = expert >> (bits + 1)
        return ((row_at * 2 + inner_at) << bits) + outer_at

    capacity = 2 * expert_ids.shape[1] * token_rows // experts
    slot_total = experts * capacity

    def shuffle(rows):
        shaped = rows.reshape(experts, capacity, width)
        return lax.all_to_all(
            shaped, GROUP, split_axis=0, concat_axis=0, tiled=True
        ).reshape(slot_total, width)

    slots = jax.ShapeDtypeStruct((slot_total, width), BF16)
    slot_bytes = slot_total * width * 2
    token_bytes = token_rows * width * 2
    place_flops = 2 * slot_total * token_rows * width
    meta, sent = call(
        functools.partial(place_tokens_kernel, capacity, place_of),
        [jax.ShapeDtypeStruct((8, token_rows), F32), slots],
        place_flops,
        token_bytes + slot_bytes,
    )(in_hbm(tokens), in_hbm(expert_ids.T), in_hbm(keep_mask.T), in_hbm(gate_weights.T))
    x = shuffle(sent)
    sent_cot = call(
        place_cotangents_kernel, slots, 2 * place_flops, token_bytes + slot_bytes
    )(in_hbm(grad_output), meta)
    cot = shuffle(sent_cot)

    chunk = 1024
    whole = pl.BlockSpec((slot_total, width), lambda i: (0, 0))
    in_spec = pl.BlockSpec((None, width, chunk), lambda i: (0, 0, i))
    out_spec = pl.BlockSpec((None, chunk, width), lambda i: (0, i, 0))
    mid_spec = pl.BlockSpec((slot_total, chunk), lambda i: (0, i))
    mid = pltpu.HBM((slot_total, hidden_width), BF16)
    product = 2 * slot_total * width * hidden_width
    traffic = 2 * slot_bytes + 4 * width * hidden_width + 4 * slot_total * hidden_width
    grid = (hidden_width // chunk,)
    total = pltpu.VMEM((slot_total, width), F32)
    weight_in, weight_out = in_hbm(weight_in), in_hbm(weight_out)
    hidden, slope, outputs = call(
        forward_kernel,
        [mid, mid, slots],
        2 * product,
        traffic,
        32,
        grid=grid,
        in_specs=[whole, in_spec, out_spec],
        out_specs=[mid_spec, mid_spec, whole],
        scratch_shapes=[total],
    )(x, weight_in, weight_out)
    back_out = shuffle(outputs)
    grad_pre, grad_rows = call(
        backward_kernel,
        [mid, slots],
        2 * product,
        traffic,
        32,
        grid=grid,
        in_specs=[whole, in_spec, out_spec, mid_spec],
        out_specs=[mid_spec, whole],
        scratch_shapes=[total],
    )(cot, weight_in, weight_out, in_hbm(slope))
    back_grad = shuffle(grad_rows)
    combined, grad_gates = call(
        pick_outputs_kernel,
        [
            jax.ShapeDtypeStruct((token_rows, width), BF16),
            jax.ShapeDtypeStruct((2, token_rows), F32),
        ],
        2 * place_flops,
        2 * token_bytes + slot_bytes,
    )(back_out, in_hbm(grad_output), meta)
    grad_in_w, grad_out_w = call(
        weights_kernel,
        [pltpu.HBM(weight_in.shape, BF16), pltpu.HBM(weight_out.shape, BF16)],
        2 * product,
        traffic,
        32,
        grid=grid,
        in_specs=[whole, whole, mid_spec, mid_spec],
        out_specs=[in_spec, out_spec],
    )(x, cot, in_hbm(hidden), in_hbm(grad_pre))
    grad_tokens = call(
        pick_gradients_kernel,
        jax.ShapeDtypeStruct((token_rows, width), BF16),
        place_flops,
        slot_bytes + token_bytes,
    )(back_grad, meta)
    return (combined, grad_tokens, grad_gates.T, grad_in_w, grad_out_w)


def solution(mesh):
    rows, cols = mesh.devices.shape
    split = Mesh(mesh.devices.reshape(rows, cols // 2, 2), AXES)
    flat, deep = P(AXES, None), P(AXES, None, None)
    return jax.shard_map(
        body,
        mesh=split,
        in_specs=(flat, flat, flat, flat, deep, deep, flat),
        out_specs=(flat, flat, flat, deep, deep),
        check_vma=False,
    )
```

```python
import functools

import jax
import jax.numpy as jnp
from jax import lax
from jax.experimental import pallas as pl
from jax.experimental.pallas import tpu as pltpu
from jax.sharding import Mesh
from jax.sharding import PartitionSpec as P

BLOCK = 128
BF16 = jnp.bfloat16
F32 = jnp.float32
MIB = 1024 * 1024
SUB = 256
CHUNK = 1024
WIDE = 512
GROUP = ("row", "rest")


def dot(a, b, contract_a, contract_b):
    return lax.dot_general(
        a, b, (((contract_a,), (contract_b,)), ((), ())), preferred_element_type=F32
    )


def column(row):
    count = row.shape[1]
    return jnp.transpose(jnp.broadcast_to(row, (count, count)))


def route_kernel(rest_bits, capacity, half_ref, ids_ref, keep_ref, gates_ref, mine_ref, other_ref):
    token_rows = ids_ref.shape[1]
    ids = ids_ref[...].astype(F32)
    earlier = lax.broadcasted_iota(jnp.int32, (token_rows, token_rows), 0) < lax.broadcasted_iota(
        jnp.int32, (token_rows, token_rows), 1
    )
    columns = (column(ids[0:1]), column(ids[1:2]))
    for k in range(2):
        count = jnp.zeros((token_rows, token_rows), F32)
        for other_choice in columns:
            count = count + jnp.where(earlier & (other_choice == ids[k : k + 1]), 1.0, 0.0)
        slot = jnp.sum(count, axis=0, keepdims=True).astype(jnp.int32)
        expert = ids_ref[k : k + 1, :]
        kept = keep_ref[k : k + 1, :] > 0
        side = (expert >> rest_bits) & 1
        local = ((expert >> (rest_bits + 1)) << rest_bits) + (expert & ((1 << rest_bits) - 1))
        base = local * (2 * capacity) + slot
        for ref, there, offset in (
            (mine_ref, kept & (side == half_ref[0]), 0),
            (other_ref, kept & (side != half_ref[0]), capacity),
        ):
            ref[k : k + 1, :] = jnp.where(there, base + offset, -1).astype(F32)
            ref[k + 2 : k + 3, :] = gates_ref[k : k + 1, :]
    for ref in (mine_ref, other_ref):
        ref[4:8, :] = jnp.zeros((4, token_rows), F32)


def hits(slot_total, meta_ref, k):
    rows = meta_ref[k : k + 1, :].astype(jnp.int32)
    index = lax.broadcasted_iota(jnp.int32, (slot_total, rows.shape[1]), 0)
    return index == rows


def one_hot(mask):
    return jnp.where(mask, 1.0, 0.0).astype(BF16)


def restore(tokens_ref):
    pieces = []
    for b in range(tokens_ref.shape[1] // BLOCK):
        x = tokens_ref[:, b * BLOCK : (b + 1) * BLOCK].astype(F32)
        scale = (jnp.max(jnp.abs(x), axis=1, keepdims=True) + 1e-06).astype(BF16).astype(F32)
        quantized = (x / scale).astype(BF16)
        pieces.append((quantized.astype(F32) * scale).astype(BF16))
    return jnp.concatenate(pieces, axis=1)


def place_tokens_kernel(own_ref, partner_ref, own_meta, partner_meta, grad_ref, out_ref, grad_copy):
    slot_total = out_ref.shape[0]
    total = None
    for tokens_ref, meta_ref in ((own_ref, own_meta), (partner_ref, partner_meta)):
        mask = hits(slot_total, meta_ref, 0) | hits(slot_total, meta_ref, 1)
        part = dot(one_hot(mask), restore(tokens_ref), 1, 0)
        total = part if total is None else total + part
    out_ref[...] = total.astype(BF16)
    grad_copy[...] = grad_ref[...]


def scaled_rows(gate_row, grad_ref):
    gate = column(gate_row)
    pieces = [
        gate * grad_ref[:, b * BLOCK : (b + 1) * BLOCK].astype(F32)
        for b in range(grad_ref.shape[1] // BLOCK)
    ]
    return jnp.concatenate(pieces, axis=1)


def place_cotangents_kernel(own_grad, partner_grad, own_meta, partner_meta, out_ref):
    slot_total = out_ref.shape[0]
    total = None
    for grad_ref, meta_ref in ((own_grad, own_meta), (partner_grad, partner_meta)):
        for k in range(2):
            rows = scaled_rows(meta_ref[k + 2 : k + 3, :], grad_ref).astype(BF16)
            part = dot(one_hot(hits(slot_total, meta_ref, k)), rows, 1, 0)
            total = part if total is None else total + part
    out_ref[...] = total.astype(BF16)


def gelu_parts(v):
    c = 0.7978845608028654
    inner = c + (c * 0.044715) * (v * v)
    s = 0.5 + 0.5 * jnp.tanh(v * inner)
    hidden = v * s
    slope = s + (hidden * (1.0 - s)) * (6.0 * inner - 4.0 * c)
    return hidden.astype(BF16), slope.astype(BF16)


def load_kernel(w_in, w_out, w_in_buf, w_out_buf, sems):
    copies = [
        pltpu.make_async_copy(w_in.at[0], w_in_buf, sems.at[0]),
        pltpu.make_async_copy(w_out.at[0], w_out_buf, sems.at[1]),
    ]
    for copy in copies:
        copy.start()
    for copy in copies:
        copy.wait()


def chunk_loop(ref, work):
    def each(j, carry):
        work(pl.multiple_of(j * CHUNK, CHUNK))
        return carry

    lax.fori_loop(0, ref.shape[1] // CHUNK, each, 0)


def part_at(start, p):
    return pl.ds(pl.multiple_of(start + p * SUB, SUB), SUB)


def forward_kernel(x, w_in, w_out, hidden, slope, out_ref, total):
    total[...] = jnp.zeros_like(total)
    parts = CHUNK // SUB

    def work(start):
        v = dot(x[...], w_in[:, part_at(start, 0)], 1, 0)
        done = []
        for p in range(parts):
            if p + 1 < parts:
                after = dot(x[...], w_in[:, part_at(start, p + 1)], 1, 0)
            hidden_part, slope_part = gelu_parts(v)
            hidden[:, part_at(start, p)] = hidden_part
            slope[:, part_at(start, p)] = slope_part
            done.append(hidden_part)
            v = after
        total[...] += dot(jnp.concatenate(done, axis=1), w_out[pl.ds(start, CHUNK), :], 1, 0)

    chunk_loop(w_in, work)
    out_ref[...] = total[...].astype(BF16)


def backward_kernel(cot, w_in, w_out, slope, grad_pre, out_ref, total):
    total[...] = jnp.zeros_like(total)

    def work(start):
        done = []
        for p in range(CHUNK // SUB):
            grad_hidden = dot(cot[...], w_out[part_at(start, p), :], 1, 1)
            part = (grad_hidden * slope[:, part_at(start, p)].astype(F32)).astype(BF16)
            grad_pre[:, part_at(start, p)] = part
            done.append(part)
        total[...] += dot(jnp.concatenate(done, axis=1), w_in[:, pl.ds(start, CHUNK)], 1, 1)

    chunk_loop(w_in, work)
    out_ref[...] = total[...].astype(BF16)


def weights_kernel(x_ref, cot_ref, hidden_ref, grad_pre_ref, grad_in_ref, grad_out_ref):
    columns = pl.ds(pl.multiple_of(pl.program_id(0) * WIDE, WIDE), WIDE)
    grad_in_ref[...] = dot(x_ref[...], grad_pre_ref[:, columns], 0, 0).astype(BF16)
    grad_out_ref[...] = dot(hidden_ref[:, columns], cot_ref[...], 0, 0).astype(BF16)


def pick_outputs_kernel(
    back_ref, own_grad, partner_grad, own_meta, partner_meta, own_out, partner_out, own_gates, partner_gates
):
    slot_total = back_ref.shape[0]
    for grad_ref, meta_ref, out_ref, gates_ref in (
        (own_grad, own_meta, own_out, own_gates),
        (partner_grad, partner_meta, partner_out, partner_gates),
    ):
        total = None
        for k in range(2):
            picked = dot(one_hot(hits(slot_total, meta_ref, k)), back_ref[...], 0, 0)
            gate = column(meta_ref[k + 2 : k + 3, :])
            weighted = jnp.concatenate(
                [
                    gate * picked[:, b * BLOCK : (b + 1) * BLOCK]
                    for b in range(picked.shape[1] // BLOCK)
                ],
                axis=1,
            )
            total = weighted if total is None else total + weighted
            sums = jnp.sum(picked * grad_ref[...].astype(F32), axis=1, keepdims=True)
            rows = jnp.transpose(jnp.broadcast_to(sums, (sums.shape[0], sums.shape[0])))
            gates_ref[k : k + 1, :] = rows[0:1, :]
        out_ref[...] = total.astype(out_ref.dtype)


def pick_partner_kernel(back_ref, meta_ref, out_ref):
    slot_total = back_ref.shape[0]
    mask = hits(slot_total, meta_ref, 0) | hits(slot_total, meta_ref, 1)
    out_ref[...] = dot(one_hot(mask), back_ref[...], 0, 0).astype(BF16)


def finish_kernel(
    back_ref, meta_ref, got_back, own_out, got_out, own_gates, got_gates, combined, grad_tokens, grad_gates
):
    slot_total = back_ref.shape[0]
    mask = hits(slot_total, meta_ref, 0) | hits(slot_total, meta_ref, 1)
    own = dot(one_hot(mask), back_ref[...], 0, 0)
    grad_tokens[...] = (own + got_back[...].astype(F32)).astype(BF16)
    combined[...] = (own_out[...] + got_out[...].astype(F32)).astype(BF16)
    grad_gates[...] = own_gates[...] + got_gates[...]


def call(kernel, outs, flops=0, traffic=0, limit=12, **options):
    return pl.pallas_call(
        kernel,
        out_shape=outs,
        compiler_params=pltpu.CompilerParams(vmem_limit_bytes=limit * MIB),
        cost_estimate=pl.CostEstimate(flops=flops, bytes_accessed=traffic, transcendentals=0),
        **options,
    )


def in_hbm(values):
    return pltpu.with_memory_space_constraint(values, pltpu.HBM)


def in_vmem(values):
    return pltpu.with_memory_space_constraint(values, pltpu.VMEM)


def body(tokens, expert_ids, keep_mask, gate_weights, weight_in, weight_out, grad_output):
    token_rows, width = tokens.shape
    hidden_width = weight_in.shape[2]
    rest_count = lax.axis_size("rest")
    members = lax.axis_size("row") * rest_count
    capacity = expert_ids.shape[1] * token_rows // members
    slot_total = 2 * members * capacity

    def exchange(values):
        return lax.ppermute(values, "half", ((0, 1), (1, 0)))

    def shuffle(rows):
        shaped = rows.reshape(members, 2 * capacity, width)
        return lax.all_to_all(shaped, GROUP, split_axis=0, concat_axis=0, tiled=True).reshape(
            rows.shape
        )

    def shape(*dims, dtype=BF16):
        return jax.ShapeDtypeStruct(dims, dtype)

    vmem = pl.BlockSpec(memory_space=pltpu.VMEM)
    hbm = pl.BlockSpec(memory_space=pl.ANY)
    meta_shape = shape(8, token_rows, dtype=F32)
    slots, token_shape = shape(slot_total, width), shape(token_rows, width)
    slot_bytes, token_bytes = slot_total * width * 2, token_rows * width * 2
    place_flops = 4 * slot_total * token_rows * width
    far = 200 * 10**9

    partner_tokens = exchange(tokens)
    half = lax.axis_index("half").astype(jnp.int32).reshape(1)
    own_meta, sent_meta = call(
        functools.partial(route_kernel, rest_count.bit_length() - 1, capacity),
        [meta_shape, meta_shape],
        traffic=64 * token_rows,
        in_specs=[pl.BlockSpec(memory_space=pltpu.SMEM)] + [vmem] * 3,
    )(half, in_hbm(expert_ids.T), in_hbm(keep_mask.T), in_hbm(gate_weights.T))
    partner_meta = exchange(sent_meta)
    sent, grad_copy = call(
        place_tokens_kernel, [slots, token_shape], place_flops, 4 * token_bytes + slot_bytes
    )(in_hbm(tokens), partner_tokens, own_meta, partner_meta, in_hbm(grad_output))
    partner_grad = exchange(grad_copy)
    x = shuffle(sent)
    sent_cot = call(place_cotangents_kernel, slots, far, 2 * token_bytes + slot_bytes)(
        in_hbm(grad_output), partner_grad, own_meta, partner_meta
    )
    cot = shuffle(sent_cot)

    w_in, w_out = call(
        load_kernel,
        [
            pltpu.VMEM((width, hidden_width), BF16),
            pltpu.VMEM((hidden_width, width), BF16),
        ],
        0,
        4 * width * hidden_width,
        in_specs=[hbm] * 2,
        out_specs=[vmem] * 2,
        scratch_shapes=[pltpu.SemaphoreType.DMA((2,))],
    )(in_hbm(weight_in), in_hbm(weight_out))
    mid = pltpu.VMEM((slot_total, hidden_width), BF16)
    total = pltpu.VMEM((slot_total, width), F32)
    product = 2 * slot_total * width * hidden_width
    hidden, slope, outputs = call(
        forward_kernel,
        [mid, mid, slots],
        2 * product,
        2 * slot_bytes,
        16,
        in_specs=[vmem] * 3,
        out_specs=[vmem] * 3,
        scratch_shapes=[total],
    )(x, in_vmem(w_in), in_vmem(w_out))
    back_out = shuffle(outputs)
    grad_pre, grad_rows = call(
        backward_kernel,
        [mid, slots],
        2 * product,
        2 * slot_bytes,
        16,
        in_specs=[vmem] * 4,
        out_specs=[vmem] * 2,
        scratch_shapes=[total],
    )(cot, in_vmem(w_in), in_vmem(w_out), in_vmem(slope))
    back_grad = shuffle(grad_rows)
    tokens_f32, gates_shape = shape(token_rows, width, dtype=F32), shape(2, token_rows, dtype=F32)
    own_out, partner_out, own_gates, partner_gates = call(
        pick_outputs_kernel,
        [tokens_f32, token_shape, gates_shape, gates_shape],
        2 * place_flops,
        4 * token_bytes + slot_bytes,
    )(back_out, in_hbm(grad_output), partner_grad, own_meta, partner_meta)
    got_out, got_gates = exchange(partner_out), exchange(partner_gates)
    partner_back = call(
        pick_partner_kernel, token_shape, place_flops, slot_bytes + token_bytes
    )(back_grad, partner_meta)
    got_back = exchange(partner_back)
    grad_pre, partner_back = lax.optimization_barrier((grad_pre, partner_back))
    grad_in_w, grad_out_w = call(
        weights_kernel,
        [pltpu.HBM(weight_in.shape, BF16), pltpu.HBM(weight_out.shape, BF16)],
        2 * product,
        2 * slot_bytes + 4 * width * hidden_width,
        16,
        grid=(hidden_width // WIDE,),
        in_specs=[vmem] * 4,
        out_specs=[
            pl.BlockSpec((None, width, WIDE), lambda i: (0, 0, i)),
            pl.BlockSpec((None, WIDE, width), lambda i: (0, i, 0)),
        ],
    )(x, cot, in_vmem(hidden), in_vmem(grad_pre))
    combined, grad_tokens, grad_gates = call(
        finish_kernel,
        [token_shape, token_shape, gates_shape],
        place_flops,
        slot_bytes + 6 * token_bytes,
    )(back_grad, own_meta, got_back, own_out, got_out, own_gates, got_gates)
    return (combined, grad_tokens, grad_gates.T, grad_in_w, grad_out_w)


def solution(mesh):
    rows, cols = mesh.devices.shape
    axes = ("row", "half", "rest")
    halves = Mesh(mesh.devices.reshape(rows, 2, cols // 2), axes)
    flat, deep = P(axes, None), P(axes, None, None)
    return jax.shard_map(
        body,
        mesh=halves,
        in_specs=(flat, flat, flat, flat, deep, deep, flat),
        out_specs=(flat, flat, flat, deep, deep),
        check_vma=False,
    )
```

```python
import functools

import jax
import jax.numpy as jnp
from jax import lax
from jax.experimental import pallas as pl
from jax.experimental.pallas import tpu as pltpu
from jax.sharding import Mesh
from jax.sharding import PartitionSpec as P

BLOCK = 128
BF16 = jnp.bfloat16
F32 = jnp.float32
MIB = 1024 * 1024
SUB = 256
AXES = ("row", "half", "rest")
ALL = ("row", "rest", "half")
GROUP = ("row", "rest")


def dot(a, b, contract_a, contract_b):
    return lax.dot_general(
        a, b, (((contract_a,), (contract_b,)), ((), ())), preferred_element_type=F32
    )


def column(row):
    count = row.shape[1]
    return jnp.transpose(jnp.broadcast_to(row, (count, count)))


def route(rest_bits, capacity, half, ids_ref, keep_ref, gates_ref, mine_ref, other_ref):
    token_rows = ids_ref.shape[1]
    ids = ids_ref[...].astype(F32)
    earlier = lax.broadcasted_iota(jnp.int32, (token_rows, token_rows), 0) < lax.broadcasted_iota(
        jnp.int32, (token_rows, token_rows), 1
    )
    columns = (column(ids[0:1]), column(ids[1:2]))
    for k in range(2):
        count = jnp.zeros((token_rows, token_rows), F32)
        for other_choice in columns:
            count = count + jnp.where(earlier & (other_choice == ids[k : k + 1]), 1.0, 0.0)
        slot = jnp.sum(count, axis=0, keepdims=True).astype(jnp.int32)
        expert = ids_ref[k : k + 1, :]
        kept = keep_ref[k : k + 1, :] > 0
        side = (expert >> rest_bits) & 1
        local = ((expert >> (rest_bits + 1)) << rest_bits) + (expert & ((1 << rest_bits) - 1))
        base = local * (2 * capacity) + slot
        row = base + half * capacity
        mine_ref[k : k + 1, :] = jnp.where(kept & (side == half), row, -1).astype(F32)
        other_ref[k : k + 1, :] = jnp.where(kept & (side != half), row, -1).astype(F32)
        mine_ref[k + 4 : k + 5, :] = jnp.where(kept, base + side * capacity, -1).astype(F32)
        for ref in (mine_ref, other_ref):
            ref[k + 2 : k + 3, :] = gates_ref[k : k + 1, :]
    mine_ref[6:8, :] = jnp.zeros((2, token_rows), F32)
    other_ref[4:8, :] = jnp.zeros((4, token_rows), F32)


def hits(slot_total, meta_ref, k):
    rows = meta_ref[k : k + 1, :].astype(jnp.int32)
    index = lax.broadcasted_iota(jnp.int32, (slot_total, rows.shape[1]), 0)
    return index == rows


def one_hot(mask):
    return jnp.where(mask, 1.0, 0.0).astype(BF16)


def restore(tokens_ref):
    pieces = []
    for b in range(tokens_ref.shape[1] // BLOCK):
        x = tokens_ref[:, b * BLOCK : (b + 1) * BLOCK].astype(F32)
        scale = (jnp.max(jnp.abs(x), axis=1, keepdims=True) + 1e-06).astype(BF16).astype(F32)
        quantized = (x / scale).astype(BF16)
        pieces.append((quantized.astype(F32) * scale).astype(BF16))
    return jnp.concatenate(pieces, axis=1)


def place_tokens_kernel(
    rest_bits, capacity, half_ref, tokens_ref, ids_ref, keep_ref, gates_ref, mine_ref, other_ref, out_ref
):
    route(rest_bits, capacity, half_ref[0], ids_ref, keep_ref, gates_ref, mine_ref, other_ref)
    slot_total = out_ref.shape[0]
    mask = hits(slot_total, mine_ref, 4) | hits(slot_total, mine_ref, 5)
    out_ref[...] = dot(one_hot(mask), restore(tokens_ref), 1, 0).astype(BF16)


def scaled_rows(gate_row, grad_ref):
    gate = column(gate_row)
    pieces = [
        gate * grad_ref[:, b * BLOCK : (b + 1) * BLOCK].astype(F32)
        for b in range(grad_ref.shape[1] // BLOCK)
    ]
    return jnp.concatenate(pieces, axis=1)


def place_cotangents_kernel(own_grad, partner_grad, own_meta, partner_meta, out_ref):
    slot_total = out_ref.shape[0]
    total = None
    for grad_ref, meta_ref in ((own_grad, own_meta), (partner_grad, partner_meta)):
        for k in range(2):
            rows = scaled_rows(meta_ref[k + 2 : k + 3, :], grad_ref).astype(BF16)
            part = dot(one_hot(hits(slot_total, meta_ref, k)), rows, 1, 0)
            total = part if total is None else total + part
    out_ref[...] = total.astype(BF16)


def gelu_parts(v):
    c = 0.7978845608028654
    inner = c + (c * 0.044715) * (v * v)
    s = 0.5 + 0.5 * jnp.tanh(v * inner)
    hidden = v * s
    slope = s + (hidden * (1.0 - s)) * (6.0 * inner - 4.0 * c)
    return hidden.astype(BF16), slope.astype(BF16)


def forward_kernel(x_ref, w_in_ref, w_out_ref, hidden_ref, slope_ref, out_ref, total):
    step = pl.program_id(0)

    @pl.when(step == 0)
    def _():
        total[...] = jnp.zeros_like(total)

    parts = hidden_ref.shape[1] // SUB
    v = dot(x_ref[...], w_in_ref[:, :SUB], 1, 0)
    pieces = []
    for j in range(parts):
        if j + 1 < parts:
            after = dot(x_ref[...], w_in_ref[:, (j + 1) * SUB : (j + 2) * SUB], 1, 0)
        hidden, slope = gelu_parts(v)
        hidden_ref[:, j * SUB : (j + 1) * SUB] = hidden
        slope_ref[:, j * SUB : (j + 1) * SUB] = slope
        pieces.append(hidden)
        v = after
    total[...] += dot(jnp.concatenate(pieces, axis=1), w_out_ref[...], 1, 0)

    @pl.when(step == pl.num_programs(0) - 1)
    def _():
        out_ref[...] = total[...].astype(BF16)


def backward_kernel(cot_ref, w_in_ref, w_out_ref, slope_ref, grad_pre_ref, out_ref, total):
    step = pl.program_id(0)

    @pl.when(step == 0)
    def _():
        total[...] = jnp.zeros_like(total)

    parts = grad_pre_ref.shape[1] // SUB
    pieces = []
    for j in range(parts):
        grad_hidden = dot(cot_ref[...], w_out_ref[j * SUB : (j + 1) * SUB, :], 1, 1)
        slope = slope_ref[:, j * SUB : (j + 1) * SUB].astype(F32)
        grad_pre = (grad_hidden * slope).astype(BF16)
        grad_pre_ref[:, j * SUB : (j + 1) * SUB] = grad_pre
        pieces.append(grad_pre)
    total[...] += dot(jnp.concatenate(pieces, axis=1), w_in_ref[...], 1, 1)

    @pl.when(step == pl.num_programs(0) - 1)
    def _():
        out_ref[...] = total[...].astype(BF16)


def weights_kernel(x_ref, cot_ref, hidden_ref, grad_pre_ref, grad_in_ref, grad_out_ref):
    grad_in_ref[...] = dot(x_ref[...], grad_pre_ref[...], 0, 0).astype(BF16)
    grad_out_ref[...] = dot(hidden_ref[...], cot_ref[...], 0, 0).astype(BF16)


def pick_outputs_kernel(
    back_ref, own_grad, partner_grad, own_meta, partner_meta, own_out, partner_out, own_gates, partner_gates
):
    slot_total = back_ref.shape[0]
    for grad_ref, meta_ref, out_ref, gates_ref in (
        (own_grad, own_meta, own_out, own_gates),
        (partner_grad, partner_meta, partner_out, partner_gates),
    ):
        total = None
        for k in range(2):
            picked = dot(one_hot(hits(slot_total, meta_ref, k)), back_ref[...], 0, 0)
            gate = column(meta_ref[k + 2 : k + 3, :])
            weighted = jnp.concatenate(
                [
                    gate * picked[:, b * BLOCK : (b + 1) * BLOCK]
                    for b in range(picked.shape[1] // BLOCK)
                ],
                axis=1,
            )
            total = weighted if total is None else total + weighted
            sums = jnp.sum(picked * grad_ref[...].astype(F32), axis=1, keepdims=True)
            rows = jnp.transpose(jnp.broadcast_to(sums, (sums.shape[0], sums.shape[0])))
            gates_ref[k : k + 1, :] = rows[0:1, :]
        out_ref[...] = total.astype(out_ref.dtype)


def pick_partner_kernel(back_ref, meta_ref, out_ref):
    slot_total = back_ref.shape[0]
    mask = hits(slot_total, meta_ref, 0) | hits(slot_total, meta_ref, 1)
    out_ref[...] = dot(one_hot(mask), back_ref[...], 0, 0).astype(BF16)


def finish_kernel(
    back_ref, meta_ref, got_back, own_out, got_out, own_gates, got_gates, combined, grad_tokens, grad_gates
):
    slot_total = back_ref.shape[0]
    mask = hits(slot_total, meta_ref, 0) | hits(slot_total, meta_ref, 1)
    own = dot(one_hot(mask), back_ref[...], 0, 0)
    grad_tokens[...] = (own + got_back[...].astype(F32)).astype(BF16)
    combined[...] = (own_out[...] + got_out[...].astype(F32)).astype(BF16)
    grad_gates[...] = own_gates[...] + got_gates[...]


def call(kernel, outs, flops=0, traffic=0, limit=12, **options):
    return pl.pallas_call(
        kernel,
        out_shape=outs,
        compiler_params=pltpu.CompilerParams(vmem_limit_bytes=limit * MIB),
        cost_estimate=pl.CostEstimate(flops=flops, bytes_accessed=traffic, transcendentals=0),
        **options,
    )


def in_hbm(values):
    return pltpu.with_memory_space_constraint(values, pltpu.HBM)


def body(tokens, expert_ids, keep_mask, gate_weights, weight_in, weight_out, grad_output):
    token_rows, width = tokens.shape
    hidden_width = weight_in.shape[2]
    rest_count = lax.axis_size("rest")
    members = lax.axis_size("row") * rest_count
    capacity = expert_ids.shape[1] * token_rows // members
    slot_total = 2 * members * capacity

    def exchange(values):
        return lax.ppermute(values, "half", ((0, 1), (1, 0)))

    def shuffle(rows, group, peers):
        shaped = rows.reshape(peers, slot_total // peers, width)
        return lax.all_to_all(shaped, group, split_axis=0, concat_axis=0, tiled=True).reshape(
            rows.shape
        )

    def shape(*dims, dtype=BF16):
        return jax.ShapeDtypeStruct(dims, dtype)

    vmem = pl.BlockSpec(memory_space=pltpu.VMEM)
    meta_shape = shape(8, token_rows, dtype=F32)
    slots, token_shape = shape(slot_total, width), shape(token_rows, width)
    slot_bytes, token_bytes = slot_total * width * 2, token_rows * width * 2
    place_flops = 2 * slot_total * token_rows * width

    partner_grad = exchange(grad_output)
    half = lax.axis_index("half").astype(jnp.int32).reshape(1)
    own_meta, sent_meta, sent = call(
        functools.partial(place_tokens_kernel, rest_count.bit_length() - 1, capacity),
        [meta_shape, meta_shape, slots],
        place_flops,
        token_bytes + slot_bytes,
        in_specs=[pl.BlockSpec(memory_space=pltpu.SMEM)] + [vmem] * 4,
    )(
        half,
        in_hbm(tokens),
        in_hbm(expert_ids.T),
        in_hbm(keep_mask.T),
        in_hbm(gate_weights.T),
    )
    x = shuffle(sent, ALL, 2 * members)
    partner_meta = exchange(sent_meta)
    sent_cot = call(
        place_cotangents_kernel, slots, 4 * place_flops, 2 * token_bytes + slot_bytes
    )(in_hbm(grad_output), partner_grad, own_meta, partner_meta)
    cot = shuffle(sent_cot, GROUP, members)

    chunk = 1024
    whole = pl.BlockSpec((slot_total, width), lambda i: (0, 0))
    in_spec = pl.BlockSpec((None, width, chunk), lambda i: (0, 0, i))
    out_spec = pl.BlockSpec((None, chunk, width), lambda i: (0, i, 0))
    mid_spec = pl.BlockSpec((slot_total, chunk), lambda i: (0, i))
    mid = pltpu.HBM((slot_total, hidden_width), BF16)
    product = 2 * slot_total * width * hidden_width
    traffic = 2 * slot_bytes + 4 * width * hidden_width + 4 * slot_total * hidden_width
    grid = (hidden_width // chunk,)
    total = pltpu.VMEM((slot_total, width), F32)
    weight_in, weight_out = in_hbm(weight_in), in_hbm(weight_out)
    hidden, slope, outputs = call(
        forward_kernel,
        [mid, mid, slots],
        2 * product,
        traffic,
        32,
        grid=grid,
        in_specs=[whole, in_spec, out_spec],
        out_specs=[mid_spec, mid_spec, whole],
        scratch_shapes=[total],
    )(x, weight_in, weight_out)
    back_out = shuffle(outputs, GROUP, members)
    grad_pre, grad_rows = call(
        backward_kernel,
        [mid, slots],
        2 * product,
        traffic,
        32,
        grid=grid,
        in_specs=[whole, in_spec, out_spec, mid_spec],
        out_specs=[mid_spec, whole],
        scratch_shapes=[total],
    )(cot, weight_in, weight_out, in_hbm(slope))
    back_grad = shuffle(grad_rows, GROUP, members)
    tokens_f32, gates_shape = shape(token_rows, width, dtype=F32), shape(2, token_rows, dtype=F32)
    own_out, partner_out, own_gates, partner_gates = call(
        pick_outputs_kernel,
        [tokens_f32, token_shape, gates_shape, gates_shape],
        4 * place_flops,
        4 * token_bytes + slot_bytes,
    )(back_out, in_hbm(grad_output), partner_grad, own_meta, partner_meta)
    got_out, got_gates = exchange(partner_out), exchange(partner_gates)
    partner_back = call(
        pick_partner_kernel, token_shape, place_flops, slot_bytes + token_bytes
    )(back_grad, partner_meta)
    got_back = exchange(partner_back)
    grad_pre, partner_back = lax.optimization_barrier((grad_pre, partner_back))
    grad_in_w, grad_out_w = call(
        weights_kernel,
        [pltpu.HBM(weight_in.shape, BF16), pltpu.HBM(weight_out.shape, BF16)],
        2 * product,
        traffic,
        32,
        grid=grid,
        in_specs=[whole, whole, mid_spec, mid_spec],
        out_specs=[in_spec, out_spec],
    )(x, cot, in_hbm(hidden), in_hbm(grad_pre))
    combined, grad_tokens, grad_gates = call(
        finish_kernel,
        [token_shape, token_shape, gates_shape],
        place_flops,
        slot_bytes + 6 * token_bytes,
    )(back_grad, own_meta, got_back, own_out, got_out, own_gates, got_gates)
    return (combined, grad_tokens, grad_gates.T, grad_in_w, grad_out_w)


def solution(mesh):
    rows, cols = mesh.devices.shape
    halves = Mesh(mesh.devices.reshape(rows, 2, cols // 2), AXES)
    flat, deep = P(AXES, None), P(AXES, None, None)
    return jax.shard_map(
        body,
        mesh=halves,
        in_specs=(flat, flat, flat, flat, deep, deep, flat),
        out_specs=(flat, flat, flat, deep, deep),
        check_vma=False,
    )
```

```python
import functools

import jax
import jax.numpy as jnp
from jax import lax
from jax.experimental import pallas as pl
from jax.experimental.pallas import tpu as pltpu
from jax.sharding import Mesh
from jax.sharding import PartitionSpec as P

BLOCK = 128
BF16 = jnp.bfloat16
F32 = jnp.float32
MIB = 1024 * 1024
SUB = 256
AXES = ("row", "half", "rest")
ALL = ("row", "rest", "half")
GROUP = ("row", "rest")


def dot(a, b, contract_a, contract_b):
    return lax.dot_general(
        a, b, (((contract_a,), (contract_b,)), ((), ())), preferred_element_type=F32
    )


def column(row):
    count = row.shape[1]
    return jnp.transpose(jnp.broadcast_to(row, (count, count)))


def route(rest_bits, capacity, half, ids_ref, keep_ref, gates_ref, mine_ref, other_ref):
    token_rows = ids_ref.shape[1]
    ids = ids_ref[...].astype(F32)
    earlier = lax.broadcasted_iota(jnp.int32, (token_rows, token_rows), 0) < lax.broadcasted_iota(
        jnp.int32, (token_rows, token_rows), 1
    )
    columns = (column(ids[0:1]), column(ids[1:2]))
    for k in range(2):
        count = jnp.zeros((token_rows, token_rows), F32)
        for other_choice in columns:
            count = count + jnp.where(earlier & (other_choice == ids[k : k + 1]), 1.0, 0.0)
        slot = jnp.sum(count, axis=0, keepdims=True).astype(jnp.int32)
        expert = ids_ref[k : k + 1, :]
        kept = keep_ref[k : k + 1, :] > 0
        side = (expert >> rest_bits) & 1
        local = ((expert >> (rest_bits + 1)) << rest_bits) + (expert & ((1 << rest_bits) - 1))
        base = local * (2 * capacity) + slot
        row = base + half * capacity
        mine_ref[k : k + 1, :] = jnp.where(kept & (side == half), row, -1).astype(F32)
        other_ref[k : k + 1, :] = jnp.where(kept & (side != half), row, -1).astype(F32)
        mine_ref[k + 4 : k + 5, :] = jnp.where(kept, base + side * capacity, -1).astype(F32)
        for ref in (mine_ref, other_ref):
            ref[k + 2 : k + 3, :] = gates_ref[k : k + 1, :]
    mine_ref[6:8, :] = jnp.zeros((2, token_rows), F32)
    other_ref[4:8, :] = jnp.zeros((4, token_rows), F32)


def hits(slot_total, meta_ref, k):
    rows = meta_ref[k : k + 1, :].astype(jnp.int32)
    index = lax.broadcasted_iota(jnp.int32, (slot_total, rows.shape[1]), 0)
    return index == rows


def one_hot(mask):
    return jnp.where(mask, 1.0, 0.0).astype(BF16)


def restore(tokens_ref):
    pieces = []
    for b in range(tokens_ref.shape[1] // BLOCK):
        x = tokens_ref[:, b * BLOCK : (b + 1) * BLOCK].astype(F32)
        scale = (jnp.max(jnp.abs(x), axis=1, keepdims=True) + 1e-06).astype(BF16).astype(F32)
        quantized = (x / scale).astype(BF16)
        pieces.append((quantized.astype(F32) * scale).astype(BF16))
    return jnp.concatenate(pieces, axis=1)


def place_tokens_kernel(
    rest_bits, capacity, half_ref, tokens_ref, ids_ref, keep_ref, gates_ref, mine_ref, other_ref, out_ref
):
    route(rest_bits, capacity, half_ref[0], ids_ref, keep_ref, gates_ref, mine_ref, other_ref)
    slot_total = out_ref.shape[0]
    mask = hits(slot_total, mine_ref, 4) | hits(slot_total, mine_ref, 5)
    out_ref[...] = dot(one_hot(mask), restore(tokens_ref), 1, 0).astype(BF16)


def scaled_rows(gate_row, grad_ref):
    gate = column(gate_row)
    pieces = [
        gate * grad_ref[:, b * BLOCK : (b + 1) * BLOCK].astype(F32)
        for b in range(grad_ref.shape[1] // BLOCK)
    ]
    return jnp.concatenate(pieces, axis=1)


def place_cotangents_kernel(half_ref, both_grads, own_meta, partner_meta, out_ref):
    slot_total = out_ref.shape[0]
    half = half_ref[0]
    total = None
    for grad_ref, meta_ref in (
        (both_grads.at[half], own_meta),
        (both_grads.at[1 - half], partner_meta),
    ):
        for k in range(2):
            rows = scaled_rows(meta_ref[k + 2 : k + 3, :], grad_ref).astype(BF16)
            part = dot(one_hot(hits(slot_total, meta_ref, k)), rows, 1, 0)
            total = part if total is None else total + part
    out_ref[...] = total.astype(BF16)


def gelu_parts(v):
    c = 0.7978845608028654
    inner = c + (c * 0.044715) * (v * v)
    s = 0.5 + 0.5 * jnp.tanh(v * inner)
    hidden = v * s
    slope = s + (hidden * (1.0 - s)) * (6.0 * inner - 4.0 * c)
    return hidden.astype(BF16), slope.astype(BF16)


def forward_kernel(x_ref, w_in_ref, w_out_ref, hidden_ref, slope_ref, out_ref, total):
    step = pl.program_id(0)

    @pl.when(step == 0)
    def _():
        total[...] = jnp.zeros_like(total)

    parts = hidden_ref.shape[1] // SUB
    v = dot(x_ref[...], w_in_ref[:, :SUB], 1, 0)
    pieces = []
    for j in range(parts):
        if j + 1 < parts:
            after = dot(x_ref[...], w_in_ref[:, (j + 1) * SUB : (j + 2) * SUB], 1, 0)
        hidden, slope = gelu_parts(v)
        hidden_ref[:, j * SUB : (j + 1) * SUB] = hidden
        slope_ref[:, j * SUB : (j + 1) * SUB] = slope
        pieces.append(hidden)
        v = after
    total[...] += dot(jnp.concatenate(pieces, axis=1), w_out_ref[...], 1, 0)

    @pl.when(step == pl.num_programs(0) - 1)
    def _():
        out_ref[...] = total[...].astype(BF16)


def backward_kernel(cot_ref, w_in_ref, w_out_ref, slope_ref, grad_pre_ref, out_ref, total):
    step = pl.program_id(0)

    @pl.when(step == 0)
    def _():
        total[...] = jnp.zeros_like(total)

    parts = grad_pre_ref.shape[1] // SUB
    pieces = []
    for j in range(parts):
        grad_hidden = dot(cot_ref[...], w_out_ref[j * SUB : (j + 1) * SUB, :], 1, 1)
        slope = slope_ref[:, j * SUB : (j + 1) * SUB].astype(F32)
        grad_pre = (grad_hidden * slope).astype(BF16)
        grad_pre_ref[:, j * SUB : (j + 1) * SUB] = grad_pre
        pieces.append(grad_pre)
    total[...] += dot(jnp.concatenate(pieces, axis=1), w_in_ref[...], 1, 1)

    @pl.when(step == pl.num_programs(0) - 1)
    def _():
        out_ref[...] = total[...].astype(BF16)


def weights_kernel(x_ref, cot_ref, hidden_ref, grad_pre_ref, grad_in_ref, grad_out_ref):
    grad_in_ref[...] = dot(x_ref[...], grad_pre_ref[...], 0, 0).astype(BF16)
    grad_out_ref[...] = dot(hidden_ref[...], cot_ref[...], 0, 0).astype(BF16)


def pick_outputs_kernel(
    half_ref, back_ref, both_grads, own_meta, partner_meta, own_out, partner_out, own_gates, partner_gates
):
    slot_total = back_ref.shape[0]
    half = half_ref[0]
    for grad_ref, meta_ref, out_ref, gates_ref in (
        (both_grads.at[half], own_meta, own_out, own_gates),
        (both_grads.at[1 - half], partner_meta, partner_out, partner_gates),
    ):
        total = None
        for k in range(2):
            picked = dot(one_hot(hits(slot_total, meta_ref, k)), back_ref[...], 0, 0)
            gate = column(meta_ref[k + 2 : k + 3, :])
            weighted = jnp.concatenate(
                [
                    gate * picked[:, b * BLOCK : (b + 1) * BLOCK]
                    for b in range(picked.shape[1] // BLOCK)
                ],
                axis=1,
            )
            total = weighted if total is None else total + weighted
            sums = jnp.sum(picked * grad_ref[...].astype(F32), axis=1, keepdims=True)
            rows = jnp.transpose(jnp.broadcast_to(sums, (sums.shape[0], sums.shape[0])))
            gates_ref[k : k + 1, :] = rows[0:1, :]
        out_ref[...] = total.astype(out_ref.dtype)


def finish_outputs_kernel(own_out, got_out, own_gates, got_gates, combined, grad_gates):
    combined[...] = (own_out[...] + got_out[...].astype(F32)).astype(BF16)
    grad_gates[...] = own_gates[...] + got_gates[...]


def pick_gradients_kernel(back_ref, meta_ref, out_ref):
    slot_total = back_ref.shape[0]
    mask = hits(slot_total, meta_ref, 4) | hits(slot_total, meta_ref, 5)
    out_ref[...] = dot(one_hot(mask), back_ref[...], 0, 0).astype(BF16)


def call(kernel, outs, flops=0, traffic=0, limit=12, **options):
    return pl.pallas_call(
        kernel,
        out_shape=outs,
        compiler_params=pltpu.CompilerParams(vmem_limit_bytes=limit * MIB),
        cost_estimate=pl.CostEstimate(flops=flops, bytes_accessed=traffic, transcendentals=0),
        **options,
    )


def in_hbm(values):
    return pltpu.with_memory_space_constraint(values, pltpu.HBM)


def body(tokens, expert_ids, keep_mask, gate_weights, weight_in, weight_out, grad_output):
    token_rows, width = tokens.shape
    hidden_width = weight_in.shape[2]
    rest_count = lax.axis_size("rest")
    members = lax.axis_size("row") * rest_count
    capacity = expert_ids.shape[1] * token_rows // members
    slot_total = 2 * members * capacity

    def exchange(values):
        return lax.ppermute(values, "half", ((0, 1), (1, 0)))

    def shuffle(rows, group, peers):
        shaped = rows.reshape(peers, slot_total // peers, width)
        return lax.all_to_all(shaped, group, split_axis=0, concat_axis=0, tiled=True).reshape(
            rows.shape
        )

    def shape(*dims, dtype=BF16):
        return jax.ShapeDtypeStruct(dims, dtype)

    vmem = pl.BlockSpec(memory_space=pltpu.VMEM)
    meta_shape = shape(8, token_rows, dtype=F32)
    slots, token_shape = shape(slot_total, width), shape(token_rows, width)
    slot_bytes, token_bytes = slot_total * width * 2, token_rows * width * 2
    place_flops = 2 * slot_total * token_rows * width

    both_grads = lax.all_gather(grad_output, "half")
    half = lax.axis_index("half").astype(jnp.int32).reshape(1)
    own_meta, sent_meta, sent = call(
        functools.partial(place_tokens_kernel, rest_count.bit_length() - 1, capacity),
        [meta_shape, meta_shape, slots],
        place_flops,
        token_bytes + slot_bytes,
        in_specs=[pl.BlockSpec(memory_space=pltpu.SMEM)] + [vmem] * 4,
    )(
        half,
        in_hbm(tokens),
        in_hbm(expert_ids.T),
        in_hbm(keep_mask.T),
        in_hbm(gate_weights.T),
    )
    x = shuffle(sent, ALL, 2 * members)
    partner_meta = exchange(sent_meta)
    smem = pl.BlockSpec(memory_space=pltpu.SMEM)
    sent_cot = call(
        place_cotangents_kernel,
        slots,
        4 * place_flops,
        2 * token_bytes + slot_bytes,
        in_specs=[smem] + [vmem] * 3,
    )(half, both_grads, own_meta, partner_meta)
    cot = shuffle(sent_cot, GROUP, members)

    chunk = 1024
    whole = pl.BlockSpec((slot_total, width), lambda i: (0, 0))
    in_spec = pl.BlockSpec((None, width, chunk), lambda i: (0, 0, i))
    out_spec = pl.BlockSpec((None, chunk, width), lambda i: (0, i, 0))
    mid_spec = pl.BlockSpec((slot_total, chunk), lambda i: (0, i))
    mid = pltpu.HBM((slot_total, hidden_width), BF16)
    product = 2 * slot_total * width * hidden_width
    traffic = 2 * slot_bytes + 4 * width * hidden_width + 4 * slot_total * hidden_width
    grid = (hidden_width // chunk,)
    total = pltpu.VMEM((slot_total, width), F32)
    weight_in, weight_out = in_hbm(weight_in), in_hbm(weight_out)
    hidden, slope, outputs = call(
        forward_kernel,
        [mid, mid, slots],
        2 * product,
        traffic,
        32,
        grid=grid,
        in_specs=[vmem, in_spec, out_spec],
        out_specs=[mid_spec, mid_spec, whole],
        scratch_shapes=[total],
    )(x, weight_in, weight_out)
    back_out = shuffle(outputs, GROUP, members)
    grad_pre, grad_rows = call(
        backward_kernel,
        [mid, slots],
        2 * product,
        traffic,
        32,
        grid=grid,
        in_specs=[vmem, in_spec, out_spec, mid_spec],
        out_specs=[mid_spec, whole],
        scratch_shapes=[total],
    )(cot, weight_in, weight_out, in_hbm(slope))
    back_grad = shuffle(grad_rows, ALL, 2 * members)
    tokens_f32, gates_shape = shape(token_rows, width, dtype=F32), shape(2, token_rows, dtype=F32)
    own_out, partner_out, own_gates, partner_gates = call(
        pick_outputs_kernel,
        [tokens_f32, token_shape, gates_shape, gates_shape],
        4 * place_flops,
        4 * token_bytes + slot_bytes,
        in_specs=[smem] + [vmem] * 4,
    )(half, back_out, both_grads, own_meta, partner_meta)
    grad_pre, partner_out = lax.optimization_barrier((grad_pre, partner_out))
    got_out, got_gates = exchange(partner_out), exchange(partner_gates)
    grad_in_w, grad_out_w = call(
        weights_kernel,
        [pltpu.HBM(weight_in.shape, BF16), pltpu.HBM(weight_out.shape, BF16)],
        2 * product,
        traffic,
        32,
        grid=grid,
        in_specs=[vmem, vmem, mid_spec, mid_spec],
        out_specs=[in_spec, out_spec],
    )(x, cot, in_hbm(hidden), in_hbm(grad_pre))
    combined, grad_gates = call(
        finish_outputs_kernel, [token_shape, gates_shape], 0, 6 * token_bytes
    )(own_out, got_out, own_gates, got_gates)
    grad_tokens = call(
        pick_gradients_kernel, token_shape, place_flops, slot_bytes + token_bytes
    )(back_grad, own_meta)
    return (combined, grad_tokens, grad_gates.T, grad_in_w, grad_out_w)


def solution(mesh):
    rows, cols = mesh.devices.shape
    halves = Mesh(mesh.devices.reshape(rows, 2, cols // 2), AXES)
    flat, deep = P(AXES, None), P(AXES, None, None)
    return jax.shard_map(
        body,
        mesh=halves,
        in_specs=(flat, flat, flat, flat, deep, deep, flat),
        out_specs=(flat, flat, flat, deep, deep),
        check_vma=False,
    )
```

```python
import functools

import jax
import jax.numpy as jnp
from jax import lax
from jax.experimental import pallas as pl
from jax.experimental.pallas import tpu as pltpu
from jax.sharding import Mesh
from jax.sharding import PartitionSpec as P

BLOCK = 128
BF16 = jnp.bfloat16
F32 = jnp.float32
MIB = 1024 * 1024
SUB = 256
AXES = ("row", "high", "low", "inner")
GROUP = ("inner", "row", "low", "high")


def dot(a, b, contract_a, contract_b):
    return lax.dot_general(
        a, b, (((contract_a,), (contract_b,)), ((), ())), preferred_element_type=F32
    )


def column(row):
    count = row.shape[1]
    return jnp.transpose(jnp.broadcast_to(row, (count, count)))


def route(ids_ref, keep_ref, gates_ref, meta_ref, capacity, place_of):
    token_rows = ids_ref.shape[1]
    ids = ids_ref[...].astype(F32)
    earlier = lax.broadcasted_iota(jnp.int32, (token_rows, token_rows), 0) < lax.broadcasted_iota(
        jnp.int32, (token_rows, token_rows), 1
    )
    columns = (column(ids[0:1]), column(ids[1:2]))
    for k in range(2):
        count = jnp.zeros((token_rows, token_rows), F32)
        for other_choice in columns:
            count = count + jnp.where(earlier & (other_choice == ids[k : k + 1]), 1.0, 0.0)
        slot = jnp.sum(count, axis=0, keepdims=True).astype(jnp.int32)
        row = place_of(ids_ref[k : k + 1, :]) * capacity + slot
        meta_ref[k : k + 1, :] = jnp.where(keep_ref[k : k + 1, :] > 0, row, -1).astype(F32)
        meta_ref[k + 2 : k + 3, :] = gates_ref[k : k + 1, :]
    meta_ref[4:8, :] = jnp.zeros((4, token_rows), F32)


def hits(slot_total, meta_ref, k):
    rows = meta_ref[k : k + 1, :].astype(jnp.int32)
    index = lax.broadcasted_iota(jnp.int32, (slot_total, rows.shape[1]), 0)
    return index == rows


def one_hot(mask):
    return jnp.where(mask, 1.0, 0.0).astype(BF16)


def restore(tokens_ref):
    pieces = []
    for b in range(tokens_ref.shape[1] // BLOCK):
        x = tokens_ref[:, b * BLOCK : (b + 1) * BLOCK].astype(F32)
        scale = (jnp.max(jnp.abs(x), axis=1, keepdims=True) + 1e-06).astype(BF16).astype(F32)
        quantized = (x / scale).astype(BF16)
        pieces.append((quantized.astype(F32) * scale).astype(BF16))
    return jnp.concatenate(pieces, axis=1)


def place_tokens_kernel(capacity, place_of, tokens_ref, ids_ref, keep_ref, gates_ref, meta_ref, out_ref):
    route(ids_ref, keep_ref, gates_ref, meta_ref, capacity, place_of)
    slot_total = out_ref.shape[0]
    mask = hits(slot_total, meta_ref, 0) | hits(slot_total, meta_ref, 1)
    out_ref[...] = dot(one_hot(mask), restore(tokens_ref), 1, 0).astype(BF16)


def scaled_rows(gate_row, grad_ref):
    gate = column(gate_row)
    pieces = [
        gate * grad_ref[:, b * BLOCK : (b + 1) * BLOCK].astype(F32)
        for b in range(grad_ref.shape[1] // BLOCK)
    ]
    return jnp.concatenate(pieces, axis=1)


def place_cotangents_kernel(grad_ref, meta_ref, out_ref):
    slot_total = out_ref.shape[0]
    parts = [
        dot(
            one_hot(hits(slot_total, meta_ref, k)),
            scaled_rows(meta_ref[k + 2 : k + 3, :], grad_ref).astype(BF16),
            1,
            0,
        )
        for k in range(2)
    ]
    out_ref[...] = (parts[0] + parts[1]).astype(BF16)


def gelu_parts(v):
    c = 0.7978845608028654
    inner = c + (c * 0.044715) * (v * v)
    s = 0.5 + 0.5 * jnp.tanh(v * inner)
    hidden = v * s
    slope = s + (hidden * (1.0 - s)) * (6.0 * inner - 4.0 * c)
    return hidden.astype(BF16), slope.astype(BF16)


def forward_kernel(x_ref, w_in_ref, w_out_ref, hidden_ref, slope_ref, out_ref, total):
    step = pl.program_id(0)

    @pl.when(step == 0)
    def _():
        total[...] = jnp.zeros_like(total)

    parts = hidden_ref.shape[1] // SUB
    v = dot(x_ref[...], w_in_ref[:, :SUB], 1, 0)
    pieces = []
    for j in range(parts):
        if j + 1 < parts:
            after = dot(x_ref[...], w_in_ref[:, (j + 1) * SUB : (j + 2) * SUB], 1, 0)
        hidden, slope = gelu_parts(v)
        hidden_ref[:, j * SUB : (j + 1) * SUB] = hidden
        slope_ref[:, j * SUB : (j + 1) * SUB] = slope
        pieces.append(hidden)
        v = after
    total[...] += dot(jnp.concatenate(pieces, axis=1), w_out_ref[...], 1, 0)

    @pl.when(step == pl.num_programs(0) - 1)
    def _():
        out_ref[...] = total[...].astype(BF16)


def backward_kernel(cot_ref, w_in_ref, w_out_ref, slope_ref, grad_pre_ref, out_ref, total):
    step = pl.program_id(0)

    @pl.when(step == 0)
    def _():
        total[...] = jnp.zeros_like(total)

    parts = grad_pre_ref.shape[1] // SUB
    pieces = []
    for j in range(parts):
        grad_hidden = dot(cot_ref[...], w_out_ref[j * SUB : (j + 1) * SUB, :], 1, 1)
        slope = slope_ref[:, j * SUB : (j + 1) * SUB].astype(F32)
        grad_pre = (grad_hidden * slope).astype(BF16)
        grad_pre_ref[:, j * SUB : (j + 1) * SUB] = grad_pre
        pieces.append(grad_pre)
    total[...] += dot(jnp.concatenate(pieces, axis=1), w_in_ref[...], 1, 1)

    @pl.when(step == pl.num_programs(0) - 1)
    def _():
        out_ref[...] = total[...].astype(BF16)


def weights_kernel(x_ref, cot_ref, hidden_ref, grad_pre_ref, grad_in_ref, grad_out_ref):
    grad_in_ref[...] = dot(x_ref[...], grad_pre_ref[...], 0, 0).astype(BF16)
    grad_out_ref[...] = dot(hidden_ref[...], cot_ref[...], 0, 0).astype(BF16)


def pick_outputs_kernel(back_ref, grad_ref, meta_ref, out_ref, gates_ref):
    slot_total = back_ref.shape[0]
    total = None
    for k in range(2):
        picked = dot(one_hot(hits(slot_total, meta_ref, k)), back_ref[...], 0, 0)
        gate = column(meta_ref[k + 2 : k + 3, :])
        weighted = jnp.concatenate(
            [
                gate * picked[:, b * BLOCK : (b + 1) * BLOCK]
                for b in range(picked.shape[1] // BLOCK)
            ],
            axis=1,
        )
        total = weighted if total is None else total + weighted
        sums = jnp.sum(picked * grad_ref[...].astype(F32), axis=1, keepdims=True)
        rows = jnp.transpose(jnp.broadcast_to(sums, (sums.shape[0], sums.shape[0])))
        gates_ref[k : k + 1, :] = rows[0:1, :]
    out_ref[...] = total.astype(BF16)


def pick_gradients_kernel(back_ref, meta_ref, out_ref):
    slot_total = back_ref.shape[0]
    mask = hits(slot_total, meta_ref, 0) | hits(slot_total, meta_ref, 1)
    out_ref[...] = dot(one_hot(mask), back_ref[...], 0, 0).astype(BF16)


def call(kernel, outs, flops=0, traffic=0, limit=12, **options):
    return pl.pallas_call(
        kernel,
        out_shape=outs,
        compiler_params=pltpu.CompilerParams(vmem_limit_bytes=limit * MIB),
        cost_estimate=pl.CostEstimate(flops=flops, bytes_accessed=traffic, transcendentals=0),
        **options,
    )


def in_hbm(values):
    return pltpu.with_memory_space_constraint(values, pltpu.HBM)


def body(tokens, expert_ids, keep_mask, gate_weights, weight_in, weight_out, grad_output):
    token_rows, width = tokens.shape
    hidden_width = weight_in.shape[2]
    row_count, low = lax.axis_size("row"), lax.axis_size("low")
    experts = row_count * low * 4
    bits = low.bit_length() - 1

    def place_of(expert):
        inner_at = expert & 1
        low_at = (expert >> 1) & (low - 1)
        high_at = (expert >> (bits + 1)) & 1
        row_at = expert >> (bits + 2)
        return ((((inner_at * row_count + row_at) << bits) + low_at) << 1) + high_at

    capacity = 2 * expert_ids.shape[1] * token_rows // experts
    slot_total = experts * capacity

    def shuffle(rows):
        shaped = rows.reshape(experts, capacity, width)
        return lax.all_to_all(
            shaped, GROUP, split_axis=0, concat_axis=0, tiled=True
        ).reshape(slot_total, width)

    slots = jax.ShapeDtypeStruct((slot_total, width), BF16)
    slot_bytes = slot_total * width * 2
    token_bytes = token_rows * width * 2
    place_flops = 2 * slot_total * token_rows * width
    meta, sent = call(
        functools.partial(place_tokens_kernel, capacity, place_of),
        [jax.ShapeDtypeStruct((8, token_rows), F32), slots],
        place_flops,
        token_bytes + slot_bytes,
    )(in_hbm(tokens), in_hbm(expert_ids.T), in_hbm(keep_mask.T), in_hbm(gate_weights.T))
    x = shuffle(sent)
    sent_cot = call(
        place_cotangents_kernel, slots, 2 * place_flops, token_bytes + slot_bytes
    )(in_hbm(grad_output), meta)
    cot = shuffle(sent_cot)

    chunk = 1024
    whole = pl.BlockSpec((slot_total, width), lambda i: (0, 0))
    in_spec = pl.BlockSpec((None, width, chunk), lambda i: (0, 0, i))
    out_spec = pl.BlockSpec((None, chunk, width), lambda i: (0, i, 0))
    mid_spec = pl.BlockSpec((slot_total, chunk), lambda i: (0, i))
    mid = pltpu.HBM((slot_total, hidden_width), BF16)
    product = 2 * slot_total * width * hidden_width
    traffic = 2 * slot_bytes + 4 * width * hidden_width + 4 * slot_total * hidden_width
    grid = (hidden_width // chunk,)
    total = pltpu.VMEM((slot_total, width), F32)
    weight_in, weight_out = in_hbm(weight_in), in_hbm(weight_out)
    hidden, slope, outputs = call(
        forward_kernel,
        [mid, mid, slots],
        2 * product,
        traffic,
        32,
        grid=grid,
        in_specs=[whole, in_spec, out_spec],
        out_specs=[mid_spec, mid_spec, whole],
        scratch_shapes=[total],
    )(x, weight_in, weight_out)
    back_out = shuffle(outputs)
    grad_pre, grad_rows = call(
        backward_kernel,
        [mid, slots],
        2 * product,
        traffic,
        32,
        grid=grid,
        in_specs=[whole, in_spec, out_spec, mid_spec],
        out_specs=[mid_spec, whole],
        scratch_shapes=[total],
    )(cot, weight_in, weight_out, in_hbm(slope))
    back_grad = shuffle(grad_rows)
    combined, grad_gates = call(
        pick_outputs_kernel,
        [
            jax.ShapeDtypeStruct((token_rows, width), BF16),
            jax.ShapeDtypeStruct((2, token_rows), F32),
        ],
        2 * place_flops,
        2 * token_bytes + slot_bytes,
    )(back_out, in_hbm(grad_output), meta)
    grad_in_w, grad_out_w = call(
        weights_kernel,
        [pltpu.HBM(weight_in.shape, BF16), pltpu.HBM(weight_out.shape, BF16)],
        2 * product,
        traffic,
        32,
        grid=grid,
        in_specs=[whole, whole, mid_spec, mid_spec],
        out_specs=[in_spec, out_spec],
    )(x, cot, in_hbm(hidden), in_hbm(grad_pre))
    grad_tokens = call(
        pick_gradients_kernel,
        jax.ShapeDtypeStruct((token_rows, width), BF16),
        place_flops,
        slot_bytes + token_bytes,
    )(back_grad, meta)
    return (combined, grad_tokens, grad_gates.T, grad_in_w, grad_out_w)


def solution(mesh):
    rows, cols = mesh.devices.shape
    split = Mesh(mesh.devices.reshape(rows, 2, cols // 4, 2), AXES)
    flat, deep = P(AXES, None), P(AXES, None, None)
    return jax.shard_map(
        body,
        mesh=split,
        in_specs=(flat, flat, flat, flat, deep, deep, flat),
        out_specs=(flat, flat, flat, deep, deep),
        check_vma=False,
    )
```

```python
import functools

import jax
import jax.numpy as jnp
from jax import lax
from jax.experimental import pallas as pl
from jax.experimental.pallas import tpu as pltpu
from jax.sharding import Mesh
from jax.sharding import PartitionSpec as P

BLOCK = 128
BF16 = jnp.bfloat16
F32 = jnp.float32
MIB = 1024 * 1024
SUB = 256
AXES = ("high", "core", "outer", "inner")
GROUP = ("outer", "high", "inner", "core")


def dot(a, b, contract_a, contract_b):
    return lax.dot_general(
        a, b, (((contract_a,), (contract_b,)), ((), ())), preferred_element_type=F32
    )


def column(row):
    count = row.shape[1]
    return jnp.transpose(jnp.broadcast_to(row, (count, count)))


def route(ids_ref, keep_ref, gates_ref, meta_ref, capacity, place_of):
    token_rows = ids_ref.shape[1]
    ids = ids_ref[...].astype(F32)
    earlier = lax.broadcasted_iota(jnp.int32, (token_rows, token_rows), 0) < lax.broadcasted_iota(
        jnp.int32, (token_rows, token_rows), 1
    )
    columns = (column(ids[0:1]), column(ids[1:2]))
    for k in range(2):
        count = jnp.zeros((token_rows, token_rows), F32)
        for other_choice in columns:
            count = count + jnp.where(earlier & (other_choice == ids[k : k + 1]), 1.0, 0.0)
        slot = jnp.sum(count, axis=0, keepdims=True).astype(jnp.int32)
        row = place_of(ids_ref[k : k + 1, :]) * capacity + slot
        meta_ref[k : k + 1, :] = jnp.where(keep_ref[k : k + 1, :] > 0, row, -1).astype(F32)
        meta_ref[k + 2 : k + 3, :] = gates_ref[k : k + 1, :]
    meta_ref[4:8, :] = jnp.zeros((4, token_rows), F32)


def hits(slot_total, meta_ref, k):
    rows = meta_ref[k : k + 1, :].astype(jnp.int32)
    index = lax.broadcasted_iota(jnp.int32, (slot_total, rows.shape[1]), 0)
    return index == rows


def one_hot(mask):
    return jnp.where(mask, 1.0, 0.0).astype(BF16)


def restore(tokens_ref):
    pieces = []
    for b in range(tokens_ref.shape[1] // BLOCK):
        x = tokens_ref[:, b * BLOCK : (b + 1) * BLOCK].astype(F32)
        scale = (jnp.max(jnp.abs(x), axis=1, keepdims=True) + 1e-06).astype(BF16).astype(F32)
        quantized = (x / scale).astype(BF16)
        pieces.append((quantized.astype(F32) * scale).astype(BF16))
    return jnp.concatenate(pieces, axis=1)


def place_tokens_kernel(capacity, place_of, tokens_ref, ids_ref, keep_ref, gates_ref, meta_ref, out_ref):
    route(ids_ref, keep_ref, gates_ref, meta_ref, capacity, place_of)
    slot_total = out_ref.shape[0]
    mask = hits(slot_total, meta_ref, 0) | hits(slot_total, meta_ref, 1)
    out_ref[...] = dot(one_hot(mask), restore(tokens_ref), 1, 0).astype(BF16)


def scaled_rows(gate_row, grad_ref):
    gate = column(gate_row)
    pieces = [
        gate * grad_ref[:, b * BLOCK : (b + 1) * BLOCK].astype(F32)
        for b in range(grad_ref.shape[1] // BLOCK)
    ]
    return jnp.concatenate(pieces, axis=1)


def place_cotangents_kernel(grad_ref, meta_ref, out_ref):
    slot_total = out_ref.shape[0]
    parts = [
        dot(
            one_hot(hits(slot_total, meta_ref, k)),
            scaled_rows(meta_ref[k + 2 : k + 3, :], grad_ref).astype(BF16),
            1,
            0,
        )
        for k in range(2)
    ]
    out_ref[...] = (parts[0] + parts[1]).astype(BF16)


def gelu_parts(v):
    c = 0.7978845608028654
    inner = c + (c * 0.044715) * (v * v)
    s = 0.5 + 0.5 * jnp.tanh(v * inner)
    hidden = v * s
    slope = s + (hidden * (1.0 - s)) * (6.0 * inner - 4.0 * c)
    return hidden.astype(BF16), slope.astype(BF16)


def forward_kernel(x_ref, w_in_ref, w_out_ref, hidden_ref, slope_ref, out_ref, total):
    step = pl.program_id(0)

    @pl.when(step == 0)
    def _():
        total[...] = jnp.zeros_like(total)

    parts = hidden_ref.shape[1] // SUB
    v = dot(x_ref[...], w_in_ref[:, :SUB], 1, 0)
    pieces = []
    for j in range(parts):
        if j + 1 < parts:
            after = dot(x_ref[...], w_in_ref[:, (j + 1) * SUB : (j + 2) * SUB], 1, 0)
        hidden, slope = gelu_parts(v)
        hidden_ref[:, j * SUB : (j + 1) * SUB] = hidden
        slope_ref[:, j * SUB : (j + 1) * SUB] = slope
        pieces.append(hidden)
        v = after
    total[...] += dot(jnp.concatenate(pieces, axis=1), w_out_ref[...], 1, 0)

    @pl.when(step == pl.num_programs(0) - 1)
    def _():
        out_ref[...] = total[...].astype(BF16)


def backward_kernel(cot_ref, w_in_ref, w_out_ref, slope_ref, grad_pre_ref, out_ref, total):
    step = pl.program_id(0)

    @pl.when(step == 0)
    def _():
        total[...] = jnp.zeros_like(total)

    parts = grad_pre_ref.shape[1] // SUB
    pieces = []
    for j in range(parts):
        grad_hidden = dot(cot_ref[...], w_out_ref[j * SUB : (j + 1) * SUB, :], 1, 1)
        slope = slope_ref[:, j * SUB : (j + 1) * SUB].astype(F32)
        grad_pre = (grad_hidden * slope).astype(BF16)
        grad_pre_ref[:, j * SUB : (j + 1) * SUB] = grad_pre
        pieces.append(grad_pre)
    total[...] += dot(jnp.concatenate(pieces, axis=1), w_in_ref[...], 1, 1)

    @pl.when(step == pl.num_programs(0) - 1)
    def _():
        out_ref[...] = total[...].astype(BF16)


def weights_kernel(x_ref, cot_ref, hidden_ref, grad_pre_ref, grad_in_ref, grad_out_ref):
    grad_in_ref[...] = dot(x_ref[...], grad_pre_ref[...], 0, 0).astype(BF16)
    grad_out_ref[...] = dot(hidden_ref[...], cot_ref[...], 0, 0).astype(BF16)


def pick_outputs_kernel(back_ref, grad_ref, meta_ref, out_ref, gates_ref):
    slot_total = back_ref.shape[0]
    total = None
    for k in range(2):
        picked = dot(one_hot(hits(slot_total, meta_ref, k)), back_ref[...], 0, 0)
        gate = column(meta_ref[k + 2 : k + 3, :])
        weighted = jnp.concatenate(
            [
                gate * picked[:, b * BLOCK : (b + 1) * BLOCK]
                for b in range(picked.shape[1] // BLOCK)
            ],
            axis=1,
        )
        total = weighted if total is None else total + weighted
        sums = jnp.sum(picked * grad_ref[...].astype(F32), axis=1, keepdims=True)
        rows = jnp.transpose(jnp.broadcast_to(sums, (sums.shape[0], sums.shape[0])))
        gates_ref[k : k + 1, :] = rows[0:1, :]
    out_ref[...] = total.astype(BF16)


def pick_gradients_kernel(back_ref, meta_ref, out_ref):
    slot_total = back_ref.shape[0]
    mask = hits(slot_total, meta_ref, 0) | hits(slot_total, meta_ref, 1)
    out_ref[...] = dot(one_hot(mask), back_ref[...], 0, 0).astype(BF16)


def call(kernel, outs, flops=0, traffic=0, limit=12, **options):
    return pl.pallas_call(
        kernel,
        out_shape=outs,
        compiler_params=pltpu.CompilerParams(vmem_limit_bytes=limit * MIB),
        cost_estimate=pl.CostEstimate(flops=flops, bytes_accessed=traffic, transcendentals=0),
        **options,
    )


def in_hbm(values):
    return pltpu.with_memory_space_constraint(values, pltpu.HBM)


def body(tokens, expert_ids, keep_mask, gate_weights, weight_in, weight_out, grad_output):
    token_rows, width = tokens.shape
    hidden_width = weight_in.shape[2]
    high, outer = lax.axis_size("high"), lax.axis_size("outer")
    experts = high * outer * 4
    high_bits, bits = high.bit_length() - 1, outer.bit_length() - 1

    def place_of(expert):
        inner_at = expert & 1
        outer_at = (expert >> 1) & (outer - 1)
        core_at = (expert >> (bits + 1)) & 1
        high_at = expert >> (bits + 2)
        return (((((outer_at << high_bits) + high_at) << 1) + inner_at) << 1) + core_at

    capacity = 2 * expert_ids.shape[1] * token_rows // experts
    slot_total = experts * capacity

    def shuffle(rows):
        shaped = rows.reshape(experts, capacity, width)
        return lax.all_to_all(
            shaped, GROUP, split_axis=0, concat_axis=0, tiled=True
        ).reshape(slot_total, width)

    slots = jax.ShapeDtypeStruct((slot_total, width), BF16)
    slot_bytes = slot_total * width * 2
    token_bytes = token_rows * width * 2
    place_flops = 2 * slot_total * token_rows * width
    meta, sent = call(
        functools.partial(place_tokens_kernel, capacity, place_of),
        [jax.ShapeDtypeStruct((8, token_rows), F32), slots],
        place_flops,
        token_bytes + slot_bytes,
    )(in_hbm(tokens), in_hbm(expert_ids.T), in_hbm(keep_mask.T), in_hbm(gate_weights.T))
    x = shuffle(sent)
    sent_cot = call(
        place_cotangents_kernel, slots, 2 * place_flops, token_bytes + slot_bytes
    )(in_hbm(grad_output), meta)
    cot = shuffle(sent_cot)

    chunk = 1024
    whole = pl.BlockSpec((slot_total, width), lambda i: (0, 0))
    in_spec = pl.BlockSpec((None, width, chunk), lambda i: (0, 0, i))
    out_spec = pl.BlockSpec((None, chunk, width), lambda i: (0, i, 0))
    mid_spec = pl.BlockSpec((slot_total, chunk), lambda i: (0, i))
    mid = pltpu.HBM((slot_total, hidden_width), BF16)
    product = 2 * slot_total * width * hidden_width
    traffic = 2 * slot_bytes + 4 * width * hidden_width + 4 * slot_total * hidden_width
    grid = (hidden_width // chunk,)
    total = pltpu.VMEM((slot_total, width), F32)
    weight_in, weight_out = in_hbm(weight_in), in_hbm(weight_out)
    hidden, slope, outputs = call(
        forward_kernel,
        [mid, mid, slots],
        2 * product,
        traffic,
        32,
        grid=grid,
        in_specs=[whole, in_spec, out_spec],
        out_specs=[mid_spec, mid_spec, whole],
        scratch_shapes=[total],
    )(x, weight_in, weight_out)
    back_out = shuffle(outputs)
    grad_pre, grad_rows = call(
        backward_kernel,
        [mid, slots],
        2 * product,
        traffic,
        32,
        grid=grid,
        in_specs=[whole, in_spec, out_spec, mid_spec],
        out_specs=[mid_spec, whole],
        scratch_shapes=[total],
    )(cot, weight_in, weight_out, in_hbm(slope))
    back_grad = shuffle(grad_rows)
    combined, grad_gates = call(
        pick_outputs_kernel,
        [
            jax.ShapeDtypeStruct((token_rows, width), BF16),
            jax.ShapeDtypeStruct((2, token_rows), F32),
        ],
        2 * place_flops,
        2 * token_bytes + slot_bytes,
    )(back_out, in_hbm(grad_output), meta)
    grad_in_w, grad_out_w = call(
        weights_kernel,
        [pltpu.HBM(weight_in.shape, BF16), pltpu.HBM(weight_out.shape, BF16)],
        2 * product,
        traffic,
        32,
        grid=grid,
        in_specs=[whole, whole, mid_spec, mid_spec],
        out_specs=[in_spec, out_spec],
    )(x, cot, in_hbm(hidden), in_hbm(grad_pre))
    grad_tokens = call(
        pick_gradients_kernel,
        jax.ShapeDtypeStruct((token_rows, width), BF16),
        place_flops,
        slot_bytes + token_bytes,
    )(back_grad, meta)
    return (combined, grad_tokens, grad_gates.T, grad_in_w, grad_out_w)


def solution(mesh):
    rows, cols = mesh.devices.shape
    split = Mesh(mesh.devices.reshape(rows // 2, 2, cols // 2, 2), AXES)
    flat, deep = P(AXES, None), P(AXES, None, None)
    return jax.shard_map(
        body,
        mesh=split,
        in_specs=(flat, flat, flat, flat, deep, deep, flat),
        out_specs=(flat, flat, flat, deep, deep),
        check_vma=False,
    )
```

```python
import functools

import jax
import jax.numpy as jnp
from jax import lax
from jax.experimental import pallas as pl
from jax.experimental.pallas import tpu as pltpu
from jax.sharding import Mesh
from jax.sharding import PartitionSpec as P

BLOCK = 128
BF16 = jnp.bfloat16
F32 = jnp.float32
MIB = 1024 * 1024
SUB = 256
AXES = ("high", "core", "outer", "inner")
GROUP = ("outer", "core", "high", "inner")


def dot(a, b, contract_a, contract_b):
    return lax.dot_general(
        a, b, (((contract_a,), (contract_b,)), ((), ())), preferred_element_type=F32
    )


def column(row):
    count = row.shape[1]
    return jnp.transpose(jnp.broadcast_to(row, (count, count)))


def route(ids_ref, keep_ref, gates_ref, meta_ref, capacity, place_of):
    token_rows = ids_ref.shape[1]
    ids = ids_ref[...].astype(F32)
    earlier = lax.broadcasted_iota(jnp.int32, (token_rows, token_rows), 0) < lax.broadcasted_iota(
        jnp.int32, (token_rows, token_rows), 1
    )
    columns = (column(ids[0:1]), column(ids[1:2]))
    for k in range(2):
        count = jnp.zeros((token_rows, token_rows), F32)
        for other_choice in columns:
            count = count + jnp.where(earlier & (other_choice == ids[k : k + 1]), 1.0, 0.0)
        slot = jnp.sum(count, axis=0, keepdims=True).astype(jnp.int32)
        row = place_of(ids_ref[k : k + 1, :]) * capacity + slot
        meta_ref[k : k + 1, :] = jnp.where(keep_ref[k : k + 1, :] > 0, row, -1).astype(F32)
        meta_ref[k + 2 : k + 3, :] = gates_ref[k : k + 1, :]
    meta_ref[4:8, :] = jnp.zeros((4, token_rows), F32)


def hits(slot_total, meta_ref, k):
    rows = meta_ref[k : k + 1, :].astype(jnp.int32)
    index = lax.broadcasted_iota(jnp.int32, (slot_total, rows.shape[1]), 0)
    return index == rows


def one_hot(mask):
    return jnp.where(mask, 1.0, 0.0).astype(BF16)


def restore(tokens_ref):
    pieces = []
    for b in range(tokens_ref.shape[1] // BLOCK):
        x = tokens_ref[:, b * BLOCK : (b + 1) * BLOCK].astype(F32)
        scale = (jnp.max(jnp.abs(x), axis=1, keepdims=True) + 1e-06).astype(BF16).astype(F32)
        quantized = (x / scale).astype(BF16)
        pieces.append((quantized.astype(F32) * scale).astype(BF16))
    return jnp.concatenate(pieces, axis=1)


def place_tokens_kernel(capacity, place_of, tokens_ref, ids_ref, keep_ref, gates_ref, meta_ref, out_ref):
    route(ids_ref, keep_ref, gates_ref, meta_ref, capacity, place_of)
    slot_total = out_ref.shape[0]
    mask = hits(slot_total, meta_ref, 0) | hits(slot_total, meta_ref, 1)
    out_ref[...] = dot(one_hot(mask), restore(tokens_ref), 1, 0).astype(BF16)


def scaled_rows(gate_row, grad_ref):
    gate = column(gate_row)
    pieces = [
        gate * grad_ref[:, b * BLOCK : (b + 1) * BLOCK].astype(F32)
        for b in range(grad_ref.shape[1] // BLOCK)
    ]
    return jnp.concatenate(pieces, axis=1)


def place_cotangents_kernel(grad_ref, meta_ref, out_ref):
    slot_total = out_ref.shape[0]
    parts = [
        dot(
            one_hot(hits(slot_total, meta_ref, k)),
            scaled_rows(meta_ref[k + 2 : k + 3, :], grad_ref).astype(BF16),
            1,
            0,
        )
        for k in range(2)
    ]
    out_ref[...] = (parts[0] + parts[1]).astype(BF16)


def gelu_parts(v):
    c = 0.7978845608028654
    inner = c + (c * 0.044715) * (v * v)
    s = 0.5 + 0.5 * jnp.tanh(v * inner)
    hidden = v * s
    slope = s + (hidden * (1.0 - s)) * (6.0 * inner - 4.0 * c)
    return hidden.astype(BF16), slope.astype(BF16)


def forward_kernel(x_ref, w_in_ref, w_out_ref, hidden_ref, slope_ref, out_ref, total):
    step = pl.program_id(0)

    @pl.when(step == 0)
    def _():
        total[...] = jnp.zeros_like(total)

    parts = hidden_ref.shape[1] // SUB
    v = dot(x_ref[...], w_in_ref[:, :SUB], 1, 0)
    pieces = []
    for j in range(parts):
        if j + 1 < parts:
            after = dot(x_ref[...], w_in_ref[:, (j + 1) * SUB : (j + 2) * SUB], 1, 0)
        hidden, slope = gelu_parts(v)
        hidden_ref[:, j * SUB : (j + 1) * SUB] = hidden
        slope_ref[:, j * SUB : (j + 1) * SUB] = slope
        pieces.append(hidden)
        v = after
    total[...] += dot(jnp.concatenate(pieces, axis=1), w_out_ref[...], 1, 0)

    @pl.when(step == pl.num_programs(0) - 1)
    def _():
        out_ref[...] = total[...].astype(BF16)


def backward_kernel(cot_ref, w_in_ref, w_out_ref, slope_ref, grad_pre_ref, out_ref, total):
    step = pl.program_id(0)

    @pl.when(step == 0)
    def _():
        total[...] = jnp.zeros_like(total)

    parts = grad_pre_ref.shape[1] // SUB
    pieces = []
    for j in range(parts):
        grad_hidden = dot(cot_ref[...], w_out_ref[j * SUB : (j + 1) * SUB, :], 1, 1)
        slope = slope_ref[:, j * SUB : (j + 1) * SUB].astype(F32)
        grad_pre = (grad_hidden * slope).astype(BF16)
        grad_pre_ref[:, j * SUB : (j + 1) * SUB] = grad_pre
        pieces.append(grad_pre)
    total[...] += dot(jnp.concatenate(pieces, axis=1), w_in_ref[...], 1, 1)

    @pl.when(step == pl.num_programs(0) - 1)
    def _():
        out_ref[...] = total[...].astype(BF16)


def weights_kernel(x_ref, cot_ref, hidden_ref, grad_pre_ref, grad_in_ref, grad_out_ref):
    grad_in_ref[...] = dot(x_ref[...], grad_pre_ref[...], 0, 0).astype(BF16)
    grad_out_ref[...] = dot(hidden_ref[...], cot_ref[...], 0, 0).astype(BF16)


def pick_outputs_kernel(back_ref, grad_ref, meta_ref, out_ref, gates_ref):
    slot_total = back_ref.shape[0]
    total = None
    for k in range(2):
        picked = dot(one_hot(hits(slot_total, meta_ref, k)), back_ref[...], 0, 0)
        gate = column(meta_ref[k + 2 : k + 3, :])
        weighted = jnp.concatenate(
            [
                gate * picked[:, b * BLOCK : (b + 1) * BLOCK]
                for b in range(picked.shape[1] // BLOCK)
            ],
            axis=1,
        )
        total = weighted if total is None else total + weighted
        sums = jnp.sum(picked * grad_ref[...].astype(F32), axis=1, keepdims=True)
        rows = jnp.transpose(jnp.broadcast_to(sums, (sums.shape[0], sums.shape[0])))
        gates_ref[k : k + 1, :] = rows[0:1, :]
    out_ref[...] = total.astype(BF16)


def pick_gradients_kernel(back_ref, meta_ref, out_ref):
    slot_total = back_ref.shape[0]
    mask = hits(slot_total, meta_ref, 0) | hits(slot_total, meta_ref, 1)
    out_ref[...] = dot(one_hot(mask), back_ref[...], 0, 0).astype(BF16)


def call(kernel, outs, flops=0, traffic=0, limit=12, **options):
    return pl.pallas_call(
        kernel,
        out_shape=outs,
        compiler_params=pltpu.CompilerParams(vmem_limit_bytes=limit * MIB),
        cost_estimate=pl.CostEstimate(flops=flops, bytes_accessed=traffic, transcendentals=0),
        **options,
    )


def in_hbm(values):
    return pltpu.with_memory_space_constraint(values, pltpu.HBM)


def body(tokens, expert_ids, keep_mask, gate_weights, weight_in, weight_out, grad_output):
    token_rows, width = tokens.shape
    hidden_width = weight_in.shape[2]
    high, outer = lax.axis_size("high"), lax.axis_size("outer")
    experts = high * outer * 4
    high_bits, bits = high.bit_length() - 1, outer.bit_length() - 1

    def place_of(expert):
        inner_at = expert & 1
        outer_at = (expert >> 1) & (outer - 1)
        core_at = (expert >> (bits + 1)) & 1
        high_at = expert >> (bits + 2)
        return (((((outer_at << 1) + core_at) << high_bits) + high_at) << 1) + inner_at

    capacity = 2 * expert_ids.shape[1] * token_rows // experts
    slot_total = experts * capacity

    def shuffle(rows):
        shaped = rows.reshape(experts, capacity, width)
        return lax.all_to_all(
            shaped, GROUP, split_axis=0, concat_axis=0, tiled=True
        ).reshape(slot_total, width)

    slots = jax.ShapeDtypeStruct((slot_total, width), BF16)
    slot_bytes = slot_total * width * 2
    token_bytes = token_rows * width * 2
    place_flops = 2 * slot_total * token_rows * width
    meta, sent = call(
        functools.partial(place_tokens_kernel, capacity, place_of),
        [jax.ShapeDtypeStruct((8, token_rows), F32), slots],
        place_flops,
        token_bytes + slot_bytes,
    )(in_hbm(tokens), in_hbm(expert_ids.T), in_hbm(keep_mask.T), in_hbm(gate_weights.T))
    x = shuffle(sent)
    sent_cot = call(
        place_cotangents_kernel, slots, 2 * place_flops, token_bytes + slot_bytes
    )(in_hbm(grad_output), meta)
    cot = shuffle(sent_cot)

    chunk = 1024
    whole = pl.BlockSpec((slot_total, width), lambda i: (0, 0))
    in_spec = pl.BlockSpec((None, width, chunk), lambda i: (0, 0, i))
    out_spec = pl.BlockSpec((None, chunk, width), lambda i: (0, i, 0))
    mid_spec = pl.BlockSpec((slot_total, chunk), lambda i: (0, i))
    mid = pltpu.HBM((slot_total, hidden_width), BF16)
    product = 2 * slot_total * width * hidden_width
    traffic = 2 * slot_bytes + 4 * width * hidden_width + 4 * slot_total * hidden_width
    grid = (hidden_width // chunk,)
    total = pltpu.VMEM((slot_total, width), F32)
    weight_in, weight_out = in_hbm(weight_in), in_hbm(weight_out)
    hidden, slope, outputs = call(
        forward_kernel,
        [mid, mid, slots],
        2 * product,
        traffic,
        32,
        grid=grid,
        in_specs=[whole, in_spec, out_spec],
        out_specs=[mid_spec, mid_spec, whole],
        scratch_shapes=[total],
    )(x, weight_in, weight_out)
    back_out = shuffle(outputs)
    grad_pre, grad_rows = call(
        backward_kernel,
        [mid, slots],
        2 * product,
        traffic,
        32,
        grid=grid,
        in_specs=[whole, in_spec, out_spec, mid_spec],
        out_specs=[mid_spec, whole],
        scratch_shapes=[total],
    )(cot, weight_in, weight_out, in_hbm(slope))
    back_grad = shuffle(grad_rows)
    combined, grad_gates = call(
        pick_outputs_kernel,
        [
            jax.ShapeDtypeStruct((token_rows, width), BF16),
            jax.ShapeDtypeStruct((2, token_rows), F32),
        ],
        2 * place_flops,
        2 * token_bytes + slot_bytes,
    )(back_out, in_hbm(grad_output), meta)
    grad_in_w, grad_out_w = call(
        weights_kernel,
        [pltpu.HBM(weight_in.shape, BF16), pltpu.HBM(weight_out.shape, BF16)],
        2 * product,
        traffic,
        32,
        grid=grid,
        in_specs=[whole, whole, mid_spec, mid_spec],
        out_specs=[in_spec, out_spec],
    )(x, cot, in_hbm(hidden), in_hbm(grad_pre))
    grad_tokens = call(
        pick_gradients_kernel,
        jax.ShapeDtypeStruct((token_rows, width), BF16),
        place_flops,
        slot_bytes + token_bytes,
    )(back_grad, meta)
    return (combined, grad_tokens, grad_gates.T, grad_in_w, grad_out_w)


def solution(mesh):
    rows, cols = mesh.devices.shape
    split = Mesh(mesh.devices.reshape(rows // 2, 2, cols // 2, 2), AXES)
    flat, deep = P(AXES, None), P(AXES, None, None)
    return jax.shard_map(
        body,
        mesh=split,
        in_specs=(flat, flat, flat, flat, deep, deep, flat),
        out_specs=(flat, flat, flat, deep, deep),
        check_vma=False,
    )
```

```python
import functools

import jax
import jax.numpy as jnp
from jax import lax
from jax.experimental import pallas as pl
from jax.experimental.pallas import tpu as pltpu
from jax.sharding import Mesh
from jax.sharding import PartitionSpec as P

BLOCK = 128
BF16 = jnp.bfloat16
F32 = jnp.float32
MIB = 1024 * 1024
SUB = 256
AXES = ("row", "half", "rest")
ALL = ("row", "rest", "half")
GROUP = ("row", "rest")


def dot(a, b, contract_a, contract_b):
    return lax.dot_general(
        a, b, (((contract_a,), (contract_b,)), ((), ())), preferred_element_type=F32
    )


def column(row):
    count = row.shape[1]
    return jnp.transpose(jnp.broadcast_to(row, (count, count)))


def route(rest_bits, capacity, half, ids_ref, keep_ref, gates_ref, mine_ref, other_ref):
    token_rows = ids_ref.shape[1]
    ids = ids_ref[...].astype(F32)
    earlier = lax.broadcasted_iota(jnp.int32, (token_rows, token_rows), 0) < lax.broadcasted_iota(
        jnp.int32, (token_rows, token_rows), 1
    )
    columns = (column(ids[0:1]), column(ids[1:2]))
    for k in range(2):
        count = jnp.zeros((token_rows, token_rows), F32)
        for other_choice in columns:
            count = count + jnp.where(earlier & (other_choice == ids[k : k + 1]), 1.0, 0.0)
        slot = jnp.sum(count, axis=0, keepdims=True).astype(jnp.int32)
        expert = ids_ref[k : k + 1, :]
        kept = keep_ref[k : k + 1, :] > 0
        side = (expert >> rest_bits) & 1
        local = ((expert >> (rest_bits + 1)) << rest_bits) + (expert & ((1 << rest_bits) - 1))
        base = local * (2 * capacity) + slot
        row = base + half * capacity
        mine_ref[k : k + 1, :] = jnp.where(kept & (side == half), row, -1).astype(F32)
        other_ref[k : k + 1, :] = jnp.where(kept & (side != half), row, -1).astype(F32)
        mine_ref[k + 4 : k + 5, :] = jnp.where(kept, base + side * capacity, -1).astype(F32)
        for ref in (mine_ref, other_ref):
            ref[k + 2 : k + 3, :] = gates_ref[k : k + 1, :]
    mine_ref[6:8, :] = jnp.zeros((2, token_rows), F32)
    other_ref[4:8, :] = jnp.zeros((4, token_rows), F32)


def hits(slot_total, meta_ref, k):
    rows = meta_ref[k : k + 1, :].astype(jnp.int32)
    index = lax.broadcasted_iota(jnp.int32, (slot_total, rows.shape[1]), 0)
    return index == rows


def one_hot(mask):
    return jnp.where(mask, 1.0, 0.0).astype(BF16)


def restore(tokens_ref):
    pieces = []
    for b in range(tokens_ref.shape[1] // BLOCK):
        x = tokens_ref[:, b * BLOCK : (b + 1) * BLOCK].astype(F32)
        scale = (jnp.max(jnp.abs(x), axis=1, keepdims=True) + 1e-06).astype(BF16).astype(F32)
        quantized = (x / scale).astype(BF16)
        pieces.append((quantized.astype(F32) * scale).astype(BF16))
    return jnp.concatenate(pieces, axis=1)


def place_tokens_kernel(
    rest_bits, capacity, half_ref, tokens_ref, ids_ref, keep_ref, gates_ref, mine_ref, other_ref, out_ref
):
    route(rest_bits, capacity, half_ref[0], ids_ref, keep_ref, gates_ref, mine_ref, other_ref)
    slot_total = out_ref.shape[0]
    mask = hits(slot_total, mine_ref, 4) | hits(slot_total, mine_ref, 5)
    out_ref[...] = dot(one_hot(mask), restore(tokens_ref), 1, 0).astype(BF16)


def scaled_rows(gate_row, grad_ref):
    gate = column(gate_row)
    pieces = [
        gate * grad_ref[:, b * BLOCK : (b + 1) * BLOCK].astype(F32)
        for b in range(grad_ref.shape[1] // BLOCK)
    ]
    return jnp.concatenate(pieces, axis=1)


def place_cotangents_kernel(own_grad, partner_grad, own_meta, partner_meta, out_ref):
    slot_total = out_ref.shape[0]
    total = None
    for grad_ref, meta_ref in ((own_grad, own_meta), (partner_grad, partner_meta)):
        for k in range(2):
            rows = scaled_rows(meta_ref[k + 2 : k + 3, :], grad_ref).astype(BF16)
            part = dot(one_hot(hits(slot_total, meta_ref, k)), rows, 1, 0)
            total = part if total is None else total + part
    out_ref[...] = total.astype(BF16)


def gelu_parts(v):
    c = 0.7978845608028654
    inner = c + (c * 0.044715) * (v * v)
    s = 0.5 + 0.5 * jnp.tanh(v * inner)
    hidden = v * s
    slope = s + (hidden * (1.0 - s)) * (6.0 * inner - 4.0 * c)
    return hidden.astype(BF16), slope.astype(BF16)


def forward_kernel(x_ref, w_in_ref, w_out_ref, hidden_ref, slope_ref, out_ref, total):
    step = pl.program_id(0)

    @pl.when(step == 0)
    def _():
        total[...] = jnp.zeros_like(total)

    parts = hidden_ref.shape[1] // SUB
    v = dot(x_ref[...], w_in_ref[:, :SUB], 1, 0)
    pieces = []
    for j in range(parts):
        if j + 1 < parts:
            after = dot(x_ref[...], w_in_ref[:, (j + 1) * SUB : (j + 2) * SUB], 1, 0)
        hidden, slope = gelu_parts(v)
        hidden_ref[:, j * SUB : (j + 1) * SUB] = hidden
        slope_ref[:, j * SUB : (j + 1) * SUB] = slope
        pieces.append(hidden)
        v = after
    total[...] += dot(jnp.concatenate(pieces, axis=1), w_out_ref[...], 1, 0)

    @pl.when(step == pl.num_programs(0) - 1)
    def _():
        out_ref[...] = total[...].astype(BF16)


def backward_kernel(cot_ref, w_in_ref, w_out_ref, slope_ref, grad_pre_ref, out_ref, total):
    step = pl.program_id(0)

    @pl.when(step == 0)
    def _():
        total[...] = jnp.zeros_like(total)

    parts = grad_pre_ref.shape[1] // SUB
    pieces = []
    for j in range(parts):
        grad_hidden = dot(cot_ref[...], w_out_ref[j * SUB : (j + 1) * SUB, :], 1, 1)
        slope = slope_ref[:, j * SUB : (j + 1) * SUB].astype(F32)
        grad_pre = (grad_hidden * slope).astype(BF16)
        grad_pre_ref[:, j * SUB : (j + 1) * SUB] = grad_pre
        pieces.append(grad_pre)
    total[...] += dot(jnp.concatenate(pieces, axis=1), w_in_ref[...], 1, 1)

    @pl.when(step == pl.num_programs(0) - 1)
    def _():
        out_ref[...] = total[...].astype(BF16)


def weights_kernel(x_ref, cot_ref, hidden_ref, grad_pre_ref, grad_in_ref, grad_out_ref):
    grad_in_ref[...] = dot(x_ref[...], grad_pre_ref[...], 0, 0).astype(BF16)
    grad_out_ref[...] = dot(hidden_ref[...], cot_ref[...], 0, 0).astype(BF16)


def pick_outputs_kernel(
    back_ref, own_grad, partner_grad, own_meta, partner_meta, own_out, partner_out, own_gates, partner_gates
):
    slot_total = back_ref.shape[0]
    for grad_ref, meta_ref, out_ref, gates_ref in (
        (own_grad, own_meta, own_out, own_gates),
        (partner_grad, partner_meta, partner_out, partner_gates),
    ):
        total = None
        for k in range(2):
            picked = dot(one_hot(hits(slot_total, meta_ref, k)), back_ref[...], 0, 0)
            gate = column(meta_ref[k + 2 : k + 3, :])
            weighted = jnp.concatenate(
                [
                    gate * picked[:, b * BLOCK : (b + 1) * BLOCK]
                    for b in range(picked.shape[1] // BLOCK)
                ],
                axis=1,
            )
            total = weighted if total is None else total + weighted
            sums = jnp.sum(picked * grad_ref[...].astype(F32), axis=1, keepdims=True)
            rows = jnp.transpose(jnp.broadcast_to(sums, (sums.shape[0], sums.shape[0])))
            gates_ref[k : k + 1, :] = rows[0:1, :]
        out_ref[...] = total.astype(out_ref.dtype)


def finish_outputs_kernel(own_out, got_out, own_gates, got_gates, combined, grad_gates):
    combined[...] = (own_out[...] + got_out[...].astype(F32)).astype(BF16)
    grad_gates[...] = own_gates[...] + got_gates[...]


def pick_gradients_kernel(back_ref, meta_ref, out_ref):
    slot_total = back_ref.shape[0]
    mask = hits(slot_total, meta_ref, 4) | hits(slot_total, meta_ref, 5)
    out_ref[...] = dot(one_hot(mask), back_ref[...], 0, 0).astype(BF16)


def call(kernel, outs, flops=0, traffic=0, limit=12, **options):
    return pl.pallas_call(
        kernel,
        out_shape=outs,
        compiler_params=pltpu.CompilerParams(vmem_limit_bytes=limit * MIB),
        cost_estimate=pl.CostEstimate(flops=flops, bytes_accessed=traffic, transcendentals=0),
        **options,
    )


def in_hbm(values):
    return pltpu.with_memory_space_constraint(values, pltpu.HBM)


def body(tokens, expert_ids, keep_mask, gate_weights, weight_in, weight_out, grad_output):
    token_rows, width = tokens.shape
    hidden_width = weight_in.shape[2]
    rest_count = lax.axis_size("rest")
    members = lax.axis_size("row") * rest_count
    capacity = expert_ids.shape[1] * token_rows // members
    slot_total = 2 * members * capacity

    def exchange(values):
        return lax.ppermute(values, "half", ((0, 1), (1, 0)))

    def shuffle(rows, group, peers):
        shaped = rows.reshape(peers, slot_total // peers, width)
        return lax.all_to_all(shaped, group, split_axis=0, concat_axis=0, tiled=True).reshape(
            rows.shape
        )

    def shape(*dims, dtype=BF16):
        return jax.ShapeDtypeStruct(dims, dtype)

    vmem = pl.BlockSpec(memory_space=pltpu.VMEM)
    meta_shape = shape(8, token_rows, dtype=F32)
    slots, token_shape = shape(slot_total, width), shape(token_rows, width)
    slot_bytes, token_bytes = slot_total * width * 2, token_rows * width * 2
    place_flops = 2 * slot_total * token_rows * width

    partner_grad = exchange(grad_output)
    half = lax.axis_index("half").astype(jnp.int32).reshape(1)
    own_meta, sent_meta, sent = call(
        functools.partial(place_tokens_kernel, rest_count.bit_length() - 1, capacity),
        [meta_shape, meta_shape, slots],
        place_flops,
        token_bytes + slot_bytes,
        in_specs=[pl.BlockSpec(memory_space=pltpu.SMEM)] + [vmem] * 4,
    )(
        half,
        in_hbm(tokens),
        in_hbm(expert_ids.T),
        in_hbm(keep_mask.T),
        in_hbm(gate_weights.T),
    )
    x = shuffle(sent, ALL, 2 * members)
    partner_meta = exchange(sent_meta)
    sent_cot = call(
        place_cotangents_kernel, slots, 4 * place_flops, 2 * token_bytes + slot_bytes
    )(in_hbm(grad_output), partner_grad, own_meta, partner_meta)
    cot = shuffle(sent_cot, GROUP, members)

    chunk = 1024
    whole = pl.BlockSpec((slot_total, width), lambda i: (0, 0))
    in_spec = pl.BlockSpec((None, width, chunk), lambda i: (0, 0, i))
    out_spec = pl.BlockSpec((None, chunk, width), lambda i: (0, i, 0))
    mid_spec = pl.BlockSpec((slot_total, chunk), lambda i: (0, i))
    mid = pltpu.HBM((slot_total, hidden_width), BF16)
    product = 2 * slot_total * width * hidden_width
    traffic = 2 * slot_bytes + 4 * width * hidden_width + 4 * slot_total * hidden_width
    grid = (hidden_width // chunk,)
    total = pltpu.VMEM((slot_total, width), F32)
    weight_in, weight_out = in_hbm(weight_in), in_hbm(weight_out)
    hidden, slope, outputs = call(
        forward_kernel,
        [mid, mid, slots],
        2 * product,
        traffic,
        32,
        grid=grid,
        in_specs=[whole, in_spec, out_spec],
        out_specs=[mid_spec, mid_spec, whole],
        scratch_shapes=[total],
    )(x, weight_in, weight_out)
    back_out = shuffle(outputs, GROUP, members)
    grad_pre, grad_rows = call(
        backward_kernel,
        [mid, slots],
        2 * product,
        traffic,
        32,
        grid=grid,
        in_specs=[whole, in_spec, out_spec, mid_spec],
        out_specs=[mid_spec, whole],
        scratch_shapes=[total],
    )(cot, weight_in, weight_out, in_hbm(slope))
    back_grad = shuffle(grad_rows, ALL, 2 * members)
    tokens_f32, gates_shape = shape(token_rows, width, dtype=F32), shape(2, token_rows, dtype=F32)
    own_out, partner_out, own_gates, partner_gates = call(
        pick_outputs_kernel,
        [tokens_f32, token_shape, gates_shape, gates_shape],
        4 * place_flops,
        4 * token_bytes + slot_bytes,
    )(back_out, in_hbm(grad_output), partner_grad, own_meta, partner_meta)
    grad_pre, partner_out = lax.optimization_barrier((grad_pre, partner_out))
    got_out, got_gates = exchange(partner_out), exchange(partner_gates)
    grad_in_w, grad_out_w = call(
        weights_kernel,
        [pltpu.HBM(weight_in.shape, BF16), pltpu.HBM(weight_out.shape, BF16)],
        2 * product,
        traffic,
        32,
        grid=grid,
        in_specs=[whole, whole, mid_spec, mid_spec],
        out_specs=[in_spec, out_spec],
    )(x, cot, in_hbm(hidden), in_hbm(grad_pre))
    combined, grad_gates = call(
        finish_outputs_kernel, [token_shape, gates_shape], 0, 6 * token_bytes
    )(own_out, got_out, own_gates, got_gates)
    grad_tokens = call(
        pick_gradients_kernel, token_shape, place_flops, slot_bytes + token_bytes
    )(back_grad, own_meta)
    return (combined, grad_tokens, grad_gates.T, grad_in_w, grad_out_w)


def solution(mesh):
    rows, cols = mesh.devices.shape
    halves = Mesh(mesh.devices.reshape(rows // 2, 2, cols), AXES)
    flat, deep = P(AXES, None), P(AXES, None, None)
    return jax.shard_map(
        body,
        mesh=halves,
        in_specs=(flat, flat, flat, flat, deep, deep, flat),
        out_specs=(flat, flat, flat, deep, deep),
        check_vma=False,
    )
```

```python
import functools

import jax
import jax.numpy as jnp
from jax import lax
from jax.experimental import pallas as pl
from jax.experimental.pallas import tpu as pltpu
from jax.sharding import Mesh
from jax.sharding import PartitionSpec as P

BLOCK = 128
BF16 = jnp.bfloat16
F32 = jnp.float32
MIB = 1024 * 1024
SUB = 256
AXES = ("row", "half", "outer", "inner")
ALL = ("row", "inner", "outer", "half")
GROUP = ("row", "inner", "outer")


def dot(a, b, contract_a, contract_b):
    return lax.dot_general(
        a, b, (((contract_a,), (contract_b,)), ((), ())), preferred_element_type=F32
    )


def column(row):
    count = row.shape[1]
    return jnp.transpose(jnp.broadcast_to(row, (count, count)))


def route(rest_bits, capacity, half, ids_ref, keep_ref, gates_ref, mine_ref, other_ref):
    token_rows = ids_ref.shape[1]
    ids = ids_ref[...].astype(F32)
    earlier = lax.broadcasted_iota(jnp.int32, (token_rows, token_rows), 0) < lax.broadcasted_iota(
        jnp.int32, (token_rows, token_rows), 1
    )
    columns = (column(ids[0:1]), column(ids[1:2]))
    for k in range(2):
        count = jnp.zeros((token_rows, token_rows), F32)
        for other_choice in columns:
            count = count + jnp.where(earlier & (other_choice == ids[k : k + 1]), 1.0, 0.0)
        slot = jnp.sum(count, axis=0, keepdims=True).astype(jnp.int32)
        expert = ids_ref[k : k + 1, :]
        kept = keep_ref[k : k + 1, :] > 0
        side = (expert >> rest_bits) & 1
        inner_at = expert & 1
        outer_at = (expert >> 1) & ((1 << (rest_bits - 1)) - 1)
        row_at = expert >> (rest_bits + 1)
        local = (((row_at << 1) + inner_at) << (rest_bits - 1)) + outer_at
        base = local * (2 * capacity) + slot
        row = base + half * capacity
        mine_ref[k : k + 1, :] = jnp.where(kept & (side == half), row, -1).astype(F32)
        other_ref[k : k + 1, :] = jnp.where(kept & (side != half), row, -1).astype(F32)
        mine_ref[k + 4 : k + 5, :] = jnp.where(kept, base + side * capacity, -1).astype(F32)
        for ref in (mine_ref, other_ref):
            ref[k + 2 : k + 3, :] = gates_ref[k : k + 1, :]
    mine_ref[6:8, :] = jnp.zeros((2, token_rows), F32)
    other_ref[4:8, :] = jnp.zeros((4, token_rows), F32)


def hits(slot_total, meta_ref, k):
    rows = meta_ref[k : k + 1, :].astype(jnp.int32)
    index = lax.broadcasted_iota(jnp.int32, (slot_total, rows.shape[1]), 0)
    return index == rows


def one_hot(mask):
    return jnp.where(mask, 1.0, 0.0).astype(BF16)


def restore(tokens_ref):
    pieces = []
    for b in range(tokens_ref.shape[1] // BLOCK):
        x = tokens_ref[:, b * BLOCK : (b + 1) * BLOCK].astype(F32)
        scale = (jnp.max(jnp.abs(x), axis=1, keepdims=True) + 1e-06).astype(BF16).astype(F32)
        quantized = (x / scale).astype(BF16)
        pieces.append((quantized.astype(F32) * scale).astype(BF16))
    return jnp.concatenate(pieces, axis=1)


def place_tokens_kernel(
    rest_bits, capacity, half_ref, tokens_ref, ids_ref, keep_ref, gates_ref, mine_ref, other_ref, out_ref
):
    route(rest_bits, capacity, half_ref[0], ids_ref, keep_ref, gates_ref, mine_ref, other_ref)
    slot_total = out_ref.shape[0]
    mask = hits(slot_total, mine_ref, 4) | hits(slot_total, mine_ref, 5)
    out_ref[...] = dot(one_hot(mask), restore(tokens_ref), 1, 0).astype(BF16)


def scaled_rows(gate_row, grad_ref):
    gate = column(gate_row)
    pieces = [
        gate * grad_ref[:, b * BLOCK : (b + 1) * BLOCK].astype(F32)
        for b in range(grad_ref.shape[1] // BLOCK)
    ]
    return jnp.concatenate(pieces, axis=1)


def place_cotangents_kernel(own_grad, partner_grad, own_meta, partner_meta, out_ref):
    slot_total = out_ref.shape[0]
    total = None
    for grad_ref, meta_ref in ((own_grad, own_meta), (partner_grad, partner_meta)):
        for k in range(2):
            rows = scaled_rows(meta_ref[k + 2 : k + 3, :], grad_ref).astype(BF16)
            part = dot(one_hot(hits(slot_total, meta_ref, k)), rows, 1, 0)
            total = part if total is None else total + part
    out_ref[...] = total.astype(BF16)


def gelu_parts(v):
    c = 0.7978845608028654
    inner = c + (c * 0.044715) * (v * v)
    s = 0.5 + 0.5 * jnp.tanh(v * inner)
    hidden = v * s
    slope = s + (hidden * (1.0 - s)) * (6.0 * inner - 4.0 * c)
    return hidden.astype(BF16), slope.astype(BF16)


def forward_kernel(x_ref, w_in_ref, w_out_ref, hidden_ref, slope_ref, out_ref, total):
    step = pl.program_id(0)

    @pl.when(step == 0)
    def _():
        total[...] = jnp.zeros_like(total)

    parts = hidden_ref.shape[1] // SUB
    v = dot(x_ref[...], w_in_ref[:, :SUB], 1, 0)
    pieces = []
    for j in range(parts):
        if j + 1 < parts:
            after = dot(x_ref[...], w_in_ref[:, (j + 1) * SUB : (j + 2) * SUB], 1, 0)
        hidden, slope = gelu_parts(v)
        hidden_ref[:, j * SUB : (j + 1) * SUB] = hidden
        slope_ref[:, j * SUB : (j + 1) * SUB] = slope
        pieces.append(hidden)
        v = after
    total[...] += dot(jnp.concatenate(pieces, axis=1), w_out_ref[...], 1, 0)

    @pl.when(step == pl.num_programs(0) - 1)
    def _():
        out_ref[...] = total[...].astype(BF16)


def backward_kernel(cot_ref, w_in_ref, w_out_ref, slope_ref, grad_pre_ref, out_ref, total):
    step = pl.program_id(0)

    @pl.when(step == 0)
    def _():
        total[...] = jnp.zeros_like(total)

    parts = grad_pre_ref.shape[1] // SUB
    pieces = []
    for j in range(parts):
        grad_hidden = dot(cot_ref[...], w_out_ref[j * SUB : (j + 1) * SUB, :], 1, 1)
        slope = slope_ref[:, j * SUB : (j + 1) * SUB].astype(F32)
        grad_pre = (grad_hidden * slope).astype(BF16)
        grad_pre_ref[:, j * SUB : (j + 1) * SUB] = grad_pre
        pieces.append(grad_pre)
    total[...] += dot(jnp.concatenate(pieces, axis=1), w_in_ref[...], 1, 1)

    @pl.when(step == pl.num_programs(0) - 1)
    def _():
        out_ref[...] = total[...].astype(BF16)


def weights_kernel(x_ref, cot_ref, hidden_ref, grad_pre_ref, grad_in_ref, grad_out_ref):
    grad_in_ref[...] = dot(x_ref[...], grad_pre_ref[...], 0, 0).astype(BF16)
    grad_out_ref[...] = dot(hidden_ref[...], cot_ref[...], 0, 0).astype(BF16)


def pick_outputs_kernel(
    back_ref, own_grad, partner_grad, own_meta, partner_meta, own_out, partner_out, own_gates, partner_gates
):
    slot_total = back_ref.shape[0]
    for grad_ref, meta_ref, out_ref, gates_ref in (
        (own_grad, own_meta, own_out, own_gates),
        (partner_grad, partner_meta, partner_out, partner_gates),
    ):
        total = None
        for k in range(2):
            picked = dot(one_hot(hits(slot_total, meta_ref, k)), back_ref[...], 0, 0)
            gate = column(meta_ref[k + 2 : k + 3, :])
            weighted = jnp.concatenate(
                [
                    gate * picked[:, b * BLOCK : (b + 1) * BLOCK]
                    for b in range(picked.shape[1] // BLOCK)
                ],
                axis=1,
            )
            total = weighted if total is None else total + weighted
            sums = jnp.sum(picked * grad_ref[...].astype(F32), axis=1, keepdims=True)
            rows = jnp.transpose(jnp.broadcast_to(sums, (sums.shape[0], sums.shape[0])))
            gates_ref[k : k + 1, :] = rows[0:1, :]
        out_ref[...] = total.astype(out_ref.dtype)


def finish_outputs_kernel(own_out, got_out, own_gates, got_gates, combined, grad_gates):
    combined[...] = (own_out[...] + got_out[...].astype(F32)).astype(BF16)
    grad_gates[...] = own_gates[...] + got_gates[...]


def pick_gradients_kernel(back_ref, meta_ref, out_ref):
    slot_total = back_ref.shape[0]
    mask = hits(slot_total, meta_ref, 4) | hits(slot_total, meta_ref, 5)
    out_ref[...] = dot(one_hot(mask), back_ref[...], 0, 0).astype(BF16)


def call(kernel, outs, flops=0, traffic=0, limit=12, **options):
    return pl.pallas_call(
        kernel,
        out_shape=outs,
        compiler_params=pltpu.CompilerParams(vmem_limit_bytes=limit * MIB),
        cost_estimate=pl.CostEstimate(flops=flops, bytes_accessed=traffic, transcendentals=0),
        **options,
    )


def in_hbm(values):
    return pltpu.with_memory_space_constraint(values, pltpu.HBM)


def body(tokens, expert_ids, keep_mask, gate_weights, weight_in, weight_out, grad_output):
    token_rows, width = tokens.shape
    hidden_width = weight_in.shape[2]
    rest_count = lax.axis_size("outer") * lax.axis_size("inner")
    members = lax.axis_size("row") * rest_count
    capacity = expert_ids.shape[1] * token_rows // members
    slot_total = 2 * members * capacity

    def exchange(values):
        return lax.ppermute(values, "half", ((0, 1), (1, 0)))

    def shuffle(rows, group, peers):
        shaped = rows.reshape(peers, slot_total // peers, width)
        return lax.all_to_all(shaped, group, split_axis=0, concat_axis=0, tiled=True).reshape(
            rows.shape
        )

    def shape(*dims, dtype=BF16):
        return jax.ShapeDtypeStruct(dims, dtype)

    vmem = pl.BlockSpec(memory_space=pltpu.VMEM)
    meta_shape = shape(8, token_rows, dtype=F32)
    slots, token_shape = shape(slot_total, width), shape(token_rows, width)
    slot_bytes, token_bytes = slot_total * width * 2, token_rows * width * 2
    place_flops = 2 * slot_total * token_rows * width

    partner_grad = exchange(grad_output)
    half = lax.axis_index("half").astype(jnp.int32).reshape(1)
    own_meta, sent_meta, sent = call(
        functools.partial(place_tokens_kernel, rest_count.bit_length() - 1, capacity),
        [meta_shape, meta_shape, slots],
        place_flops,
        token_bytes + slot_bytes,
        in_specs=[pl.BlockSpec(memory_space=pltpu.SMEM)] + [vmem] * 4,
    )(
        half,
        in_hbm(tokens),
        in_hbm(expert_ids.T),
        in_hbm(keep_mask.T),
        in_hbm(gate_weights.T),
    )
    x = shuffle(sent, ALL, 2 * members)
    partner_meta = exchange(sent_meta)
    sent_cot = call(
        place_cotangents_kernel, slots, 4 * place_flops, 2 * token_bytes + slot_bytes
    )(in_hbm(grad_output), partner_grad, own_meta, partner_meta)
    cot = shuffle(sent_cot, GROUP, members)

    chunk = 1024
    whole = pl.BlockSpec((slot_total, width), lambda i: (0, 0))
    in_spec = pl.BlockSpec((None, width, chunk), lambda i: (0, 0, i))
    out_spec = pl.BlockSpec((None, chunk, width), lambda i: (0, i, 0))
    mid_spec = pl.BlockSpec((slot_total, chunk), lambda i: (0, i))
    mid = pltpu.HBM((slot_total, hidden_width), BF16)
    product = 2 * slot_total * width * hidden_width
    traffic = 2 * slot_bytes + 4 * width * hidden_width + 4 * slot_total * hidden_width
    grid = (hidden_width // chunk,)
    total = pltpu.VMEM((slot_total, width), F32)
    weight_in, weight_out = in_hbm(weight_in), in_hbm(weight_out)
    hidden, slope, outputs = call(
        forward_kernel,
        [mid, mid, slots],
        2 * product,
        traffic,
        32,
        grid=grid,
        in_specs=[whole, in_spec, out_spec],
        out_specs=[mid_spec, mid_spec, whole],
        scratch_shapes=[total],
    )(x, weight_in, weight_out)
    back_out = shuffle(outputs, GROUP, members)
    grad_pre, grad_rows = call(
        backward_kernel,
        [mid, slots],
        2 * product,
        traffic,
        32,
        grid=grid,
        in_specs=[whole, in_spec, out_spec, mid_spec],
        out_specs=[mid_spec, whole],
        scratch_shapes=[total],
    )(cot, weight_in, weight_out, in_hbm(slope))
    back_grad = shuffle(grad_rows, ALL, 2 * members)
    tokens_f32, gates_shape = shape(token_rows, width, dtype=F32), shape(2, token_rows, dtype=F32)
    own_out, partner_out, own_gates, partner_gates = call(
        pick_outputs_kernel,
        [tokens_f32, token_shape, gates_shape, gates_shape],
        4 * place_flops,
        4 * token_bytes + slot_bytes,
    )(back_out, in_hbm(grad_output), partner_grad, own_meta, partner_meta)
    got_out, got_gates = exchange(partner_out), exchange(partner_gates)
    combined, grad_gates = call(
        finish_outputs_kernel, [token_shape, gates_shape], 0, 6 * token_bytes
    )(own_out, got_out, own_gates, got_gates)
    grad_pre, grad_gates = lax.optimization_barrier((grad_pre, grad_gates))
    grad_in_w, grad_out_w = call(
        weights_kernel,
        [pltpu.HBM(weight_in.shape, BF16), pltpu.HBM(weight_out.shape, BF16)],
        2 * product,
        traffic,
        32,
        grid=grid,
        in_specs=[whole, whole, mid_spec, mid_spec],
        out_specs=[in_spec, out_spec],
    )(x, cot, in_hbm(hidden), in_hbm(grad_pre))
    grad_tokens = call(
        pick_gradients_kernel, token_shape, place_flops, slot_bytes + token_bytes
    )(back_grad, own_meta)
    return (combined, grad_tokens, grad_gates.T, grad_in_w, grad_out_w)


def solution(mesh):
    rows, cols = mesh.devices.shape
    halves = Mesh(mesh.devices.reshape(rows // 2, 2, cols // 2, 2), AXES)
    flat, deep = P(AXES, None), P(AXES, None, None)
    return jax.shard_map(
        body,
        mesh=halves,
        in_specs=(flat, flat, flat, flat, deep, deep, flat),
        out_specs=(flat, flat, flat, deep, deep),
        check_vma=False,
    )
```

```python
import functools

import jax
import jax.numpy as jnp
from jax import lax
from jax.experimental import pallas as pl
from jax.experimental.pallas import tpu as pltpu
from jax.sharding import Mesh
from jax.sharding import PartitionSpec as P

BLOCK = 128
BF16 = jnp.bfloat16
F32 = jnp.float32
MIB = 1024 * 1024
SUB = 256
AXES = ("row", "outer", "inner")
GROUP = ("row", "inner", "outer")


def dot(a, b, contract_a, contract_b):
    return lax.dot_general(
        a, b, (((contract_a,), (contract_b,)), ((), ())), preferred_element_type=F32
    )


def column(row):
    count = row.shape[1]
    return jnp.transpose(jnp.broadcast_to(row, (count, count)))


def route(ids_ref, keep_ref, gates_ref, meta_ref, capacity, place_of):
    token_rows = ids_ref.shape[1]
    ids = ids_ref[...].astype(F32)
    earlier = lax.broadcasted_iota(jnp.int32, (token_rows, token_rows), 0) < lax.broadcasted_iota(
        jnp.int32, (token_rows, token_rows), 1
    )
    columns = (column(ids[0:1]), column(ids[1:2]))
    for k in range(2):
        count = jnp.zeros((token_rows, token_rows), F32)
        for other_choice in columns:
            count = count + jnp.where(earlier & (other_choice == ids[k : k + 1]), 1.0, 0.0)
        slot = jnp.sum(count, axis=0, keepdims=True).astype(jnp.int32)
        row = place_of(ids_ref[k : k + 1, :]) * capacity + slot
        meta_ref[k : k + 1, :] = jnp.where(keep_ref[k : k + 1, :] > 0, row, -1).astype(F32)
        meta_ref[k + 2 : k + 3, :] = gates_ref[k : k + 1, :]
    meta_ref[4:8, :] = jnp.zeros((4, token_rows), F32)


def hits(slot_total, meta_ref, k):
    rows = meta_ref[k : k + 1, :].astype(jnp.int32)
    index = lax.broadcasted_iota(jnp.int32, (slot_total, rows.shape[1]), 0)
    return index == rows


def one_hot(mask):
    return jnp.where(mask, 1.0, 0.0).astype(BF16)


def restore(tokens_ref):
    pieces = []
    for b in range(tokens_ref.shape[1] // BLOCK):
        x = tokens_ref[:, b * BLOCK : (b + 1) * BLOCK].astype(F32)
        scale = (jnp.max(jnp.abs(x), axis=1, keepdims=True) + 1e-06).astype(BF16).astype(F32)
        quantized = (x / scale).astype(BF16)
        pieces.append((quantized.astype(F32) * scale).astype(BF16))
    return jnp.concatenate(pieces, axis=1)


def place_tokens_kernel(
    capacity, place_of, tokens_ref, ids_ref, keep_ref, gates_ref, meta_ref, out_ref, restored
):
    step = pl.program_id(0)

    @pl.when(step == 0)
    def _():
        route(ids_ref, keep_ref, gates_ref, meta_ref, capacity, place_of)
        restored[...] = restore(tokens_ref)

    rows, token_rows = out_ref.shape[0], meta_ref.shape[1]
    index = lax.broadcasted_iota(jnp.int32, (rows, token_rows), 0) + step * rows
    mask = (index == meta_ref[0:1, :].astype(jnp.int32)) | (
        index == meta_ref[1:2, :].astype(jnp.int32)
    )
    out_ref[...] = dot(one_hot(mask), restored[...], 1, 0).astype(BF16)


def scaled_rows(gate_row, grad_ref):
    gate = column(gate_row)
    pieces = [
        gate * grad_ref[:, b * BLOCK : (b + 1) * BLOCK].astype(F32)
        for b in range(grad_ref.shape[1] // BLOCK)
    ]
    return jnp.concatenate(pieces, axis=1)


def place_cotangents_kernel(grad_ref, meta_ref, out_ref):
    slot_total = out_ref.shape[0]
    parts = [
        dot(
            one_hot(hits(slot_total, meta_ref, k)),
            scaled_rows(meta_ref[k + 2 : k + 3, :], grad_ref).astype(BF16),
            1,
            0,
        )
        for k in range(2)
    ]
    out_ref[...] = (parts[0] + parts[1]).astype(BF16)


def gelu_parts(v):
    c = 0.7978845608028654
    inner = c + (c * 0.044715) * (v * v)
    s = 0.5 + 0.5 * jnp.tanh(v * inner)
    hidden = v * s
    slope = s + (hidden * (1.0 - s)) * (6.0 * inner - 4.0 * c)
    return hidden.astype(BF16), slope.astype(BF16)


def forward_kernel(x_ref, w_in_ref, w_out_ref, hidden_ref, slope_ref, out_ref, total):
    step = pl.program_id(0)

    @pl.when(step == 0)
    def _():
        total[...] = jnp.zeros_like(total)

    parts = hidden_ref.shape[1] // SUB
    v = dot(x_ref[...], w_in_ref[:, :SUB], 1, 0)
    pieces = []
    for j in range(parts):
        if j + 1 < parts:
            after = dot(x_ref[...], w_in_ref[:, (j + 1) * SUB : (j + 2) * SUB], 1, 0)
        hidden, slope = gelu_parts(v)
        hidden_ref[:, j * SUB : (j + 1) * SUB] = hidden
        slope_ref[:, j * SUB : (j + 1) * SUB] = slope
        pieces.append(hidden)
        v = after
    total[...] += dot(jnp.concatenate(pieces, axis=1), w_out_ref[...], 1, 0)

    @pl.when(step == pl.num_programs(0) - 1)
    def _():
        out_ref[...] = total[...].astype(BF16)


def backward_kernel(cot_ref, w_in_ref, w_out_ref, slope_ref, grad_pre_ref, out_ref, total):
    step = pl.program_id(0)

    @pl.when(step == 0)
    def _():
        total[...] = jnp.zeros_like(total)

    parts = grad_pre_ref.shape[1] // SUB
    pieces = []
    for j in range(parts):
        grad_hidden = dot(cot_ref[...], w_out_ref[j * SUB : (j + 1) * SUB, :], 1, 1)
        slope = slope_ref[:, j * SUB : (j + 1) * SUB].astype(F32)
        grad_pre = (grad_hidden * slope).astype(BF16)
        grad_pre_ref[:, j * SUB : (j + 1) * SUB] = grad_pre
        pieces.append(grad_pre)
    total[...] += dot(jnp.concatenate(pieces, axis=1), w_in_ref[...], 1, 1)

    @pl.when(step == pl.num_programs(0) - 1)
    def _():
        out_ref[...] = total[...].astype(BF16)


def weights_kernel(x_ref, cot_ref, hidden_ref, grad_pre_ref, grad_in_ref, grad_out_ref):
    grad_in_ref[...] = dot(x_ref[...], grad_pre_ref[...], 0, 0).astype(BF16)
    grad_out_ref[...] = dot(hidden_ref[...], cot_ref[...], 0, 0).astype(BF16)


def pick_outputs_kernel(back_ref, grad_ref, meta_ref, out_ref, gates_ref):
    slot_total = back_ref.shape[0]
    total = None
    for k in range(2):
        picked = dot(one_hot(hits(slot_total, meta_ref, k)), back_ref[...], 0, 0)
        gate = column(meta_ref[k + 2 : k + 3, :])
        weighted = jnp.concatenate(
            [
                gate * picked[:, b * BLOCK : (b + 1) * BLOCK]
                for b in range(picked.shape[1] // BLOCK)
            ],
            axis=1,
        )
        total = weighted if total is None else total + weighted
        sums = jnp.sum(picked * grad_ref[...].astype(F32), axis=1, keepdims=True)
        rows = jnp.transpose(jnp.broadcast_to(sums, (sums.shape[0], sums.shape[0])))
        gates_ref[k : k + 1, :] = rows[0:1, :]
    out_ref[...] = total.astype(BF16)


def pick_gradients_kernel(back_ref, meta_ref, out_ref):
    slot_total = back_ref.shape[0]
    mask = hits(slot_total, meta_ref, 0) | hits(slot_total, meta_ref, 1)
    out_ref[...] = dot(one_hot(mask), back_ref[...], 0, 0).astype(BF16)


def call(kernel, outs, flops=0, traffic=0, limit=12, **options):
    return pl.pallas_call(
        kernel,
        out_shape=outs,
        compiler_params=pltpu.CompilerParams(vmem_limit_bytes=limit * MIB),
        cost_estimate=pl.CostEstimate(flops=flops, bytes_accessed=traffic, transcendentals=0),
        **options,
    )


def in_hbm(values):
    return pltpu.with_memory_space_constraint(values, pltpu.HBM)


def body(tokens, expert_ids, keep_mask, gate_weights, weight_in, weight_out, grad_output):
    token_rows, width = tokens.shape
    hidden_width = weight_in.shape[2]
    row_count, outer = lax.axis_size("row"), lax.axis_size("outer")
    experts = row_count * outer * lax.axis_size("inner")
    bits = outer.bit_length() - 1

    def place_of(expert):
        inner_at = expert & 1
        outer_at = (expert >> 1) & (outer - 1)
        row_at = expert >> (bits + 1)
        return ((row_at * 2 + inner_at) << bits) + outer_at

    capacity = 2 * expert_ids.shape[1] * token_rows // experts
    slot_total = experts * capacity

    def shuffle(rows):
        shaped = rows.reshape(experts, capacity, width)
        return lax.all_to_all(
            shaped, GROUP, split_axis=0, concat_axis=0, tiled=True
        ).reshape(slot_total, width)

    slots = jax.ShapeDtypeStruct((slot_total, width), BF16)
    slot_bytes = slot_total * width * 2
    token_bytes = token_rows * width * 2
    place_flops = 2 * slot_total * token_rows * width
    meta, sent = call(
        functools.partial(place_tokens_kernel, capacity, place_of),
        [jax.ShapeDtypeStruct((8, token_rows), F32), slots],
        place_flops,
        token_bytes + slot_bytes,
        grid=(2,),
        in_specs=[pl.BlockSpec((token_rows, width), lambda i: (0, 0))]
        + [pl.BlockSpec((2, token_rows), lambda i: (0, 0))] * 3,
        out_specs=[
            pl.BlockSpec((8, token_rows), lambda i: (0, 0)),
            pl.BlockSpec((slot_total // 2, width), lambda i: (i, 0)),
        ],
        scratch_shapes=[pltpu.VMEM((token_rows, width), BF16)],
    )(in_hbm(tokens), in_hbm(expert_ids.T), in_hbm(keep_mask.T), in_hbm(gate_weights.T))
    x = shuffle(sent)
    sent_cot = call(
        place_cotangents_kernel, slots, 2 * place_flops, token_bytes + slot_bytes
    )(in_hbm(grad_output), meta)
    cot = shuffle(sent_cot)

    chunk = 1024
    whole = pl.BlockSpec((slot_total, width), lambda i: (0, 0))
    in_spec = pl.BlockSpec((None, width, chunk), lambda i: (0, 0, i))
    out_spec = pl.BlockSpec((None, chunk, width), lambda i: (0, i, 0))
    mid_spec = pl.BlockSpec((slot_total, chunk), lambda i: (0, i))
    mid = pltpu.HBM((slot_total, hidden_width), BF16)
    product = 2 * slot_total * width * hidden_width
    traffic = 2 * slot_bytes + 4 * width * hidden_width + 4 * slot_total * hidden_width
    grid = (hidden_width // chunk,)
    total = pltpu.VMEM((slot_total, width), F32)
    weight_in, weight_out = in_hbm(weight_in), in_hbm(weight_out)
    hidden, slope, outputs = call(
        forward_kernel,
        [mid, mid, slots],
        2 * product,
        traffic,
        32,
        grid=grid,
        in_specs=[whole, in_spec, out_spec],
        out_specs=[mid_spec, mid_spec, whole],
        scratch_shapes=[total],
    )(x, weight_in, weight_out)
    back_out = shuffle(outputs)
    grad_pre, grad_rows = call(
        backward_kernel,
        [mid, slots],
        2 * product,
        traffic,
        32,
        grid=grid,
        in_specs=[whole, in_spec, out_spec, mid_spec],
        out_specs=[mid_spec, whole],
        scratch_shapes=[total],
    )(cot, weight_in, weight_out, in_hbm(slope))
    back_grad = shuffle(grad_rows)
    combined, grad_gates = call(
        pick_outputs_kernel,
        [
            jax.ShapeDtypeStruct((token_rows, width), BF16),
            jax.ShapeDtypeStruct((2, token_rows), F32),
        ],
        2 * place_flops,
        2 * token_bytes + slot_bytes,
    )(back_out, in_hbm(grad_output), meta)
    grad_in_w, grad_out_w = call(
        weights_kernel,
        [pltpu.HBM(weight_in.shape, BF16), pltpu.HBM(weight_out.shape, BF16)],
        2 * product,
        traffic,
        32,
        grid=grid,
        in_specs=[whole, whole, mid_spec, mid_spec],
        out_specs=[in_spec, out_spec],
    )(x, cot, in_hbm(hidden), in_hbm(grad_pre))
    grad_tokens = call(
        pick_gradients_kernel,
        jax.ShapeDtypeStruct((token_rows, width), BF16),
        place_flops,
        slot_bytes + token_bytes,
    )(back_grad, meta)
    return (combined, grad_tokens, grad_gates.T, grad_in_w, grad_out_w)


def solution(mesh):
    rows, cols = mesh.devices.shape
    split = Mesh(mesh.devices.reshape(rows, cols // 2, 2), AXES)
    flat, deep = P(AXES, None), P(AXES, None, None)
    return jax.shard_map(
        body,
        mesh=split,
        in_specs=(flat, flat, flat, flat, deep, deep, flat),
        out_specs=(flat, flat, flat, deep, deep),
        check_vma=False,
    )
```
